32 devices in a mesh: row: 8 (over y, x, core), seq: 4 (over z).
Axes of the slice: x: 2, y: 2, z: 4, core: 2. Of those that a mesh axis runs over, the one named last changes fastest.
Arguments:
- activations: bfloat16 [8, 2048, 1280], P('row', 'seq'), may hold values from -6 to 6
- cotangent: bfloat16 [8, 2048, 1280], P('row', 'seq'), may hold values from -6 to 6
- pic_lengths: int32 [8, 8], P('row'), may hold values from 0 to 1536, as said below
- pic_widths: int32 [8, 8], P('row'), may hold values from 8 to 32
- ln1_gain: bfloat16 [1280], P(('row', 'seq')), may hold values from 0.5 to 1.5
- ln1_bias: bfloat16 [1280], P(('row', 'seq')), may hold values from -4 to 4
- qkv_weight: bfloat16 [1280, 3840], P(('row', 'seq')), may hold values from -0.15625 to 0.15625
- qkv_bias: bfloat16 [3840], P(('row', 'seq')), may hold values from -4 to 4
- proj_weight: bfloat16 [1280, 1280], P(('row', 'seq')), may hold values from -1.25 to 1.25
- proj_bias: bfloat16 [1280], P(('row', 'seq')), may hold values from -4 to 4
- ln2_gain: bfloat16 [1280], P(('row', 'seq')), may hold values from 0.5 to 1.5
- ln2_bias: bfloat16 [1280], P(('row', 'seq')), may hold values from -4 to 4
- fc1_weight: bfloat16 [1280, 5120], P(('row', 'seq')), may hold values from -0.15625 to 0.15625
- fc1_bias: bfloat16 [5120], P(('row', 'seq')), may hold values from -4 to 4
- fc2_weight: bfloat16 [5120, 1280], P(('row', 'seq')), may hold values from -0.078125 to 0.078125
- fc2_bias: bfloat16 [1280], P(('row', 'seq')), may hold values from -4 to 4
Outputs:
- layer_out: bfloat16 [8, 2048, 1280], P('row', 'seq')
- grad_activations: bfloat16 [8, 2048, 1280], P('row', 'seq')
- grad_ln1_gain: float32 [1280], P(('row', 'seq'))
- grad_ln1_bias: float32 [1280], P(('row', 'seq'))
- grad_qkv_weight: float32 [1280, 3840], P(('row', 'seq'))
- grad_qk_bias: float32 [2560], P(('row', 'seq'))
- grad_value_bias: float32 [1280], P(('row', 'seq'))
- grad_proj_weight: float32 [1280, 1280], P(('row', 'seq'))
- grad_proj_bias: float32 [1280], P(('row', 'seq'))
- grad_ln2_gain: float32 [1280], P(('row', 'seq'))
- grad_ln2_bias: float32 [1280], P(('row', 'seq'))
- grad_fc1_weight: float32 [1280, 5120], P(('row', 'seq'))
- grad_fc1_bias: float32 [5120], P(('row', 'seq'))
- grad_fc2_weight: float32 [5120, 1280], P(('row', 'seq'))
- grad_fc2_bias: float32 [1280], P(('row', 'seq'))
The draws below stay inside these ranges and needn't reach their ends.
Inputs may be any that keep to these rules, and one draw needn't show every extreme that they name: `pic_lengths`: patches of each picture packed into a row, in order from the row's start; 0 marks an unused slot. Each row's lengths sum to between 1792 and 2047; the rest of the row is padding. `pic_widths`: patch i of a picture, in row-major order, lies at grid row i // width and grid column i % width.
All inputs are finite; a program needn't handle non-finite values.
Results may differ from the reference program's by a relative error of at most 0.015.
Values may be sent and summed in bfloat16 or wider, within the bound.
A program may use at most 512 MiB of HBM per device.

```python
import math
import jax
import jax.numpy as jnp
from jax import lax

D = 1280
HEADS = 16
HEAD_DIM = 80
FF = 5120
PICS = 8
ROW_LEN = 2048
ROWS_DEV = 1
TOK_DEV = 512
ROWS = 8


def draw_pic_lengths(key, part):
    key = jax.random.fold_in(key, 11)
    key_list = jax.random.split(key, 5)
    padding = jax.random.randint(key_list[0], (ROWS,), 1, TOK_DEV // 2 + 1)
    row_total = ROW_LEN - padding
    raw_lengths = jax.random.randint(key_list[1], (ROWS, PICS), ROW_LEN // 8, ROW_LEN // 2 + 1)
    before_sum = jnp.cumsum(raw_lengths, axis=1) - raw_lengths
    general = jnp.clip(row_total[:, None] - before_sum, 0, raw_lengths)
    last_slot = row_total - jnp.sum(general[:, :-1], axis=1)
    general = jnp.concatenate([general[:, :-1], last_slot[:, None]], axis=1)
    front = jax.random.randint(key_list[2], (ROWS,), 1, TOK_DEV // 2 + 1)
    tail_len = jax.random.randint(key_list[3], (ROWS,), TOK_DEV // 2 - front, TOK_DEV - front)
    spanning = jnp.full((ROWS,), ROW_LEN - TOK_DEV, jnp.int32)
    spanning_rows = jnp.concatenate([front[:, None], spanning[:, None], tail_len[:, None], jnp.zeros((ROWS, PICS - 3), jnp.int32)], axis=1)
    chosen = jax.random.randint(key_list[4], (ROWS // ROWS_DEV,), 0, ROWS_DEV)
    picked = jnp.arange(ROWS, dtype=jnp.int32) % ROWS_DEV == jnp.repeat(chosen, ROWS_DEV)
    return jnp.where(picked[:, None], spanning_rows, general).astype(jnp.int32)


def set_ends(values, stream_key, least, high):
    spot = [jax.random.randint(jax.random.fold_in(stream_key, axis), (), 0, length) for axis, length in enumerate(values.shape)]
    longest = values.shape.index(max(values.shape))
    beside = spot[:longest] + [(spot[longest] + 1) % values.shape[longest]] + spot[longest + 1:]
    return values.at[tuple(spot)].set(least).at[tuple(beside)].set(high)


def block_scale(key, dims, pieces, smallest, high):
    level, own = 1.0, jax.random.fold_in(key, 6)
    for axis_at, parts in pieces:
        draws = jnp.exp(jax.random.uniform(jax.random.fold_in(own, axis_at), (parts,), jnp.float32, smallest / len(pieces), high / len(pieces)))
        level = level * jnp.repeat(draws, dims[axis_at] // parts).reshape([-1 if axis == axis_at else 1 for axis in range(len(dims))])
    return level


def noise(key, shape, width, limit, shards=(), held_as=jnp.bfloat16):
    values = width * jax.random.normal(key, shape, jnp.float32)
    if shards:
        values = values * block_scale(key, shape, shards, -0.22, 0.18)
    return jnp.clip(values, -limit, limit).astype(held_as)


def setup_inputs(seed: int = 0) -> dict:
    keys = jax.random.split(jax.random.key(seed), 17)
    return {
        "activations": noise(keys[0], (ROWS, ROW_LEN, D), 1.0, 6.0, ((0, 8), (1, 4))),
        "cotangent": noise(keys[1], (ROWS, ROW_LEN, D), 1.0, 6.0, ((0, 8), (1, 4))),
        "pic_lengths": draw_pic_lengths(jax.random.fold_in(keys[16], 71), 0),
        "pic_widths": set_ends(jax.random.randint(keys[3], (ROWS, PICS), 8, 33), jax.random.fold_in(keys[3], 1), 8, 32).astype(jnp.int32),
        "ln1_gain": jnp.clip(1.0 + 0.1 * jax.random.normal(keys[4], (D,), jnp.float32), 0.5, 1.5).astype(jnp.bfloat16),
        "ln1_bias": noise(keys[5], (D,), 0.3, 4.0, ((0, 32),)),
        "qkv_weight": noise(keys[6], (D, 3 * D), D ** -0.5, 0.15625, ((0, 32),)),
        "qkv_bias": noise(keys[7], (3 * D,), 0.3, 4.0, ((0, 32),)),
        "proj_weight": noise(keys[8], (D, D), (D // 64) ** -0.5, 1.25, ((0, 32),)),
        "proj_bias": noise(keys[9], (D,), 0.3, 4.0, ((0, 32),)),
        "ln2_gain": jnp.clip(1.0 + 0.1 * jax.random.normal(keys[10], (D,), jnp.float32), 0.5, 1.5).astype(jnp.bfloat16),
        "ln2_bias": noise(keys[11], (D,), 0.3, 4.0, ((0, 32),)),
        "fc1_weight": noise(keys[12], (D, FF), D ** -0.5, 0.15625, ((0, 32),)),
        "fc1_bias": noise(keys[13], (FF,), 0.3, 4.0, ((0, 32),)),
        "fc2_weight": noise(keys[14], (FF, D), FF ** -0.5, 0.078125, ((0, 32),)),
        "fc2_bias": noise(keys[15], (D,), 0.3, 4.0, ((0, 32),)),
    }


NORM_EPS = 1e-06

@jax.custom_vjp
def low(v):
    return lax.optimization_barrier(v.astype(jnp.bfloat16)).astype(jnp.float32)

@jax.custom_vjp
def low_back(v):
    return v

def low_keep(v):
    return (low(v), None)

def low_pass(kept, grad):
    return (grad,)

def back_keep(v):
    return (v, None)

def back_low(kept, grad):
    return (low(grad),)
low.defvjp(low_keep, low_pass)
low_back.defvjp(back_keep, back_low)

def layer_norm(values, norm_gain, norm_shift):
    centre = lax.optimization_barrier(jnp.mean(values, axis=-1, keepdims=True))
    centered = values - centre
    variance = lax.optimization_barrier(jnp.mean(centered * centered, axis=-1, keepdims=True))
    return centered * lax.rsqrt(variance + NORM_EPS) * norm_gain + norm_shift

def quick_gelu(values):
    return values * jax.nn.sigmoid(1.702 * values)

def rotate_half(values):
    half_width = values.shape[-1] // 2
    return jnp.concatenate([-values[..., half_width:], values[..., :half_width]], axis=-1)

def rotate(values, cosine, sine_all):
    return values * cosine + rotate_half(values) * sine_all

def token_layout(lengths, widths):
    slot_count = lengths.shape[1]
    pic_ends = jnp.cumsum(lengths, axis=1).astype(jnp.int32)
    pic_starts = (pic_ends - lengths).astype(jnp.int32)
    positions = jnp.arange(ROW_LEN, dtype=jnp.int32)
    picture = lax.optimization_barrier(jnp.sum((positions[None, :, None] >= pic_ends[:, None, :]).astype(jnp.int32), axis=2)).astype(jnp.int32)
    matches = picture[:, :, None] == jnp.arange(slot_count, dtype=jnp.int32)[None, None, :]
    pic_first = lax.optimization_barrier(jnp.sum(jnp.where(matches, pic_starts[:, None, :], 0), axis=2)).astype(jnp.int32)
    grid_width = lax.optimization_barrier(jnp.sum(jnp.where(matches, widths[:, None, :], 0), axis=2)).astype(jnp.int32)
    grid_width = jnp.maximum(grid_width, 1)
    within = positions[None, :] - pic_first
    down_pos = (within // grid_width).astype(jnp.float32)
    side_pos = (within % grid_width).astype(jnp.float32)
    quarter = HEAD_DIM // 4
    frequency = 1.0 / 10000.0 ** (jnp.arange(quarter, dtype=jnp.float32) * 4.0 / HEAD_DIM)
    angles = jnp.concatenate([down_pos[..., None] * frequency, side_pos[..., None] * frequency], axis=-1)
    angles = jnp.concatenate([angles, angles], axis=-1)
    return (picture, jnp.cos(angles), jnp.sin(angles))

def forward(inputs, params, picture, cosine, sine_all):
    ln1_gain, ln1_bias, qkv_weight, qkv_bias, proj_weight, proj_bias, ln2_gain, ln2_bias, fc1_weight, fc1_bias, fc2_weight, fc2_bias = params
    highest = lax.Precision.HIGHEST
    group_size, length, model_width = inputs.shape
    normed_one = low(layer_norm(inputs, ln1_gain, ln1_bias))
    mixed_qkv = jnp.einsum('gld,de->gle', normed_one, qkv_weight, precision=highest) + qkv_bias
    mixed_qkv = low_back(mixed_qkv).reshape(group_size, length, 3, HEADS, HEAD_DIM)
    cos_heads = cosine[:, :, None, :]
    sin_heads = sine_all[:, :, None, :]
    queries = low(rotate(mixed_qkv[:, :, 0], cos_heads, sin_heads))
    keys_rot = low(rotate(mixed_qkv[:, :, 1], cos_heads, sin_heads))
    values = low(mixed_qkv[:, :, 2])
    scores = jnp.einsum('glhe,gmhe->ghlm', queries, keys_rot, precision=highest) * (1.0 / math.sqrt(HEAD_DIM))
    scores = low_back(scores)
    same_pic = picture[:, None, :, None] == picture[:, None, None, :]
    scores = jnp.where(same_pic, scores, -1000000000.0)
    probs = low(jax.nn.softmax(scores, axis=-1))
    attended = jnp.einsum('ghlm,gmhe->glhe', probs, values, precision=highest).reshape(group_size, length, model_width)
    attended = low(low_back(attended))
    branch = low_back(jnp.einsum('gld,de->gle', attended, proj_weight, precision=highest) + proj_bias)
    middle = inputs + branch
    normed_two = low(layer_norm(middle, ln2_gain, ln2_bias))
    before = low_back(jnp.einsum('gld,df->glf', normed_two, fc1_weight, precision=highest) + fc1_bias)
    activated = low(quick_gelu(before))
    result = low_back(jnp.einsum('glf,fd->gld', activated, fc2_weight, precision=highest) + fc2_bias)
    return middle + result

def reference(activations, cotangent, pic_lengths, pic_widths, ln1_gain, ln1_bias, qkv_weight, qkv_bias, proj_weight, proj_bias, ln2_gain, ln2_bias, fc1_weight, fc1_bias, fc2_weight, fc2_bias):
    params = tuple((member.astype(jnp.float32) for member in (ln1_gain, ln1_bias, qkv_weight, qkv_bias, proj_weight, proj_bias, ln2_gain, ln2_bias, fc1_weight, fc1_bias, fc2_weight, fc2_bias)))
    picture, cosine, sine_all = token_layout(pic_lengths, pic_widths)
    group_rows = math.gcd(ROWS, max(1, 2048 // ROW_LEN))
    group_count = ROWS // group_rows

    def by_groups(values):
        return values.reshape((group_count, group_rows) + values.shape[1:])

    def one_group(totals, inputs):
        rows_in, cot_in, pic_in, cos_in, sin_in = inputs

        def apply_layer(layer_in, layer_params):
            return forward(layer_in, layer_params, pic_in, cos_in, sin_in)
        output, pullback = jax.vjp(apply_layer, rows_in.astype(jnp.float32), params)
        grad_rows, grad_params = pullback(cot_in.astype(jnp.float32))
        totals = tuple((first_sum + second_sum for first_sum, second_sum in zip(totals, grad_params)))
        return (totals, (output.astype(jnp.bfloat16), grad_rows.astype(jnp.bfloat16)))
    zero_grads = tuple((jnp.zeros(member.shape, jnp.float32) for member in params))
    totals, (layer_out, grad_rows) = lax.scan(one_group, zero_grads, (by_groups(activations), by_groups(cotangent), by_groups(picture), by_groups(cosine), by_groups(sine_all)))
    return (layer_out.reshape(activations.shape), grad_rows.reshape(activations.shape), totals[0], totals[1], totals[2], totals[3][:2 * D], totals[3][2 * D:], totals[4], totals[5], totals[6], totals[7], totals[8], totals[9], totals[10], totals[11])
```

```python
import functools
import math

import jax
import jax.numpy as jnp
from jax import lax
from jax.experimental import pallas as pl
from jax.experimental.pallas import tpu as pltpu
from jax.sharding import PartitionSpec as P

HEADS = 16
HEAD_DIM = 80
HALF = HEAD_DIM // 2
LANE = 128
NORM_EPS = 1e-06
SCALE = 1.0 / math.sqrt(HEAD_DIM)
LOG2E = 1.4426950408889634
EXP_SCALE = SCALE * LOG2E
QBLK = 256
MESH = pl.DeviceIdType.MESH
ANY = pl.BlockSpec(memory_space=pl.ANY)
VMEM = pl.BlockSpec(memory_space=pltpu.VMEM)


def round_up(value, unit):
    return -(-value // unit) * unit


def flip(index, bit):
    return index + bit - 2 * bit * ((index // bit) % 2)


def remote(src, dst, send_sem, recv_sem, row, seq):
    return pltpu.make_async_remote_copy(
        src_ref=src,
        dst_ref=dst,
        send_sem=send_sem,
        recv_sem=recv_sem,
        device_id=(row, seq),
        device_id_type=MESH,
    )


class Sems:
    def __init__(self, ref):
        self.ref = ref
        self.used = 0

    def take(self, count):
        first = self.used
        self.used += count
        assert self.used <= self.ref.shape[0]
        return [self.ref.at[first + i] for i in range(count)]


class Chain:
    def __init__(self, own, buf, base, row, seq, size, sems):
        self.own, self.buf, self.base = own, buf, base
        self.row, self.seq, self.size = row, seq, size
        self.sems = [[(sems.take(1)[0], sems.take(1)[0]) for _ in range(size - 1)] for _ in range(2)]
        (self.local,) = sems.take(1)

    def _copies(self, step):
        seq, size = self.seq, self.size
        out = []
        for way in range(2):
            sign = 1 - 2 * way
            block = seq - sign * (step - 1)
            peer = seq + sign
            going = (peer >= 0) & (peer < size) & (block >= 0) & (block < size)
            slot = self.buf.at[self.base + block]
            src = self.own if step == 1 else slot
            copy = functools.partial(remote, src, slot, *self.sems[way][step - 1], self.row, peer)
            come = seq - sign * step
            coming = (come >= 0) & (come < size)
            into = self.buf.at[self.base + come]
            arrive = functools.partial(remote, into, into, *self.sems[way][step - 1], self.row, peer)
            out.append((going, copy, coming, arrive))
        return out

    def keep(self):
        return pltpu.make_async_copy(self.own, self.buf.at[self.base + self.seq], self.local)

    def send(self, step):
        if step == 1:
            self.keep().start()
        for going, copy, _, _ in self._copies(step):
            pl.when(going)(lambda copy=copy: copy().start())

    def recv(self, step):
        for _, _, coming, arrive in self._copies(step):
            pl.when(coming)(lambda arrive=arrive: arrive().wait_recv())

    def finish(self):
        for step in range(1, self.size):
            for going, copy, _, _ in self._copies(step):
                pl.when(going)(lambda copy=copy: copy().wait_send())


class Scatter:
    def __init__(self, src, dst_of, row, seq, size, sems):
        self.src, self.dst_of = src, dst_of
        self.row, self.seq, self.size = row, seq, size
        self.sems = [(sems.take(1)[0], sems.take(1)[0]) for _ in range(size - 1)]
        (self.local,) = sems.take(1)

    def _to(self, step):
        peer = (self.seq + step) % self.size
        return remote(self.src.at[peer], self.dst_of(self.seq), *self.sems[step - 1], self.row, peer)

    def _from(self, step):
        peer = (self.seq + self.size - step) % self.size
        into = self.dst_of(peer)
        return remote(into, into, *self.sems[step - 1], self.row, peer)

    def keep(self):
        return pltpu.make_async_copy(self.src.at[self.seq], self.dst_of(self.seq), self.local)

    def send(self, step):
        self._to(step).start()

    def send_all(self):
        self.keep().start()
        for step in range(1, self.size):
            self.send(step)

    def recv(self):
        self.keep().wait()
        for step in range(1, self.size):
            self._from(step).wait_recv()

    def finish(self):
        for step in range(1, self.size):
            self._to(step).wait_send()


class Spread:
    def __init__(self, buf, row, seq, rows, size, sems):
        self.buf, self.row, self.seq, self.size = buf, row, seq, size
        bits = [1 << i for i in range(1, rows.bit_length() - 1)]
        self.stages = len(bits)
        self.orders = (bits, bits[::-1])
        self.half = buf.shape[2] // 2
        self.sems = [
            [[(sems.take(1)[0], sems.take(1)[0]) for _ in range(1 << j)] for j in range(self.stages)]
            for _ in range(2)
        ]
        self.core_sems = [(sems.take(1)[0], sems.take(1)[0])]
        self.core_sems += [
            (sems.take(1)[0], sems.take(1)[0]) for _ in range(2 * ((1 << self.stages) - 1))
        ]

    def _block(self, row, half):
        first = row * self.size
        if half is None:
            return self.buf.at[pl.ds(first, self.size)]
        return self.buf.at[pl.ds(first, self.size), :, pl.ds(half * self.half, self.half)]

    def _rows(self, start, half, stage):
        rows = [start]
        for bit in self.orders[half][:stage]:
            rows += [flip(row, bit) for row in rows]
        return rows

    def _pairs(self, stage):
        out = []
        for half in range(2):
            bit = self.orders[half][stage]
            peer = flip(self.row, bit)
            for i, row in enumerate(self._rows(self.row, half, stage)):
                here = self._block(row, half)
                there = self._block(flip(row, bit), half)
                pair = self.sems[half][stage][i]
                out.append((here, there, pair, peer))
        return out

    def _core(self, index, block):
        return remote(block, block, *self.core_sems[index], flip(self.row, 1), self.seq)

    def _core_blocks(self, row):
        out = [[self._block(row, None)]]
        for stage in range(self.stages):
            out.append([])
            for half in range(2):
                bit = self.orders[half][stage]
                for other in self._rows(row, half, stage):
                    out[-1].append(self._block(flip(other, bit), half))
        return out

    def _first(self, stage):
        return 0 if stage == 0 else 1 + 2 * ((1 << (stage - 1)) - 1)

    def send(self, stage):
        if stage < self.stages:
            for here, _, pair, peer in self._pairs(stage):
                remote(here, here, *pair, peer, self.seq).start()
        for i, block in enumerate(self._core_blocks(self.row)[stage]):
            self._core(self._first(stage) + i, block).start()

    def recv(self, stage):
        for _, there, pair, peer in self._pairs(stage):
            remote(there, there, *pair, peer, self.seq).wait_recv()

    def finish(self):
        for stage in range(self.stages):
            for here, _, pair, peer in self._pairs(stage):
                remote(here, here, *pair, peer, self.seq).wait_send()
        mine, theirs = self._core_blocks(self.row), self._core_blocks(flip(self.row, 1))
        for stage in range(self.stages + 1):
            for i, block in enumerate(theirs[stage]):
                self._core(self._first(stage) + i, block).wait_recv()
            for i, block in enumerate(mine[stage]):
                self._core(self._first(stage) + i, block).wait_send()


def greet(row, seq, rows, size):
    barrier = pltpu.get_barrier_semaphore()
    count = 0
    bit = 1
    while bit < rows:
        pl.semaphore_signal(barrier, inc=1, device_id=(flip(row, bit), seq), device_id_type=MESH)
        bit *= 2
        count += 1
    for step in range(1, size):
        pl.semaphore_signal(barrier, inc=1, device_id=(row, (seq + step) % size), device_id_type=MESH)
        count += 1
    pl.semaphore_wait(barrier, count)


def forward_kernel(
    rows, size, shard, group,
    x, wq, wp, w1, w2, small, cos, sin, pic_col, pic_row,
    wp_all, w1_all, w2_all, att, small_sum, normed, qkv, wq_full, lse,
    xg, wq_buf, small_buf, wq_wide, v_turn, o_part, o_send, sem_ref,
):
    row, seq = lax.axis_index("row"), lax.axis_index("seq")
    toks, width = x.shape
    length = toks * size
    part = group * LANE
    sems = Sems(sem_ref)
    base = row * size
    g_small = Chain(small, small_buf, base, row, seq, size, sems)
    g_wp = Chain(wp, wp_all, base, row, seq, size, sems)
    g_w1 = Chain(w1, w1_all, base, row, seq, size, sems)
    g_w2 = Chain(w2, w2_all, base, row, seq, size, sems)
    g_x = Chain(x, xg, 0, row, seq, size, sems)
    a_wq = Scatter(wq, lambda j: wq_buf.at[base + j], row, seq, size, sems)
    s_small = Spread(small_buf, row, seq, rows, size, sems)
    s_wq = Spread(wq_buf, row, seq, rows, size, sems)
    s_wp = Spread(wp_all, row, seq, rows, size, sems)
    s_w1 = Spread(w1_all, row, seq, rows, size, sems)
    s_w2 = Spread(w2_all, row, seq, rows, size, sems)
    a_o = Scatter(o_send, lambda j: att.at[j], row, seq, size, sems)
    last = s_small.stages

    greet(row, seq, rows, size)
    g_small.send(1)
    a_wq.send_all()
    g_wp.send(1)
    g_w1.send(1)
    g_x.send(1)
    for step in range(1, size):
        for g in (g_small, g_wp, g_w1):
            g.recv(step)
            if step < size - 1:
                g.send(step + 1)
    a_wq.recv()
    for g in (g_small, g_wp, g_w1, g_x):
        g.keep().wait()
    for s in (s_small, s_wq, s_wp, s_w1):
        s.send(0)
    for stage in range(last):
        for s in (s_small, s_wq):
            s.recv(stage)
            s.send(stage + 1)
    s_small.finish()
    s_wq.finish()

    total = jnp.zeros(small_sum.shape, jnp.float32)
    for i in range(rows * size):
        total += small_buf[i].astype(jnp.float32)
    small_sum[...] = total
    bias = jnp.zeros((1, 3 * part), jnp.float32)
    for i in range(rows * size):
        block = wq_buf[i].astype(jnp.float32)
        wq_wide[pl.ds(i * shard, shard), :] = block[:shard]
        bias += block[shard : shard + 1]
    for i in range(0, width, LANE):
        wq_full[pl.ds(i, LANE), :] = wq_wide[pl.ds(i, LANE), :].astype(jnp.bfloat16)
    wq_wide[0:1, :] = bias

    def project(chunk):
        first = pl.multiple_of(chunk * toks, toks)
        block = 128

        def norm(i, carry):
            at = pl.multiple_of(i * block, block)
            values = xg[chunk, pl.ds(at, block), :].astype(jnp.float32)
            centered = values - jnp.mean(values, axis=-1, keepdims=True)
            variance = jnp.mean(centered * centered, axis=-1, keepdims=True)
            out = centered * lax.rsqrt(variance + NORM_EPS) * small_sum[0:1, :] + small_sum[1:2, :]
            normed[pl.ds(pl.multiple_of(first + at, block), block), :] = out.astype(jnp.bfloat16)
            return carry

        lax.fori_loop(0, toks // block, norm, 0)
        span = pl.ds(first, toks)

        def turned(i, carry):
            at = pl.multiple_of(i * 2 * LANE, 2 * LANE)
            mixed = jnp.dot(normed[span, :], wq_full[:, pl.ds(at, 2 * LANE)], preferred_element_type=jnp.float32)
            mixed += wq_wide[0:1, pl.ds(at, 2 * LANE)]
            for j in range(2):
                u = mixed[:, j * LANE : (j + 1) * LANE]
                u = u * cos[span, :] + pltpu.roll(u, LANE // 2, 1) * sin[span, :]
                qkv[span, pl.ds(pl.multiple_of(at + j * LANE, LANE), LANE)] = u.astype(jnp.bfloat16)
            return carry

        lax.fori_loop(0, part // LANE, turned, 0)

        def plain(i, carry):
            at = pl.multiple_of(i * 2 * LANE, 2 * LANE)
            col = pl.ds(pl.multiple_of(2 * part + at, 2 * LANE), 2 * LANE)
            mixed = jnp.dot(normed[span, :], wq_full[:, col], preferred_element_type=jnp.float32)
            mixed += wq_wide[0:1, col]
            qkv[span, col] = mixed.astype(jnp.bfloat16)
            v_turn[pl.ds(at, 2 * LANE), span] = mixed.T.astype(jnp.bfloat16)
            return carry

        lax.fori_loop(0, part // (2 * LANE), plain, 0)

    project(seq)
    for step in range(1, size):
        g_x.recv(step)
        if step < size - 1:
            g_x.send(step + 1)
        if step == 1:
            g_w2.send(1)
            if last > 0:
                for s in (s_wp, s_w1):
                    s.recv(0)
                    s.send(1)

        def arrived(i, carry):
            chunk = seq + (2 * i - 1) * step
            pl.when((chunk >= 0) & (chunk < size))(lambda: project(chunk))
            return carry

        lax.fori_loop(0, 2, arrived, 0)

    def attend(chunk):
        def one(i, carry):
            head = i % group
            block = chunk * (toks // QBLK) + i // group
            span = pl.ds(pl.multiple_of(block * QBLK, QBLK), QBLK)
            at = pl.multiple_of(head * LANE, LANE)
            q = qkv[span, pl.ds(at, LANE)]
            k = qkv[:, pl.ds(pl.multiple_of(part + at, LANE), LANE)]
            scores = lax.dot_general(k, q, (((1,), (1,)), ((), ())), preferred_element_type=jnp.float32)
            scores = jnp.where(pic_col[...] == pic_row[:, span], scores, -1e30)
            top = jnp.max(scores, axis=0, keepdims=True)
            weights = jnp.exp2((scores - top) * EXP_SCALE)
            sums = jnp.sum(weights, axis=0, keepdims=True)
            out = jnp.dot(v_turn[pl.ds(at, LANE), :], weights.astype(jnp.bfloat16), preferred_element_type=jnp.float32)
            out = out / sums
            o_part[pl.ds(pl.multiple_of(head * HEAD_DIM, 8), HEAD_DIM), :] = out[:HEAD_DIM]
            lse[head, :, span] = top * EXP_SCALE + jnp.log2(sums)

            @pl.when(head == group - 1)
            def _():
                within = pl.multiple_of((i // group) * QBLK, QBLK)
                o_send[chunk, pl.ds(within, QBLK), :] = o_part[...].T.astype(jnp.bfloat16)

            return carry

        lax.fori_loop(0, group * (toks // QBLK), one, 0)

    o_part[...] = jnp.zeros_like(o_part)
    for step in range(1, size + 1):
        attend((seq + step) % size)
        if step < size:
            a_o.send(step)
        else:
            a_o.keep().start()
        if step < size:
            g_w2.recv(step)
            if step < size - 1:
                g_w2.send(step + 1)
            else:
                g_w2.keep().wait()
                s_w2.send(0)
        if step == 1:
            for stage in range(1, last):
                for s in (s_wp, s_w1):
                    s.recv(stage)
                    s.send(stage + 1)
    for stage in range(last):
        s_w2.recv(stage)
        s_w2.send(stage + 1)
    for s in (s_wp, s_w1, s_w2):
        s.finish()
    a_o.recv()
    for g in (g_small, g_wp, g_w1, g_w2, g_x, a_wq, a_o):
        g.finish()


def forward_call(mesh, x, wq, wp, w1, w2, small, cos, sin, pic_col, pic_row):
    rows, size = mesh.shape["row"], mesh.shape["seq"]
    toks, width = x.shape
    length = toks * size
    group = HEADS // size
    part = group * LANE
    shard = wp.shape[0]
    out_width = round_up(group * HEAD_DIM, LANE)
    total = rows * size
    bf, f32 = jnp.bfloat16, jnp.float32
    shape = jax.ShapeDtypeStruct
    return pl.pallas_call(
        functools.partial(forward_kernel, rows, size, shard, group),
        out_shape=(
            shape((total,) + wp.shape, bf),
            shape((total,) + w1.shape, bf),
            shape((total,) + w2.shape, bf),
            shape((size, toks, out_width), bf),
            shape(small.shape, f32),
            shape((length, width), bf),
            shape((length, 3 * part), bf),
            shape((width, 3 * part), bf),
            shape((group, 1, length), f32),
        ),
        in_specs=[ANY] * 6 + [VMEM] * 4,
        out_specs=(ANY,) * 4 + (VMEM,) * 5,
        scratch_shapes=[
            pltpu.VMEM((size, toks, width), bf),
            pltpu.VMEM((total,) + wq.shape[1:], bf),
            pltpu.VMEM((total,) + small.shape, bf),
            pltpu.VMEM((width, 3 * part), f32),
            pltpu.VMEM((part, length), bf),
            pltpu.VMEM((out_width, QBLK), f32),
            pltpu.VMEM((size, toks, out_width), bf),
            pltpu.SemaphoreType.DMA((512,)),
        ],
        compiler_params=pltpu.CompilerParams(
            collective_id=0, has_side_effects=True, vmem_limit_bytes=62 * 1024 * 1024
        ),
        name="forward",
    )(x, wq, wp, w1, w2, small, cos, sin, pic_col, pic_row)


def token_layout(lengths, widths, row_len):
    pic_ends = jnp.cumsum(lengths)
    pic_starts = pic_ends - lengths
    positions = jnp.arange(row_len, dtype=jnp.int32)
    picture = jnp.sum((positions[:, None] >= pic_ends[None, :]).astype(jnp.int32), axis=1)
    matches = picture[:, None] == jnp.arange(lengths.shape[0], dtype=jnp.int32)[None, :]
    first = jnp.sum(jnp.where(matches, pic_starts[None, :], 0), axis=1)
    grid_width = jnp.maximum(jnp.sum(jnp.where(matches, widths[None, :], 0), axis=1), 1)
    within = positions - first
    down = (within // grid_width).astype(jnp.float32)
    side = (within % grid_width).astype(jnp.float32)
    quarter = HEAD_DIM // 4
    frequency = 1.0 / 10000.0 ** (jnp.arange(quarter, dtype=jnp.float32) * 4.0 / HEAD_DIM)
    angles = jnp.concatenate([down[:, None] * frequency, side[:, None] * frequency], axis=-1)
    cosine, sine = jnp.cos(angles), jnp.sin(angles)
    gap = jnp.zeros((row_len, LANE // 2 - HALF), jnp.float32)
    return (
        picture,
        jnp.concatenate([cosine, gap, cosine, gap], axis=-1),
        jnp.concatenate([-sine, gap, sine, gap], axis=-1),
    )


def head_columns(values, size, pieces):
    a = values.shape[0]
    group = HEADS // size
    values = values.reshape(a, size, group, pieces, HEAD_DIM // pieces)
    values = jnp.pad(values, ((0, 0),) * 4 + ((0, (LANE - HEAD_DIM) // pieces),))
    return values.reshape(a, size, group * LANE).transpose(1, 0, 2)


def head_columns_back(values, pieces):
    size, a, lanes = values.shape
    group = lanes // LANE
    values = values.transpose(1, 0, 2).reshape(a, size, group, pieces, LANE // pieces)
    return values[..., : HEAD_DIM // pieces].reshape(a, HEADS * HEAD_DIM)


def qkv_columns(values, size):
    width = HEADS * HEAD_DIM
    return jnp.concatenate(
        [
            head_columns(values[:, :width], size, 2),
            head_columns(values[:, width : 2 * width], size, 2),
            head_columns(values[:, 2 * width :], size, 1),
        ],
        axis=-1,
    )


def layer_norm(values, norm_gain, norm_shift):
    centre = jnp.mean(values, axis=-1, keepdims=True)
    centered = values - centre
    variance = jnp.mean(centered * centered, axis=-1, keepdims=True)
    return centered * lax.rsqrt(variance + NORM_EPS) * norm_gain + norm_shift


def quick_gelu(values):
    return values * jax.nn.sigmoid(1.702 * values)


def pack_small(vectors, width, index, total):
    lines = []
    for values in vectors:
        full = values.shape[0] * total
        line = lax.dynamic_update_slice(jnp.zeros((full,), values.dtype), values, (index * values.shape[0],))
        lines.append(line.reshape(-1, width))
    lines = jnp.concatenate(lines, axis=0)
    return jnp.pad(lines, ((0, 16 - lines.shape[0]), (0, 0)))


def shards(
    mesh,
    activations,
    cotangent,
    pic_lengths,
    pic_widths,
    ln1_gain,
    ln1_bias,
    qkv_weight,
    qkv_bias,
    proj_weight,
    proj_bias,
    ln2_gain,
    ln2_bias,
    fc1_weight,
    fc1_bias,
    fc2_weight,
    fc2_bias,
):
    rows, size = mesh.shape["row"], mesh.shape["seq"]
    total = rows * size
    index = lax.axis_index("row") * size + lax.axis_index("seq")
    _, toks, width = activations.shape
    length = toks * size
    group = HEADS // size
    part = group * LANE
    shard = proj_weight.shape[0]
    bf, f32 = jnp.bfloat16, jnp.float32

    picture, cos, sin = token_layout(pic_lengths[0], pic_widths[0], length)
    small = pack_small((ln1_gain, ln1_bias, proj_bias, ln2_gain, ln2_bias, fc2_bias, fc1_bias), width, index, total)
    bias_line = lax.dynamic_update_slice(jnp.zeros((1, 3 * width), bf), qkv_bias[None], (0, index * qkv_bias.shape[0]))
    wq = jnp.concatenate([qkv_weight, bias_line], axis=0)
    wq = jnp.pad(qkv_columns(wq, size), ((0, 0), (0, round_up(shard + 3, 16) - shard - 1), (0, 0)))
    x = activations[0]
    wp, w1, w2, att, lines, normed, qkv, wq_full, lse = forward_call(
        mesh, x, wq, proj_weight, fc1_weight, fc2_weight, small, cos, sin, picture[:, None], picture[None, :]
    )
    wp, w1, w2 = (w.reshape(-1, w.shape[-1]) for w in (wp, w1, w2))
    b_proj, gain_two, shift_two, b_down = lines[2], lines[3], lines[4], lines[5]
    b_up = lines[6 : 6 + w1.shape[1] // width].reshape(-1)

    inputs = x.astype(f32)
    attended = jnp.concatenate([att[g, :, : group * HEAD_DIM] for g in range(size)], axis=-1)
    middle = inputs + jnp.dot(attended, wp, preferred_element_type=f32) + b_proj
    normed_two, norm_two_back = jax.vjp(layer_norm, middle, gain_two, shift_two)
    normed_two_low = normed_two.astype(bf)
    before = jnp.dot(normed_two_low, w1, preferred_element_type=f32) + b_up
    activated, gelu_back = jax.vjp(quick_gelu, before)
    activated_low = activated.astype(bf)
    result = jnp.dot(activated_low, w2, preferred_element_type=f32) + b_down
    layer_out = (middle + result).astype(bf)

    grad_out = cotangent[0]
    grad_out_wide = grad_out.astype(f32)
    grad_down = jnp.dot(activated_low.T, grad_out, preferred_element_type=f32)
    grad_down_bias = jnp.sum(grad_out_wide, axis=0)
    (grad_before,) = gelu_back(jnp.dot(grad_out, w2.T, preferred_element_type=f32))
    grad_before_low = grad_before.astype(bf)
    grad_up_bias = jnp.sum(grad_before_low.astype(f32), axis=0)
    grad_up = jnp.dot(normed_two_low.T, grad_before_low, preferred_element_type=f32)
    grad_normed_two = jnp.dot(grad_before_low, w1.T, preferred_element_type=f32)
    grad_middle, grad_gain_two, grad_shift_two = norm_two_back(grad_normed_two)
    grad_middle = grad_middle + grad_out_wide
    grad_branch = grad_middle.astype(bf)
    grad_proj_bias = jnp.sum(grad_branch.astype(f32), axis=0)
    grad_proj = jnp.dot(attended.T, grad_branch, preferred_element_type=f32)
    grad_attended = jnp.dot(grad_branch, wp.T, preferred_element_type=f32).astype(bf)

    grad_att = lax.all_to_all(
        grad_attended.reshape(toks, size, group * HEAD_DIM), "seq", split_axis=1, concat_axis=0, tiled=True
    ).reshape(length, group, HEAD_DIM)
    heads = qkv.reshape(length, 3, group, LANE)
    q, k, v = heads[:, 0], heads[:, 1], heads[:, 2, :, :HEAD_DIM]
    scores = jnp.einsum("khe,qhe->hkq", k, q, preferred_element_type=f32)
    scores = jnp.where((picture[:, None] == picture[None, :])[None], scores, -1e30)
    probs = jnp.exp2(scores * EXP_SCALE - lse)
    grad_probs = jnp.einsum("khe,qhe->hkq", v, grad_att, preferred_element_type=f32)
    delta = jnp.sum(probs * grad_probs, axis=1, keepdims=True)
    grad_scores = (probs * (grad_probs - delta)).astype(bf)
    grad_q = jnp.einsum("hkq,khe->qhe", grad_scores, k, preferred_element_type=f32) * SCALE
    grad_k = jnp.einsum("hkq,qhe->khe", grad_scores, q, preferred_element_type=f32) * SCALE
    grad_v = jnp.einsum("hkq,qhe->khe", probs.astype(bf), grad_att, preferred_element_type=f32)
    grad_v = jnp.pad(grad_v, ((0, 0), (0, 0), (0, LANE - HEAD_DIM)))

    def unturn(g):
        return g * cos[:, None] + jnp.roll(g * sin[:, None], LANE // 2, axis=-1)

    grad_mixed = jnp.concatenate(
        [g.reshape(length, part) for g in (unturn(grad_q), unturn(grad_k), grad_v)], axis=-1
    ).astype(bf)
    grad_normed = jnp.dot(grad_mixed, wq_full.T, preferred_element_type=f32).astype(bf)
    grad_normed = lax.psum_scatter(grad_normed, "seq", scatter_dimension=0, tiled=True).astype(f32)
    grad_qkv = jnp.dot(normed.T, grad_mixed, preferred_element_type=f32).astype(bf)
    grad_qkv = lax.psum_scatter(grad_qkv, "row", scatter_dimension=0, tiled=True).reshape(size, shard, 3 * part)
    grad_qkv = lax.all_to_all(grad_qkv, "seq", split_axis=0, concat_axis=0, tiled=True).astype(f32)

    def natural(g):
        return jnp.concatenate(
            [
                head_columns_back(g[:, :, :part], 2),
                head_columns_back(g[:, :, part : 2 * part], 2),
                head_columns_back(g[:, :, 2 * part :], 1),
            ],
            axis=-1,
        )

    grad_qkv = natural(grad_qkv)
    grad_bias = jnp.sum(grad_mixed.astype(f32), axis=0)
    grad_bias = natural(lax.all_gather(lax.psum(grad_bias, "row"), "seq")[:, None, :])[0]
    grad_qk = lax.dynamic_slice_in_dim(grad_bias[: 2 * width], index * 2 * shard, 2 * shard)
    grad_value = lax.dynamic_slice_in_dim(grad_bias[2 * width :], index * shard, shard)
    _, norm_one_back = jax.vjp(layer_norm, inputs, lines[0], lines[1])
    grad_inputs, grad_gain_one, grad_shift_one = norm_one_back(grad_normed)
    grad_acts = (grad_inputs + grad_middle).astype(bf)

    def owned(values):
        return lax.psum_scatter(values, ("row", "seq"), scatter_dimension=0, tiled=True)

    def owned_low(values):
        return owned(values.astype(bf)).astype(f32)

    return (
        layer_out[None],
        grad_acts[None],
        owned(grad_gain_one),
        owned(grad_shift_one),
        grad_qkv,
        grad_qk,
        grad_value,
        owned_low(grad_proj),
        owned(grad_proj_bias),
        owned(grad_gain_two),
        owned(grad_shift_two),
        owned_low(grad_up),
        owned(grad_up_bias),
        owned_low(grad_down),
        owned(grad_down_bias),
    )


def solution(mesh):
    one, two = P(("row", "seq")), P(("row", "seq"), None)
    tokens = P("row", "seq", None)
    return jax.shard_map(
        functools.partial(shards, mesh),
        mesh=mesh,
        in_specs=(tokens, tokens, P("row", None), P("row", None), one, one, two, one, two, one, one, one, two, one, two, one),
        out_specs=(tokens, tokens, one, one, two, one, one, two, one, one, one, two, one, two, one),
        check_vma=False,
    )
```

```python
import functools
import math

import jax
import jax.numpy as jnp
from jax import lax
from jax.experimental import pallas as pl
from jax.experimental.pallas import tpu as pltpu
from jax.sharding import PartitionSpec as P

HEADS = 16
HEAD_DIM = 80
HALF = HEAD_DIM // 2
LANE = 128
NORM_EPS = 1e-06
SCALE = 1.0 / math.sqrt(HEAD_DIM)
LOG2E = 1.4426950408889634
EXP_SCALE = SCALE * LOG2E
QBLK = 256
MESH = pl.DeviceIdType.MESH
ANY = pl.BlockSpec(memory_space=pl.ANY)
VMEM = pl.BlockSpec(memory_space=pltpu.VMEM)


def round_up(value, unit):
    return -(-value // unit) * unit


def flip(index, bit):
    return index + bit - 2 * bit * ((index // bit) % 2)


def remote(src, dst, send_sem, recv_sem, row, seq):
    return pltpu.make_async_remote_copy(
        src_ref=src,
        dst_ref=dst,
        send_sem=send_sem,
        recv_sem=recv_sem,
        device_id=(row, seq),
        device_id_type=MESH,
    )


class Sems:
    def __init__(self, ref):
        self.ref = ref
        self.used = 0

    def take(self, count):
        first = self.used
        self.used += count
        assert self.used <= self.ref.shape[0]
        return [self.ref.at[first + i] for i in range(count)]


class Chain:
    def __init__(self, own, buf, base, row, seq, size, sems):
        self.own, self.buf, self.base = own, buf, base
        self.row, self.seq, self.size = row, seq, size
        self.sems = [[(sems.take(1)[0], sems.take(1)[0]) for _ in range(size - 1)] for _ in range(2)]
        (self.local,) = sems.take(1)

    def _copies(self, step):
        seq, size = self.seq, self.size
        out = []
        for way in range(2):
            sign = 1 - 2 * way
            block = seq - sign * (step - 1)
            peer = seq + sign
            going = (peer >= 0) & (peer < size) & (block >= 0) & (block < size)
            slot = self.buf.at[self.base + block]
            src = self.own if step == 1 else slot
            copy = functools.partial(remote, src, slot, *self.sems[way][step - 1], self.row, peer)
            come = seq - sign * step
            coming = (come >= 0) & (come < size)
            into = self.buf.at[self.base + come]
            arrive = functools.partial(remote, into, into, *self.sems[way][step - 1], self.row, peer)
            out.append((going, copy, coming, arrive))
        return out

    def keep(self):
        return pltpu.make_async_copy(self.own, self.buf.at[self.base + self.seq], self.local)

    def send(self, step):
        if step == 1:
            self.keep().start()
        for going, copy, _, _ in self._copies(step):
            pl.when(going)(lambda copy=copy: copy().start())

    def recv(self, step):
        for _, _, coming, arrive in self._copies(step):
            pl.when(coming)(lambda arrive=arrive: arrive().wait_recv())

    def finish(self):
        for step in range(1, self.size):
            for going, copy, _, _ in self._copies(step):
                pl.when(going)(lambda copy=copy: copy().wait_send())


class Scatter:
    def __init__(self, src, dst_of, row, seq, size, sems):
        self.src, self.dst_of = src, dst_of
        self.row, self.seq, self.size = row, seq, size
        self.sems = [(sems.take(1)[0], sems.take(1)[0]) for _ in range(size - 1)]
        (self.local,) = sems.take(1)

    def _to(self, step):
        peer = (self.seq + step) % self.size
        return remote(self.src.at[peer], self.dst_of(self.seq), *self.sems[step - 1], self.row, peer)

    def _from(self, step):
        peer = (self.seq + self.size - step) % self.size
        into = self.dst_of(peer)
        return remote(into, into, *self.sems[step - 1], self.row, peer)

    def keep(self):
        return pltpu.make_async_copy(self.src.at[self.seq], self.dst_of(self.seq), self.local)

    def send(self, step):
        self._to(step).start()

    def send_all(self):
        self.keep().start()
        for step in range(1, self.size):
            self.send(step)

    def recv(self):
        self.keep().wait()
        for step in range(1, self.size):
            self._from(step).wait_recv()

    def finish(self):
        for step in range(1, self.size):
            self._to(step).wait_send()


class Spread:
    def __init__(self, buf, row, seq, rows, size, sems):
        self.buf, self.row, self.seq, self.size = buf, row, seq, size
        bits = [1 << i for i in range(1, rows.bit_length() - 1)]
        self.stages = len(bits)
        self.orders = (bits, bits[::-1])
        self.half = buf.shape[2] // 2
        self.sems = [
            [[(sems.take(1)[0], sems.take(1)[0]) for _ in range(1 << j)] for j in range(self.stages)]
            for _ in range(2)
        ]
        self.core_sems = [(sems.take(1)[0], sems.take(1)[0])]
        self.core_sems += [
            (sems.take(1)[0], sems.take(1)[0]) for _ in range(2 * ((1 << self.stages) - 1))
        ]

    def _block(self, row, half):
        first = row * self.size
        if half is None:
            return self.buf.at[pl.ds(first, self.size)]
        return self.buf.at[pl.ds(first, self.size), :, pl.ds(half * self.half, self.half)]

    def _rows(self, start, half, stage):
        rows = [start]
        for bit in self.orders[half][:stage]:
            rows += [flip(row, bit) for row in rows]
        return rows

    def _pairs(self, stage):
        out = []
        for half in range(2):
            bit = self.orders[half][stage]
            peer = flip(self.row, bit)
            for i, row in enumerate(self._rows(self.row, half, stage)):
                here = self._block(row, half)
                there = self._block(flip(row, bit), half)
                pair = self.sems[half][stage][i]
                out.append((here, there, pair, peer))
        return out

    def _core(self, index, block):
        return remote(block, block, *self.core_sems[index], flip(self.row, 1), self.seq)

    def _core_blocks(self, row):
        out = [[self._block(row, None)]]
        for stage in range(self.stages):
            out.append([])
            for half in range(2):
                bit = self.orders[half][stage]
                for other in self._rows(row, half, stage):
                    out[-1].append(self._block(flip(other, bit), half))
        return out

    def _first(self, stage):
        return 0 if stage == 0 else 1 + 2 * ((1 << (stage - 1)) - 1)

    def send(self, stage):
        if stage < self.stages:
            for here, _, pair, peer in self._pairs(stage):
                remote(here, here, *pair, peer, self.seq).start()
        for i, block in enumerate(self._core_blocks(self.row)[stage]):
            self._core(self._first(stage) + i, block).start()

    def recv(self, stage):
        for _, there, pair, peer in self._pairs(stage):
            remote(there, there, *pair, peer, self.seq).wait_recv()

    def finish(self):
        for stage in range(self.stages):
            for here, _, pair, peer in self._pairs(stage):
                remote(here, here, *pair, peer, self.seq).wait_send()
        mine, theirs = self._core_blocks(self.row), self._core_blocks(flip(self.row, 1))
        for stage in range(self.stages + 1):
            for i, block in enumerate(theirs[stage]):
                self._core(self._first(stage) + i, block).wait_recv()
            for i, block in enumerate(mine[stage]):
                self._core(self._first(stage) + i, block).wait_send()


def greet(row, seq, rows, size):
    barrier = pltpu.get_barrier_semaphore()
    count = 0
    bit = 1
    while bit < rows:
        pl.semaphore_signal(barrier, inc=1, device_id=(flip(row, bit), seq), device_id_type=MESH)
        bit *= 2
        count += 1
    for step in range(1, size):
        pl.semaphore_signal(barrier, inc=1, device_id=(row, (seq + step) % size), device_id_type=MESH)
        count += 1
    pl.semaphore_wait(barrier, count)


def forward_kernel(
    rows, size, shard, group,
    x, wq, wp, w1, w2, small, cos, sin, pic_col, pic_row,
    wp_all, w1_all, w2_all, att, small_sum, xg, qkv, wq_full, lse,
    normed, wq_buf, small_buf, wq_wide, v_turn, o_part, o_send, sem_ref,
):
    row, seq = lax.axis_index("row"), lax.axis_index("seq")
    toks, width = x.shape
    length = toks * size
    part = group * LANE
    sems = Sems(sem_ref)
    base = row * size
    g_small = Chain(small, small_buf, base, row, seq, size, sems)
    g_wp = Chain(wp, wp_all, base, row, seq, size, sems)
    g_w1 = Chain(w1, w1_all, base, row, seq, size, sems)
    g_w2 = Chain(w2, w2_all, base, row, seq, size, sems)
    g_x = Chain(x, xg, 0, row, seq, size, sems)
    a_wq = Scatter(wq, lambda j: wq_buf.at[base + j], row, seq, size, sems)
    s_small = Spread(small_buf, row, seq, rows, size, sems)
    s_wq = Spread(wq_buf, row, seq, rows, size, sems)
    s_wp = Spread(wp_all, row, seq, rows, size, sems)
    s_w1 = Spread(w1_all, row, seq, rows, size, sems)
    s_w2 = Spread(w2_all, row, seq, rows, size, sems)
    a_o = Scatter(o_send, lambda j: att.at[j], row, seq, size, sems)
    last = s_small.stages

    greet(row, seq, rows, size)
    g_small.send(1)
    a_wq.send_all()
    g_wp.send(1)
    g_w1.send(1)
    g_x.send(1)
    for step in range(1, size):
        for g in (g_small, g_wp, g_w1):
            g.recv(step)
            if step < size - 1:
                g.send(step + 1)
    a_wq.recv()
    for g in (g_small, g_wp, g_w1, g_x):
        g.keep().wait()
    for s in (s_small, s_wq, s_wp, s_w1):
        s.send(0)
    for stage in range(last):
        for s in (s_small, s_wq):
            s.recv(stage)
            s.send(stage + 1)
    s_small.finish()
    s_wq.finish()

    total = jnp.zeros(small_sum.shape, jnp.float32)
    for i in range(rows * size):
        total += small_buf[i].astype(jnp.float32)
    small_sum[...] = total
    bias = jnp.zeros((1, 3 * part), jnp.float32)
    for i in range(rows * size):
        block = wq_buf[i].astype(jnp.float32)
        wq_wide[pl.ds(i * shard, shard), :] = block[:shard]
        bias += block[shard : shard + 1]
    for i in range(0, width, LANE):
        wq_full[pl.ds(i, LANE), :] = wq_wide[pl.ds(i, LANE), :].astype(jnp.bfloat16)
    wq_wide[0:1, :] = bias

    def project(chunk):
        first = pl.multiple_of(chunk * toks, toks)
        block = 128

        def norm(i, carry):
            at = pl.multiple_of(i * block, block)
            values = xg[chunk, pl.ds(at, block), :].astype(jnp.float32)
            centered = values - jnp.mean(values, axis=-1, keepdims=True)
            variance = jnp.mean(centered * centered, axis=-1, keepdims=True)
            out = centered * lax.rsqrt(variance + NORM_EPS) * small_sum[0:1, :] + small_sum[1:2, :]
            normed[pl.ds(pl.multiple_of(first + at, block), block), :] = out.astype(jnp.bfloat16)
            return carry

        lax.fori_loop(0, toks // block, norm, 0)
        span = pl.ds(first, toks)

        def turned(i, carry):
            at = pl.multiple_of(i * 2 * LANE, 2 * LANE)
            mixed = jnp.dot(normed[span, :], wq_full[:, pl.ds(at, 2 * LANE)], preferred_element_type=jnp.float32)
            mixed += wq_wide[0:1, pl.ds(at, 2 * LANE)]
            for j in range(2):
                u = mixed[:, j * LANE : (j + 1) * LANE]
                u = u * cos[span, :] + pltpu.roll(u, LANE // 2, 1) * sin[span, :]
                qkv[span, pl.ds(pl.multiple_of(at + j * LANE, LANE), LANE)] = u.astype(jnp.bfloat16)
            return carry

        lax.fori_loop(0, part // LANE, turned, 0)

        def plain(i, carry):
            at = pl.multiple_of(i * 2 * LANE, 2 * LANE)
            col = pl.ds(pl.multiple_of(2 * part + at, 2 * LANE), 2 * LANE)
            mixed = jnp.dot(normed[span, :], wq_full[:, col], preferred_element_type=jnp.float32)
            mixed += wq_wide[0:1, col]
            qkv[span, col] = mixed.astype(jnp.bfloat16)
            v_turn[pl.ds(at, 2 * LANE), span] = mixed.T.astype(jnp.bfloat16)
            return carry

        lax.fori_loop(0, part // (2 * LANE), plain, 0)

    project(seq)
    for step in range(1, size):
        g_x.recv(step)
        if step < size - 1:
            g_x.send(step + 1)
        if step == 1:
            g_w2.send(1)
            if last > 0:
                for s in (s_wp, s_w1):
                    s.recv(0)
                    s.send(1)

        def arrived(i, carry):
            chunk = seq + (2 * i - 1) * step
            pl.when((chunk >= 0) & (chunk < size))(lambda: project(chunk))
            return carry

        lax.fori_loop(0, 2, arrived, 0)

    def attend(chunk):
        def one(i, carry):
            head = i % group
            block = chunk * (toks // QBLK) + i // group
            span = pl.ds(pl.multiple_of(block * QBLK, QBLK), QBLK)
            at = pl.multiple_of(head * LANE, LANE)
            q = qkv[span, pl.ds(at, LANE)]
            k = qkv[:, pl.ds(pl.multiple_of(part + at, LANE), LANE)]
            scores = lax.dot_general(k, q, (((1,), (1,)), ((), ())), preferred_element_type=jnp.float32)
            scores = jnp.where(pic_col[...] == pic_row[:, span], scores, -1e30)
            top = jnp.max(scores, axis=0, keepdims=True)
            weights = jnp.exp2((scores - top) * EXP_SCALE)
            sums = jnp.sum(weights, axis=0, keepdims=True)
            out = jnp.dot(v_turn[pl.ds(at, LANE), :], weights.astype(jnp.bfloat16), preferred_element_type=jnp.float32)
            out = out / sums
            o_part[pl.ds(pl.multiple_of(head * HEAD_DIM, 8), HEAD_DIM), :] = out[:HEAD_DIM]
            lse[head, :, span] = top * EXP_SCALE + jnp.log2(sums)

            @pl.when(head == group - 1)
            def _():
                within = pl.multiple_of((i // group) * QBLK, QBLK)
                o_send[chunk, pl.ds(within, QBLK), :] = o_part[...].T.astype(jnp.bfloat16)

            return carry

        lax.fori_loop(0, group * (toks // QBLK), one, 0)

    o_part[...] = jnp.zeros_like(o_part)
    for step in range(1, size + 1):
        attend((seq + step) % size)
        if step < size:
            a_o.send(step)
        else:
            a_o.keep().start()
        if step < size:
            g_w2.recv(step)
            if step < size - 1:
                g_w2.send(step + 1)
            else:
                g_w2.keep().wait()
                s_w2.send(0)
        if step == 1:
            for stage in range(1, last):
                for s in (s_wp, s_w1):
                    s.recv(stage)
                    s.send(stage + 1)
    for stage in range(last):
        s_w2.recv(stage)
        s_w2.send(stage + 1)
    for s in (s_wp, s_w1, s_w2):
        s.finish()
    a_o.recv()
    for g in (g_small, g_wp, g_w1, g_w2, g_x, a_wq, a_o):
        g.finish()


def forward_call(mesh, x, wq, wp, w1, w2, small, cos, sin, pic_col, pic_row):
    rows, size = mesh.shape["row"], mesh.shape["seq"]
    toks, width = x.shape
    length = toks * size
    group = HEADS // size
    part = group * LANE
    shard = wp.shape[0]
    out_width = round_up(group * HEAD_DIM, LANE)
    total = rows * size
    bf, f32 = jnp.bfloat16, jnp.float32
    shape = jax.ShapeDtypeStruct
    return pl.pallas_call(
        functools.partial(forward_kernel, rows, size, shard, group),
        out_shape=(
            shape((total,) + wp.shape, bf),
            shape((total,) + w1.shape, bf),
            shape((total,) + w2.shape, bf),
            shape((size, toks, out_width), bf),
            shape(small.shape, f32),
            shape((size, toks, width), bf),
            shape((length, 3 * part), bf),
            shape((width, 3 * part), bf),
            shape((group, 1, length), f32),
        ),
        in_specs=[ANY] * 6 + [VMEM] * 4,
        out_specs=(ANY,) * 4 + (VMEM,) * 5,
        scratch_shapes=[
            pltpu.VMEM((length, width), bf),
            pltpu.VMEM((total,) + wq.shape[1:], bf),
            pltpu.VMEM((total,) + small.shape, bf),
            pltpu.VMEM((width, 3 * part), f32),
            pltpu.VMEM((part, length), bf),
            pltpu.VMEM((out_width, QBLK), f32),
            pltpu.VMEM((size, toks, out_width), bf),
            pltpu.SemaphoreType.DMA((512,)),
        ],
        compiler_params=pltpu.CompilerParams(
            collective_id=0, has_side_effects=True, vmem_limit_bytes=62 * 1024 * 1024
        ),
        name="forward",
    )(x, wq, wp, w1, w2, small, cos, sin, pic_col, pic_row)


def token_layout(lengths, widths, row_len):
    pic_ends = jnp.cumsum(lengths)
    pic_starts = pic_ends - lengths
    positions = jnp.arange(row_len, dtype=jnp.int32)
    picture = jnp.sum((positions[:, None] >= pic_ends[None, :]).astype(jnp.int32), axis=1)
    matches = picture[:, None] == jnp.arange(lengths.shape[0], dtype=jnp.int32)[None, :]
    first = jnp.sum(jnp.where(matches, pic_starts[None, :], 0), axis=1)
    grid_width = jnp.maximum(jnp.sum(jnp.where(matches, widths[None, :], 0), axis=1), 1)
    within = positions - first
    down = (within // grid_width).astype(jnp.float32)
    side = (within % grid_width).astype(jnp.float32)
    quarter = HEAD_DIM // 4
    frequency = 1.0 / 10000.0 ** (jnp.arange(quarter, dtype=jnp.float32) * 4.0 / HEAD_DIM)
    angles = jnp.concatenate([down[:, None] * frequency, side[:, None] * frequency], axis=-1)
    cosine, sine = jnp.cos(angles), jnp.sin(angles)
    gap = jnp.zeros((row_len, LANE // 2 - HALF), jnp.float32)
    return (
        picture,
        jnp.concatenate([cosine, gap, cosine, gap], axis=-1),
        jnp.concatenate([-sine, gap, sine, gap], axis=-1),
    )


def head_columns(values, size, pieces):
    a = values.shape[0]
    group = HEADS // size
    values = values.reshape(a, size, group, pieces, HEAD_DIM // pieces)
    values = jnp.pad(values, ((0, 0),) * 4 + ((0, (LANE - HEAD_DIM) // pieces),))
    return values.reshape(a, size, group * LANE).transpose(1, 0, 2)


def head_columns_back(values, pieces):
    size, a, lanes = values.shape
    group = lanes // LANE
    values = values.transpose(1, 0, 2).reshape(a, size, group, pieces, LANE // pieces)
    return values[..., : HEAD_DIM // pieces].reshape(a, HEADS * HEAD_DIM)


def qkv_columns(values, size):
    width = HEADS * HEAD_DIM
    return jnp.concatenate(
        [
            head_columns(values[:, :width], size, 2),
            head_columns(values[:, width : 2 * width], size, 2),
            head_columns(values[:, 2 * width :], size, 1),
        ],
        axis=-1,
    )


def add_blocks(out, first, second, count, block, first_map, second_map):
    def body(a, b, o):
        o[...] = (a[...].astype(jnp.float32) + b[...].astype(jnp.float32)).astype(o.dtype)

    pltpu.emit_pipeline(
        body,
        grid=(count,),
        in_specs=[pl.BlockSpec(block, first_map), pl.BlockSpec(block, second_map)],
        out_specs=[pl.BlockSpec(block, lambda i: (i, 0, 0))],
    )(first, second, out)


class Reduce:
    def __init__(self, src, core, acc, come, done, row, seq, rows, size, sems, in_vmem):
        self.src, self.core, self.acc, self.come, self.done = src, core, acc, come, done
        self.row, self.seq, self.size, self.in_vmem = row, seq, size, in_vmem
        bits = [1 << i for i in range(1, rows.bit_length() - 1)]
        self.orders = (bits, bits[::-1])
        self.stages = len(bits)
        self.chips = rows // 2
        self.half = src.shape[2] // 2
        self.block = (size, src.shape[1], self.half)
        self.core_sems = [(sems.take(1)[0], sems.take(1)[0]) for _ in range(self.chips)]
        self.sems = [[(sems.take(1)[0], sems.take(1)[0]) for _ in bits] for _ in range(2)]

    def _core_copies(self):
        size = self.size
        other = flip(self.row, 1)
        for chip in range(self.chips):
            theirs = 2 * chip + other % 2
            yield remote(
                self.src.at[pl.ds(theirs * size, size)],
                self.core.at[pl.ds(chip * size, size)],
                *self.core_sems[chip],
                other,
                self.seq,
            )

    def core_send(self):
        for copy in self._core_copies():
            copy.start()

    def _chip(self, half, i):
        chip = self.row // 2
        for k in range(self.stages):
            bit = self.orders[half][self.stages - 1 - k] // 2
            chip = chip + ((i // (1 << k)) % 2) * (flip(chip, bit) - chip)
        return chip

    def core_add(self):
        size = self.size
        for copy in self._core_copies():
            copy.wait_recv()
        core = self.row % 2
        for half in range(2):
            if self.in_vmem:
                cols = pl.ds(half * self.half, self.half)

                def body(i, carry, half=half, cols=cols):
                    chip, z = self._chip(half, i // size), i % size
                    mine = self.src[(2 * chip + core) * size + z, :, cols].astype(jnp.float32)
                    total = mine + self.core[chip * size + z, :, cols].astype(jnp.float32)
                    self.acc[half][i] = total.astype(self.acc[half].dtype)
                    return carry

                lax.fori_loop(0, self.chips * size, body, 0)
            else:
                add_blocks(
                    self.acc[half],
                    self.src,
                    self.core,
                    self.chips,
                    self.block,
                    lambda i, half=half: (2 * self._chip(half, i) + core, 0, half),
                    lambda i, half=half: (self._chip(half, i), 0, half),
                )

    def _held(self, half, stage):
        return self.acc[half] if stage == 0 else self.done[half][stage - 1]

    def _stage_copy(self, half, stage):
        count = (self.chips >> (stage + 1)) * self.size
        return remote(
            self._held(half, stage).at[pl.ds(count, count)],
            self.come[half][stage],
            *self.sems[half][stage],
            flip(self.row, self.orders[half][stage]),
            self.seq,
        )

    def stage_send(self, stage):
        for half in range(2):
            self._stage_copy(half, stage).start()

    def stage_add(self, stage):
        count = self.chips >> (stage + 1)
        for half in range(2):
            self._stage_copy(half, stage).wait_recv()
            held, come, done = self._held(half, stage), self.come[half][stage], self.done[half][stage]
            if self.in_vmem:

                def body(i, carry, held=held, come=come, done=done):
                    total = held[i].astype(jnp.float32) + come[i].astype(jnp.float32)
                    done[i] = total.astype(done.dtype)
                    return carry

                lax.fori_loop(0, count * self.size, body, 0)
            else:
                plain = lambda i: (i, 0, 0)
                add_blocks(done, held, come, count, self.block, plain, plain)

    @property
    def kept(self):
        return [self._held(half, self.stages) for half in range(2)]

    def finish(self):
        for copy in self._core_copies():
            copy.wait_send()
        for half in range(2):
            for stage in range(self.stages):
                self._stage_copy(half, stage).wait_send()


def reduce_shapes(src, rows, size):
    a, b = src[1], src[2] // 2
    chips = rows // 2
    stages = rows.bit_length() - 2
    shapes = [(chips * size, a, 2 * b)] + [(chips * size, a, b)] * 2
    for _ in range(2):
        for stage in range(stages):
            shapes += [((chips >> (stage + 1)) * size, a, b)] * 2
    return shapes + [(size, a, b)] * 2


def reduce_refs(refs, rows):
    stages = rows.bit_length() - 2
    core, acc, rest = refs[0], refs[1:3], refs[3:-2]
    come = [[rest[2 * (half * stages + j)] for j in range(stages)] for half in range(2)]
    done = [[rest[2 * (half * stages + j) + 1] for j in range(stages)] for half in range(2)]
    return (core, acc, come, done), refs[-2:]


class ChainSum:
    def __init__(self, part, slots, row, seq, size, sems):
        self.part, self.slots = part, slots
        self.row, self.seq, self.size = row, seq, size
        self.sems = [[(sems.take(1)[0], sems.take(1)[0]) for _ in range(size - 1)] for _ in range(2)]

    def _copy(self, way, step):
        sign = 1 - 2 * way
        peer = self.seq + sign
        chunk = self.seq + sign * (self.size - step)
        ok = (chunk >= 0) & (chunk < self.size) & (peer >= 0) & (peer < self.size)
        slot = self.slots.at[way * (self.size - 1) + step - 1]
        return ok, lambda: remote(self.part(chunk), slot, *self.sems[way][step - 1], self.row, peer)

    def send(self, step):
        for way in range(2):
            ok, copy = self._copy(way, step)
            pl.when(ok)(lambda copy=copy: copy().start())

    def recv(self, step, use):
        for way in range(2):
            sign = 1 - 2 * way
            source = self.seq - sign
            chunk = self.seq + sign * (self.size - step - 1)
            ok = (chunk >= 0) & (chunk < self.size) & (source >= 0) & (source < self.size)
            slot = self.slots.at[way * (self.size - 1) + step - 1]

            def take(way=way, chunk=chunk, slot=slot):
                remote(slot, slot, *self.sems[way][step - 1], self.row, self.seq + 1 - 2 * way).wait_recv()
                use(chunk, slot)

            pl.when(ok)(take)

    def finish(self):
        for step in range(1, self.size):
            for way in range(2):
                ok, copy = self._copy(way, step)
                pl.when(ok)(lambda copy=copy: copy().wait_send())


def backward_kernel(rows, size, shard, group, counts, *refs):
    refs = list(refs)

    def take(count):
        out = refs[:count]
        del refs[:count]
        return out

    g2, g1, gp, gs, go, xg, qkv, cos, sin, pic_col, pic_row, wq_full, lse, small = take(14)
    dx_out, dq_out, gs_out, g2_out, g1_out, gp_out = take(6)
    slots = take(1)[0]
    big = [take(counts) for _ in range(3)]
    vm = [take(counts) for _ in range(2)]
    (qkv_s, do_in, do_full, k_turn, gk_sum, gv_sum, gm, n_turn, x_chunk, dq, rows_sum, sem_ref, load_sem) = refs

    row, seq = lax.axis_index("row"), lax.axis_index("seq")
    length, part = qkv.shape[0], group * LANE
    toks = length // size
    width = xg.shape[2]
    base = row * size
    sems = Sems(sem_ref)
    f32, bf = jnp.float32, jnp.bfloat16

    a_do = Scatter(go, lambda j: do_in.at[j], row, seq, size, sems)
    reducers, z_moves = [], []
    for src, bufs, in_vmem in (
        (g2, big[0], False), (g1, big[1], False), (gp, big[2], False), (gs, vm[0], True), (dq, vm[1], True),
    ):
        inner, z_refs = reduce_refs(bufs, rows)
        r = Reduce(src, *inner, row, seq, rows, size, sems, in_vmem)
        reducers.append(r)
        z_moves.append(
            [Scatter(kept, lambda j, to=to: to.at[j], row, seq, size, sems) for kept, to in zip(r.kept, z_refs)]
        )
    r2, r1, rp, rs, rq = reducers

    def z_send(which):
        for move in z_moves[which]:
            move.send_all()

    dx = ChainSum(lambda c: qkv_s.at[pl.ds(c * toks, toks), pl.ds(0, width)], slots, row, seq, size, sems)

    greet(row, seq, rows, size)
    a_do.send_all()
    load_qkv = pltpu.make_async_copy(qkv, qkv_s.at[:, pl.ds(0, 3 * part)], load_sem.at[0])
    load_qkv.start()
    for r in (r2, r1, rp, rs):
        r.core_send()
    for r in (r2, r1, rp, rs):
        r.core_add()
        r.stage_send(0)
    load_qkv.wait()
    for i in range(0, part, LANE):
        k_turn[pl.ds(i, LANE), :] = qkv_s[:, pl.ds(part + i, LANE)].astype(f32).T.astype(bf)
    a_do.recv()

    def widen(i, carry):
        chunk, at = i // (toks // QBLK), (i % (toks // QBLK)) * QBLK
        values = do_in[chunk, pl.ds(pl.multiple_of(at, QBLK), QBLK), :].astype(f32)
        lanes = lax.broadcasted_iota(jnp.int32, (QBLK, LANE), 1)
        for head in range(group):
            first = head * HEAD_DIM
            start = first // LANE * LANE
            window = values[:, start : min(start + 2 * LANE, values.shape[1])]
            shift = first - start
            if shift:
                window = pltpu.roll(window, window.shape[1] - shift, 1)
            piece = jnp.where(lanes < HEAD_DIM, window[:, :LANE], 0.0)
            do_full[pl.ds(pl.multiple_of(i * QBLK, QBLK), QBLK), pl.ds(head * LANE, LANE)] = piece.astype(bf)
        return carry

    lax.fori_loop(0, length // QBLK, widen, 0)

    def unturn(grad, span):
        return grad * cos[span, :] + pltpu.roll(grad * sin[span, :], LANE // 2, 1)

    def head_back(head):
        at = pl.multiple_of(head * LANE, LANE)
        lane = pl.ds(at, LANE)
        k_lane = pl.ds(pl.multiple_of(part + at, LANE), LANE)
        v_lane = pl.ds(pl.multiple_of(2 * part + at, LANE), LANE)
        gk_sum[...] = jnp.zeros_like(gk_sum)
        gv_sum[...] = jnp.zeros_like(gv_sum)

        def one(i, carry):
            span = pl.ds(pl.multiple_of(i * QBLK, QBLK), QBLK)
            q = qkv_s[span, lane]
            do = do_full[span, lane]
            scores = lax.dot_general(
                qkv_s[:, k_lane], q, (((1,), (1,)), ((), ())), preferred_element_type=f32
            )
            probs = jnp.exp2(scores * EXP_SCALE - lse[head, :, span])
            probs = jnp.where(pic_col[...] == pic_row[:, span], probs, 0.0)
            gv_sum[...] += jnp.dot(probs.astype(bf), do, preferred_element_type=f32)
            grad_probs = lax.dot_general(
                qkv_s[:, v_lane], do, (((1,), (1,)), ((), ())), preferred_element_type=f32
            )
            delta = jnp.sum(probs * grad_probs, axis=0, keepdims=True)
            grad_scores = (probs * (grad_probs - delta)).astype(bf)
            gk_sum[...] += jnp.dot(grad_scores, q, preferred_element_type=f32)
            gq = jnp.dot(k_turn[lane, :], grad_scores, preferred_element_type=f32).T
            gm[span, lane] = unturn(gq * SCALE, span).astype(bf)
            return carry

        lax.fori_loop(0, length // QBLK, one, 0)

        def close(i, carry):
            span = pl.ds(pl.multiple_of(i * QBLK, QBLK), QBLK)
            gm[span, k_lane] = unturn(gk_sum[span, :] * SCALE, span).astype(bf)
            gm[span, v_lane] = gv_sum[span, :].astype(bf)
            return carry

        lax.fori_loop(0, length // QBLK, close, 0)

    def heads_back(first, count):
        def body(i, carry):
            head_back(first + i)
            return carry

        lax.fori_loop(0, count, body, 0)

    steps = []
    for stage in range(r2.stages):
        for which in (0, 1, 2, 3):

            def step(which=which, stage=stage):
                r = reducers[which]
                r.stage_add(stage)
                if stage + 1 < r.stages:
                    r.stage_send(stage + 1)
                else:
                    z_send(which)

            steps.append(step)
    done_steps = 0
    for head in range(group):
        heads_back(head, 1)
        upto = len(steps) * (head + 1) // group
        for step in steps[done_steps:upto]:
            step()
        done_steps = upto

    rows_sum[...] = jnp.zeros_like(rows_sum)

    def chunk_back(chunk):
        load = pltpu.make_async_copy(xg.at[chunk], x_chunk, load_sem.at[1])
        load.start()
        load.wait()
        block = LANE

        def one(i, carry):
            at = pl.multiple_of(i * block, block)
            span = pl.ds(pl.multiple_of(chunk * toks + at, block), block)
            values = x_chunk[pl.ds(at, block), :].astype(f32)
            centered = values - jnp.mean(values, axis=-1, keepdims=True)
            variance = jnp.mean(centered * centered, axis=-1, keepdims=True)
            hat = centered * lax.rsqrt(variance + NORM_EPS)
            n_turn[:, span] = (hat * small[0:1, :] + small[1:2, :]).T.astype(bf)
            mixed = gm[span, :]
            grad = lax.dot_general(mixed, wq_full[...], (((1,), (1,)), ((), ())), preferred_element_type=f32)
            rows_sum[0:1, pl.ds(0, 3 * part)] += jnp.sum(mixed.astype(f32), axis=0, keepdims=True)
            rows_sum[1:2, pl.ds(0, width)] += jnp.sum(grad * hat, axis=0, keepdims=True)
            rows_sum[2:3, pl.ds(0, width)] += jnp.sum(grad, axis=0, keepdims=True)
            qkv_s[span, pl.ds(0, width)] = grad.astype(bf)
            return carry

        lax.fori_loop(0, toks // block, one, 0)

    def far_chunks(distance):
        def body(i, carry):
            chunk = seq + (2 * i - 1) * distance
            pl.when((chunk >= 0) & (chunk < size))(lambda: chunk_back(chunk))
            return carry

        lax.fori_loop(0, 2 if distance else 1, body, 0)

    for step in range(1, size):
        far_chunks(size - step)
        if step == 1:
            dx.send(1)
    far_chunks(0)

    lines = -(-width // (3 * part))
    tall = width // 2
    per = tall // shard
    for i in range(2):

        def columns(j, carry, i=i):
            cols = pl.ds(pl.multiple_of(j * 2 * LANE, 2 * LANE), 2 * LANE)
            grad = jnp.dot(n_turn[pl.ds(i * tall, tall), :], gm[:, cols], preferred_element_type=f32).astype(bf)
            for s in range(per):
                dq[i * per + s, pl.ds(0, shard), cols] = grad[s * shard : (s + 1) * shard]
            return carry

        lax.fori_loop(0, 3 * part // (2 * LANE), columns, 0)
    tail = [rows_sum[0:1, pl.ds(0, 3 * part)]]
    for line in (1, 2):
        tail += [rows_sum[line : line + 1, pl.ds(k * 3 * part, 3 * part)] for k in range(lines)]
    tail = jnp.concatenate(tail, axis=0).astype(bf)

    def put_tail(i, carry):
        dq[i, pl.ds(shard, tail.shape[0]), :] = tail
        return carry

    lax.fori_loop(0, rows * size, put_tail, 0)
    rq.core_send()

    def add_sum(chunk, slot):
        load = pltpu.make_async_copy(slot, x_chunk, load_sem.at[1])
        load.start()
        load.wait()
        span = pl.ds(pl.multiple_of(chunk * toks, toks), toks)
        mine = qkv_s[span, pl.ds(0, width)].astype(f32)
        qkv_s[span, pl.ds(0, width)] = (mine + x_chunk[...].astype(f32)).astype(bf)

    for step in range(1, size):
        if step == size - 1:
            dx_out[...] = qkv_s[pl.ds(pl.multiple_of(seq * toks, toks), toks), pl.ds(0, width)].astype(f32)

            def last_sum(chunk, slot):
                load = pltpu.make_async_copy(slot, x_chunk, load_sem.at[1])
                load.start()
                load.wait()
                dx_out[...] += x_chunk[...].astype(f32)

        else:
            dx.recv(step, add_sum)
            dx.send(step + 1)
        if step == 1:
            rq.core_add()
            rq.stage_send(0)
        elif step == 2:
            for stage in range(rq.stages):
                rq.stage_add(stage)
                if stage + 1 < rq.stages:
                    rq.stage_send(stage + 1)
            z_send(4)

    def z_sum(which, out):
        for half, move in enumerate(z_moves[which]):
            move.recv()

    z_buf = [reduce_refs(bufs, rows)[1] for bufs in big + vm]
    for which, out in ((0, g2_out), (1, g1_out), (2, gp_out)):
        z_sum(which, out)
        half_cols = reducers[which].half
        for half in range(2):

            def body(a, o):
                total = a[0].astype(f32)
                for z in range(1, size):
                    total += a[z].astype(f32)
                o[...] = total

            pltpu.emit_pipeline(
                body,
                grid=(1,),
                in_specs=[pl.BlockSpec(reducers[which].block, lambda i: (0, 0, 0))],
                out_specs=[pl.BlockSpec((reducers[which].block[1], half_cols), lambda i, half=half: (0, half))],
            )(z_buf[which][half], out)
    z_sum(3, None)
    for half in range(2):
        total = z_buf[3][half][0]
        for z in range(1, size):
            total += z_buf[3][half][z]
        gs_out[:, pl.ds(half * LANE, LANE)] = total
    z_sum(4, None)
    for half in range(2):
        dq_out[:, :, pl.ds(half * rq.half, rq.half)] = z_buf[4][half][...]
    dx.recv(size - 1, last_sum)
    for r in reducers:
        r.finish()
    for moves in z_moves:
        for move in moves:
            move.finish()
    a_do.finish()
    dx.finish()


def backward_call(mesh, g2, g1, gp, gs, go, xg, qkv, cos, sin, pic_col, pic_row, wq_full, lse, small, tall):
    rows, size = mesh.shape["row"], mesh.shape["seq"]
    _, toks, width = xg.shape
    length = toks * size
    group = HEADS // size
    part = group * LANE
    shard = gp.shape[1]
    total = rows * size
    bf, f32 = jnp.bfloat16, jnp.float32
    shape = jax.ShapeDtypeStruct
    dq_shape = (total, tall, 3 * part)
    big = [[shape(s, bf) for s in reduce_shapes(g.shape, rows, size)] for g in (g2, g1, gp)]
    vm = [[pltpu.VMEM(s, t) for s in reduce_shapes(d, rows, size)] for d, t in ((gs.shape, f32), (dq_shape, bf))]
    counts = len(vm[0])
    outs = (
        shape((toks, width), f32),
        shape((size, tall, 3 * part), bf),
        shape(gs.shape[1:], f32),
        shape(g2.shape[1:], f32),
        shape(g1.shape[1:], f32),
        shape(gp.shape[1:], f32),
        shape((2 * (size - 1), toks, width), bf),
        *big[0], *big[1], *big[2],
    )
    wide = max(3 * part, width)
    results = pl.pallas_call(
        functools.partial(backward_kernel, rows, size, shard, group, counts),
        out_shape=outs,
        in_specs=[ANY] * 3 + [VMEM] + [ANY] * 3 + [VMEM] * 7,
        out_specs=(VMEM,) * 3 + (ANY,) * (len(outs) - 3),
        scratch_shapes=[
            *vm[0], *vm[1],
            pltpu.VMEM((length, wide), bf),
            pltpu.VMEM(go.shape, bf),
            pltpu.VMEM((length, part), bf),
            pltpu.VMEM((part, length), bf),
            pltpu.VMEM((length, LANE), f32),
            pltpu.VMEM((length, LANE), f32),
            pltpu.VMEM((length, 3 * part), bf),
            pltpu.VMEM((width, length), bf),
            pltpu.VMEM((toks, width), bf),
            pltpu.VMEM(dq_shape, bf),
            pltpu.VMEM((8, round_up(width, 3 * part)), f32),
            pltpu.SemaphoreType.DMA((512,)),
            pltpu.SemaphoreType.DMA((2,)),
        ],
        compiler_params=pltpu.CompilerParams(
            collective_id=1, has_side_effects=True, vmem_limit_bytes=62 * 1024 * 1024
        ),
        name="backward",
    )(g2, g1, gp, gs, go, xg, qkv, cos, sin, pic_col, pic_row, wq_full, lse, small)
    return results[:6]


def layer_norm(values, norm_gain, norm_shift):
    centre = jnp.mean(values, axis=-1, keepdims=True)
    centered = values - centre
    variance = jnp.mean(centered * centered, axis=-1, keepdims=True)
    return centered * lax.rsqrt(variance + NORM_EPS) * norm_gain + norm_shift


def quick_gelu(values):
    return values * jax.nn.sigmoid(1.702 * values)


def pack_small(vectors, width, index, total):
    lines = []
    for values in vectors:
        full = values.shape[0] * total
        line = lax.dynamic_update_slice(jnp.zeros((full,), values.dtype), values, (index * values.shape[0],))
        lines.append(line.reshape(-1, width))
    lines = jnp.concatenate(lines, axis=0)
    return jnp.pad(lines, ((0, 16 - lines.shape[0]), (0, 0)))


def shards(
    mesh,
    activations,
    cotangent,
    pic_lengths,
    pic_widths,
    ln1_gain,
    ln1_bias,
    qkv_weight,
    qkv_bias,
    proj_weight,
    proj_bias,
    ln2_gain,
    ln2_bias,
    fc1_weight,
    fc1_bias,
    fc2_weight,
    fc2_bias,
):
    rows, size = mesh.shape["row"], mesh.shape["seq"]
    total = rows * size
    index = lax.axis_index("row") * size + lax.axis_index("seq")
    _, toks, width = activations.shape
    length = toks * size
    group = HEADS // size
    part = group * LANE
    shard = proj_weight.shape[0]
    bf, f32 = jnp.bfloat16, jnp.float32

    picture, cos, sin = token_layout(pic_lengths[0], pic_widths[0], length)
    small = pack_small((ln1_gain, ln1_bias, proj_bias, ln2_gain, ln2_bias, fc2_bias, fc1_bias), width, index, total)
    bias_line = lax.dynamic_update_slice(jnp.zeros((1, 3 * width), bf), qkv_bias[None], (0, index * qkv_bias.shape[0]))
    wq = jnp.concatenate([qkv_weight, bias_line], axis=0)
    wq = jnp.pad(qkv_columns(wq, size), ((0, 0), (0, round_up(shard + 1 + 2 * -(-width // (3 * part)), 16) - shard - 1), (0, 0)))
    x = activations[0]
    wp, w1, w2, att, lines, xg, qkv, wq_full, lse = forward_call(
        mesh, x, wq, proj_weight, fc1_weight, fc2_weight, small, cos, sin, picture[:, None], picture[None, :]
    )
    wp, w1, w2 = (w.reshape(-1, w.shape[-1]) for w in (wp, w1, w2))
    b_proj, gain_two, shift_two, b_down = lines[2], lines[3], lines[4], lines[5]
    b_up = lines[6 : 6 + w1.shape[1] // width].reshape(-1)

    inputs = x.astype(f32)
    attended = jnp.concatenate([att[g, :, : group * HEAD_DIM] for g in range(size)], axis=-1)
    middle = inputs + jnp.dot(attended, wp, preferred_element_type=f32) + b_proj
    normed_two, norm_two_back = jax.vjp(layer_norm, middle, gain_two, shift_two)
    normed_two_low = normed_two.astype(bf)
    before = jnp.dot(normed_two_low, w1, preferred_element_type=f32) + b_up
    activated, gelu_back = jax.vjp(quick_gelu, before)
    activated_low = activated.astype(bf)
    result = jnp.dot(activated_low, w2, preferred_element_type=f32) + b_down
    layer_out = (middle + result).astype(bf)

    grad_out = cotangent[0]
    grad_out_wide = grad_out.astype(f32)
    grad_down = jnp.dot(activated_low.T, grad_out, preferred_element_type=f32)
    grad_down_bias = jnp.sum(grad_out_wide, axis=0)
    (grad_before,) = gelu_back(jnp.dot(grad_out, w2.T, preferred_element_type=f32))
    grad_before_low = grad_before.astype(bf)
    grad_up_bias = jnp.sum(grad_before_low.astype(f32), axis=0)
    grad_up = jnp.dot(normed_two_low.T, grad_before_low, preferred_element_type=f32)
    grad_normed_two = jnp.dot(grad_before_low, w1.T, preferred_element_type=f32)
    grad_middle, grad_gain_two, grad_shift_two = norm_two_back(grad_normed_two)
    grad_middle = grad_middle + grad_out_wide
    grad_branch = grad_middle.astype(bf)
    grad_proj_bias = jnp.sum(grad_branch.astype(f32), axis=0)
    grad_proj = jnp.dot(attended.T, grad_branch, preferred_element_type=f32)
    grad_attended = jnp.dot(grad_branch, wp.T, preferred_element_type=f32).astype(bf)

    go = grad_attended.reshape(toks, size, group * HEAD_DIM).transpose(1, 0, 2)
    go = jnp.pad(go, ((0, 0), (0, 0), (0, round_up(group * HEAD_DIM, LANE) - group * HEAD_DIM)))
    smalls = jnp.concatenate(
        [
            g.reshape(total, -1)
            for g in (grad_proj_bias, grad_gain_two, grad_shift_two, grad_down_bias, grad_up_bias)
        ],
        axis=-1,
    )
    smalls = jnp.pad(smalls, ((0, 0), (0, 8 * 2 * LANE - smalls.shape[1]))).reshape(total, 8, 2 * LANE)
    grad_normed, grad_qkv, smalls, grad_down, grad_up, grad_proj = backward_call(
        mesh,
        grad_down.astype(bf).reshape(total, -1, width),
        grad_up.astype(bf).reshape(total, shard, -1),
        grad_proj.astype(bf).reshape(total, shard, width),
        smalls, go, xg, qkv, cos, sin, picture[:, None], picture[None, :], wq_full, lse, lines, wq.shape[1],
    )
    smalls = smalls.reshape(-1)
    grad_proj_bias, grad_gain_two, grad_shift_two, grad_down_bias = (
        smalls[i * shard : (i + 1) * shard] for i in range(4)
    )
    grad_up_bias = smalls[4 * shard : 4 * shard + fc1_bias.shape[0]]

    def natural(g):
        return jnp.concatenate(
            [
                head_columns_back(g[:, :, :part], 2),
                head_columns_back(g[:, :, part : 2 * part], 2),
                head_columns_back(g[:, :, 2 * part :], 1),
            ],
            axis=-1,
        )

    grad_qkv = grad_qkv.astype(f32)
    grad_bias = natural(grad_qkv[:, shard : shard + 1])[0]
    lined = -(-width // (3 * part))
    norm_lines = jnp.sum(grad_qkv[:, shard + 1 : shard + 1 + 2 * lined], axis=0).reshape(2, -1)[:, :width]
    grad_gain_one, grad_shift_one = (
        lax.dynamic_slice_in_dim(norm_lines[i], index * shard, shard) for i in range(2)
    )
    grad_qkv = natural(grad_qkv[:, :shard])
    grad_qk = lax.dynamic_slice_in_dim(grad_bias[: 2 * width], index * 2 * shard, 2 * shard)
    grad_value = lax.dynamic_slice_in_dim(grad_bias[2 * width :], index * shard, shard)
    _, norm_one_back = jax.vjp(layer_norm, inputs, lines[0], lines[1])
    grad_inputs, _, _ = norm_one_back(grad_normed)
    grad_acts = (grad_inputs + grad_middle).astype(bf)

    return (
        layer_out[None],
        grad_acts[None],
        grad_gain_one,
        grad_shift_one,
        grad_qkv,
        grad_qk,
        grad_value,
        grad_proj,
        grad_proj_bias,
        grad_gain_two,
        grad_shift_two,
        grad_up,
        grad_up_bias,
        grad_down,
        grad_down_bias,
    )


def solution(mesh):
    one, two = P(("row", "seq")), P(("row", "seq"), None)
    tokens = P("row", "seq", None)
    return jax.shard_map(
        functools.partial(shards, mesh),
        mesh=mesh,
        in_specs=(tokens, tokens, P("row", None), P("row", None), one, one, two, one, two, one, one, one, two, one, two, one),
        out_specs=(tokens, tokens, one, one, two, one, one, two, one, one, one, two, one, two, one),
        check_vma=False,
    )
```

```python
import functools
import math

import jax
import jax.numpy as jnp
from jax import lax
from jax.experimental import pallas as pl
from jax.experimental.pallas import tpu as pltpu
from jax.sharding import PartitionSpec as P

HEADS = 16
HEAD_DIM = 80
HALF = HEAD_DIM // 2
LANE = 128
NORM_EPS = 1e-06
SCALE = 1.0 / math.sqrt(HEAD_DIM)
LOG2E = 1.4426950408889634
EXP_SCALE = SCALE * LOG2E
QBLK = 256
MESH = pl.DeviceIdType.MESH
ANY = pl.BlockSpec(memory_space=pl.ANY)
VMEM = pl.BlockSpec(memory_space=pltpu.VMEM)


def round_up(value, unit):
    return -(-value // unit) * unit


def flip(index, bit):
    return index + bit - 2 * bit * ((index // bit) % 2)


def remote(src, dst, send_sem, recv_sem, row, seq):
    return pltpu.make_async_remote_copy(
        src_ref=src,
        dst_ref=dst,
        send_sem=send_sem,
        recv_sem=recv_sem,
        device_id=(row, seq),
        device_id_type=MESH,
    )


class Sems:
    def __init__(self, ref):
        self.ref = ref
        self.used = 0

    def take(self, count):
        first = self.used
        self.used += count
        assert self.used <= self.ref.shape[0]
        return [self.ref.at[first + i] for i in range(count)]


class Chain:
    def __init__(self, own, buf, base, row, seq, size, sems):
        self.own, self.buf, self.base = own, buf, base
        self.row, self.seq, self.size = row, seq, size
        self.sems = [[(sems.take(1)[0], sems.take(1)[0]) for _ in range(size - 1)] for _ in range(2)]
        (self.local,) = sems.take(1)

    def _copies(self, step):
        seq, size = self.seq, self.size
        out = []
        for way in range(2):
            sign = 1 - 2 * way
            block = seq - sign * (step - 1)
            peer = seq + sign
            going = (peer >= 0) & (peer < size) & (block >= 0) & (block < size)
            slot = self.buf.at[self.base + block]
            src = self.own if step == 1 else slot
            copy = functools.partial(remote, src, slot, *self.sems[way][step - 1], self.row, peer)
            come = seq - sign * step
            coming = (come >= 0) & (come < size)
            into = self.buf.at[self.base + come]
            arrive = functools.partial(remote, into, into, *self.sems[way][step - 1], self.row, peer)
            out.append((going, copy, coming, arrive))
        return out

    def keep(self):
        return pltpu.make_async_copy(self.own, self.buf.at[self.base + self.seq], self.local)

    def send(self, step):
        if step == 1:
            self.keep().start()
        for going, copy, _, _ in self._copies(step):
            pl.when(going)(lambda copy=copy: copy().start())

    def recv(self, step):
        for _, _, coming, arrive in self._copies(step):
            pl.when(coming)(lambda arrive=arrive: arrive().wait_recv())

    def finish(self):
        for step in range(1, self.size):
            for going, copy, _, _ in self._copies(step):
                pl.when(going)(lambda copy=copy: copy().wait_send())


class Scatter:
    def __init__(self, src, dst_of, row, seq, size, sems):
        self.src, self.dst_of = src, dst_of
        self.row, self.seq, self.size = row, seq, size
        self.sems = [(sems.take(1)[0], sems.take(1)[0]) for _ in range(size - 1)]
        (self.local,) = sems.take(1)

    def _to(self, step):
        peer = (self.seq + step) % self.size
        return remote(self.src.at[peer], self.dst_of(self.seq), *self.sems[step - 1], self.row, peer)

    def _from(self, step):
        peer = (self.seq + self.size - step) % self.size
        into = self.dst_of(peer)
        return remote(into, into, *self.sems[step - 1], self.row, peer)

    def keep(self):
        return pltpu.make_async_copy(self.src.at[self.seq], self.dst_of(self.seq), self.local)

    def send(self, step):
        self._to(step).start()

    def send_all(self):
        self.keep().start()
        for step in range(1, self.size):
            self.send(step)

    def recv(self):
        self.keep().wait()
        for step in range(1, self.size):
            self._from(step).wait_recv()

    def finish(self):
        for step in range(1, self.size):
            self._to(step).wait_send()


class Spread:
    def __init__(self, buf, row, seq, rows, size, sems):
        self.buf, self.row, self.seq, self.size = buf, row, seq, size
        bits = [1 << i for i in range(1, rows.bit_length() - 1)]
        self.stages = len(bits)
        self.orders = (bits, bits[::-1])
        self.half = buf.shape[2] // 2
        self.sems = [
            [[(sems.take(1)[0], sems.take(1)[0]) for _ in range(1 << j)] for j in range(self.stages)]
            for _ in range(2)
        ]
        self.core_sems = [(sems.take(1)[0], sems.take(1)[0])]
        self.core_sems += [
            (sems.take(1)[0], sems.take(1)[0]) for _ in range(2 * ((1 << self.stages) - 1))
        ]

    def _block(self, row, half):
        first = row * self.size
        if half is None:
            return self.buf.at[pl.ds(first, self.size)]
        return self.buf.at[pl.ds(first, self.size), :, pl.ds(half * self.half, self.half)]

    def _rows(self, start, half, stage):
        rows = [start]
        for bit in self.orders[half][:stage]:
            rows += [flip(row, bit) for row in rows]
        return rows

    def _pairs(self, stage):
        out = []
        for half in range(2):
            bit = self.orders[half][stage]
            peer = flip(self.row, bit)
            for i, row in enumerate(self._rows(self.row, half, stage)):
                here = self._block(row, half)
                there = self._block(flip(row, bit), half)
                pair = self.sems[half][stage][i]
                out.append((here, there, pair, peer))
        return out

    def _core(self, index, block):
        return remote(block, block, *self.core_sems[index], flip(self.row, 1), self.seq)

    def _core_blocks(self, row):
        out = [[self._block(row, None)]]
        for stage in range(self.stages):
            out.append([])
            for half in range(2):
                bit = self.orders[half][stage]
                for other in self._rows(row, half, stage):
                    out[-1].append(self._block(flip(other, bit), half))
        return out

    def _first(self, stage):
        return 0 if stage == 0 else 1 + 2 * ((1 << (stage - 1)) - 1)

    def send(self, stage):
        if stage < self.stages:
            for here, _, pair, peer in self._pairs(stage):
                remote(here, here, *pair, peer, self.seq).start()
        for i, block in enumerate(self._core_blocks(self.row)[stage]):
            self._core(self._first(stage) + i, block).start()

    def recv(self, stage):
        for _, there, pair, peer in self._pairs(stage):
            remote(there, there, *pair, peer, self.seq).wait_recv()

    def finish(self):
        for stage in range(self.stages):
            for here, _, pair, peer in self._pairs(stage):
                remote(here, here, *pair, peer, self.seq).wait_send()
        mine, theirs = self._core_blocks(self.row), self._core_blocks(flip(self.row, 1))
        for stage in range(self.stages + 1):
            for i, block in enumerate(theirs[stage]):
                self._core(self._first(stage) + i, block).wait_recv()
            for i, block in enumerate(mine[stage]):
                self._core(self._first(stage) + i, block).wait_send()


def greet(row, seq, rows, size):
    barrier = pltpu.get_barrier_semaphore()
    count = 0
    bit = 1
    while bit < rows:
        pl.semaphore_signal(barrier, inc=1, device_id=(flip(row, bit), seq), device_id_type=MESH)
        bit *= 2
        count += 1
    for step in range(1, size):
        pl.semaphore_signal(barrier, inc=1, device_id=(row, (seq + step) % size), device_id_type=MESH)
        count += 1
    pl.semaphore_wait(barrier, count)


def pieces(own, buf):
    a, b = own.shape
    if b % (8 * LANE) == 0:
        cut = [(slice(None), pl.ds(i * (b // 2), b // 2)) for i in range(2)]
    elif a % 32 == 0:
        cut = [(pl.ds(i * (a // 2), a // 2), slice(None)) for i in range(2)]
    else:
        cut = [(slice(None), slice(None))]
    return [(own.at[p], buf.at[(slice(None),) + p]) for p in cut]


def forward_kernel(
    rows, size, group,
    x, wq, wp, w1, w2, small, sel_t, cos, sin, pic_col, pic_row,
    wp_all, w1_all, w2_all, att, hat_out, qkv_out, k_out, wq_out, o_out, small_sum, lse,
    xg, normed, wq_buf, small_buf, wide, wq_full, bias, qkv, v_turn, k_turn, hat_turn, o_turn, o_part, o_send, sem_ref, out_sem,
):
    row, seq = lax.axis_index("row"), lax.axis_index("seq")
    toks, width = x.shape
    shard = wp.shape[0]
    packed = 2 * LANE
    sems = Sems(sem_ref)
    base = row * size

    def gather(own, buf):
        return Chain(own, buf, base, row, seq, size, sems), Spread(buf, row, seq, rows, size, sems)

    small_g, wp_g = gather(small, small_buf), gather(wp, wp_all)
    a_wq, s_wq = Scatter(wq, lambda j: wq_buf.at[base + j], row, seq, size, sems), Spread(wq_buf, row, seq, rows, size, sems)
    w1_g = [gather(*p) for p in pieces(w1, w1_all)]
    w2_g = [gather(*p) for p in pieces(w2, w2_all)]
    first, second, third = [small_g], w1_g, w2_g + [wp_g]
    g_x = Chain(x, xg, 0, row, seq, size, sems)
    a_o = Scatter(o_send, lambda j: att.at[j], row, seq, size, sems)
    last = small_g[1].stages

    def chain(group, step):
        for g, _ in group:
            if step > 0:
                g.recv(step)
            if step < size - 1:
                g.send(step + 1)
            else:
                g.keep().wait()

    def spread(group, stage):
        for _, s in group:
            if stage > 0:
                s.recv(stage - 1)
            s.send(stage)

    greet(row, seq, rows, size)
    chain(first, 0)
    a_wq.send_all()
    chain(second, 0)
    for step in range(1, size):
        chain(first, step)
        if step < size - 1:
            chain(second, step)
    a_wq.recv()
    early = first + [(a_wq, s_wq)]
    spread(early, 0)
    g_x.send(1)
    chain(second, size - 1)
    spread(second, 0)
    chain(third, 0)
    if last > 0:
        spread(early, 1)
    for step in range(1, size - 1):
        chain(third, step)
    for stage in range(2, last + 1):
        spread(early, stage)
    for _, s in early:
        s.finish()
    total = jnp.zeros(small_sum.shape, jnp.float32)
    for i in range(rows * size):
        total += small_buf[i].astype(jnp.float32)
    small_sum[...] = total
    for i in range(rows * size):
        wide[pl.ds(i * shard, shard), :] = wq_buf[i].astype(jnp.float32)
    own_bias = small_sum[pl.ds(10 + seq, 1), pl.ds(0, group * packed)]
    for head in range(group):
        cols = pl.ds(head * packed, packed)
        out = pl.ds(head * 3 * LANE, 3 * LANE)
        part = jnp.dot(wide[:, cols].astype(jnp.bfloat16), sel_t[...], preferred_element_type=jnp.float32)
        wq_full[:, out] = part.astype(jnp.bfloat16)
        line = jnp.broadcast_to(own_bias[:, head * packed : (head + 1) * packed], (16, packed))
        bias[:, out] = jnp.dot(line.astype(jnp.bfloat16), sel_t[...], preferred_element_type=jnp.float32)

    def project(chunk):
        start = pl.multiple_of(chunk * toks, toks)
        block = 128

        def norm(i, carry):
            at = pl.multiple_of(i * block, block)
            values = xg[chunk, pl.ds(at, block), :].astype(jnp.float32)
            centered = values - jnp.mean(values, axis=-1, keepdims=True)
            variance = jnp.mean(centered * centered, axis=-1, keepdims=True)
            hat = centered * lax.rsqrt(variance + NORM_EPS)
            hat_turn[:, pl.ds(pl.multiple_of(start + at, block), block)] = hat.T.astype(jnp.bfloat16)
            out = hat * small_sum[0:1, :] + small_sum[1:2, :]
            normed[pl.ds(at, block), :] = out.astype(jnp.bfloat16)
            return carry

        lax.fori_loop(0, toks // block, norm, 0)
        span = pl.ds(start, toks)

        def two_heads(i, carry):
            at = pl.multiple_of(i * 6 * LANE, 6 * LANE)
            mixed = jnp.dot(normed[...], wq_full[:, pl.ds(at, 6 * LANE)], preferred_element_type=jnp.float32)
            mixed += bias[0:1, pl.ds(at, 6 * LANE)]
            for j in range(6):
                u = mixed[:, j * LANE : (j + 1) * LANE]
                if j % 3 < 2:
                    u = u * cos[span, :] + pltpu.roll(u, LANE // 2, 1) * sin[span, :]
                if j % 3:
                    turned = pl.ds(pl.multiple_of((2 * i + j // 3) * LANE, LANE), LANE)
                    (k_turn, v_turn)[j % 3 - 1][turned, span] = u.T.astype(jnp.bfloat16)
                qkv[span, pl.ds(pl.multiple_of(at + j * LANE, LANE), LANE)] = u.astype(jnp.bfloat16)
            return carry

        lax.fori_loop(0, group // 2, two_heads, 0)

    g_x.keep().wait()
    project(seq)
    for step in range(1, size):
        g_x.recv(step)
        if step < size - 1:
            g_x.send(step + 1)
        def arrived(i, carry):
            chunk = seq + (2 * i - 1) * step
            pl.when((chunk >= 0) & (chunk < size))(lambda: project(chunk))
            return carry

        lax.fori_loop(0, 2, arrived, 0)
        if step == 1:
            chain(third, size - 1)
            spread(third, 0)
        if step == size - 2 and last > 0:
            spread(second, 1)
        if step == size - 1 and last > 0:
            spread(third, 1)
    outs = [
        pltpu.make_async_copy(a, b, out_sem.at[1 + i])
        for i, (a, b) in enumerate(((hat_turn, hat_out), (qkv, qkv_out), (k_turn, k_out), (wq_full, wq_out)))
    ]
    for copy in outs:
        copy.start()

    def attend(chunk):
        def one(i, carry):
            head = i % group
            block = chunk * (toks // QBLK) + i // group
            span = pl.ds(pl.multiple_of(block * QBLK, QBLK), QBLK)
            at = pl.multiple_of(head * 3 * LANE, LANE)
            q = qkv[span, pl.ds(at, LANE)]
            k = qkv[:, pl.ds(pl.multiple_of(at + LANE, LANE), LANE)]
            scores = lax.dot_general(k, q, (((1,), (1,)), ((), ())), preferred_element_type=jnp.float32)
            scores = jnp.where(pic_col[...] == pic_row[:, span], scores, -1e30)
            top = jnp.max(scores, axis=0, keepdims=True)
            weights = jnp.exp2((scores - top) * EXP_SCALE)
            sums = jnp.sum(weights, axis=0, keepdims=True)
            turned = pl.ds(pl.multiple_of(head * LANE, LANE), LANE)
            out = jnp.dot(v_turn[turned, :], weights.astype(jnp.bfloat16), preferred_element_type=jnp.float32)
            out = out / sums
            o_part[pl.ds(pl.multiple_of(head * HEAD_DIM, 8), HEAD_DIM), :] = out[:HEAD_DIM]
            lse[head, :, span] = top * EXP_SCALE + jnp.log2(sums)

            @pl.when(head == group - 1)
            def _():
                within = pl.multiple_of((i // group) * QBLK, QBLK)
                o_send[chunk, pl.ds(within, QBLK), :] = o_part[...].T.astype(jnp.bfloat16)
                o_turn[:, span] = o_part[...]

            return carry

        lax.fori_loop(0, group * (toks // QBLK), one, 0)

    o_part[...] = jnp.zeros_like(o_part)
    later = [(second, stage) for stage in range(2, last + 1)] + [(third, stage) for stage in range(2, last + 1)]
    for step in range(1, size + 1):
        attend((seq + step) % size)
        if step < size:
            a_o.send(step)
        else:
            a_o.keep().start()
        if step > 1 and later:
            spread(*later.pop(0))
    for group_of, stage in later:
        spread(group_of, stage)
    o_copy = pltpu.make_async_copy(o_turn, o_out, out_sem.at[0])
    o_copy.start()
    for _, s in second + third:
        s.finish()
    a_o.recv()
    for g, _ in early + second + third:
        g.finish()
    g_x.finish()
    a_o.finish()
    for copy in outs + [o_copy]:
        copy.wait()


def forward_call(mesh, x, wq, wp, w1, w2, small, sel_t, cos, sin, pic_col, pic_row):
    rows, size = mesh.shape["row"], mesh.shape["seq"]
    toks, width = x.shape
    length = toks * size
    group = HEADS // size
    shard = wp.shape[0]
    out_width = round_up(group * HEAD_DIM, LANE)
    total = rows * size
    wide = group * 3 * LANE
    bf, f32 = jnp.bfloat16, jnp.float32
    shape = jax.ShapeDtypeStruct
    return pl.pallas_call(
        functools.partial(forward_kernel, rows, size, group),
        out_shape=(
            shape((total,) + wp.shape, bf),
            shape((total,) + w1.shape, bf),
            shape((total,) + w2.shape, bf),
            shape((size, toks, out_width), bf),
            shape((width, length), bf),
            shape((length, wide), bf),
            shape((group * LANE, length), bf),
            shape((width, wide), bf),
            shape((out_width, length), f32),
            shape(small.shape, f32),
            shape((group, 1, length), f32),
        ),
        in_specs=[ANY] * 6 + [VMEM] * 5,
        out_specs=(ANY,) * 9 + (VMEM,) * 2,
        scratch_shapes=[
            pltpu.VMEM((size, toks, width), bf),
            pltpu.VMEM((toks, width), bf),
            pltpu.VMEM((total, shard, group * 2 * LANE), bf),
            pltpu.VMEM((total,) + small.shape, bf),
            pltpu.VMEM((width, group * 2 * LANE), f32),
            pltpu.VMEM((width, wide), bf),
            pltpu.VMEM((16, wide), f32),
            pltpu.VMEM((length, wide), bf),
            pltpu.VMEM((group * LANE, length), bf),
            pltpu.VMEM((group * LANE, length), bf),
            pltpu.VMEM((width, length), bf),
            pltpu.VMEM((out_width, length), f32),
            pltpu.VMEM((out_width, QBLK), f32),
            pltpu.VMEM((size, toks, out_width), bf),
            pltpu.SemaphoreType.DMA((640,)),
            pltpu.SemaphoreType.DMA((5,)),
        ],
        compiler_params=pltpu.CompilerParams(
            collective_id=0, has_side_effects=True, vmem_limit_bytes=62 * 1024 * 1024
        ),
        name="forward",
    )(x, wq, wp, w1, w2, small, sel_t, cos, sin, pic_col, pic_row)


def token_layout(lengths, widths, row_len):
    pic_ends = jnp.cumsum(lengths)
    pic_starts = pic_ends - lengths
    positions = jnp.arange(row_len, dtype=jnp.int32)
    picture = jnp.sum((positions[:, None] >= pic_ends[None, :]).astype(jnp.int32), axis=1)
    matches = picture[:, None] == jnp.arange(lengths.shape[0], dtype=jnp.int32)[None, :]
    first = jnp.sum(jnp.where(matches, pic_starts[None, :], 0), axis=1)
    grid_width = jnp.maximum(jnp.sum(jnp.where(matches, widths[None, :], 0), axis=1), 1)
    within = positions - first
    down = (within // grid_width).astype(jnp.float32)
    side = (within % grid_width).astype(jnp.float32)
    quarter = HEAD_DIM // 4
    frequency = 1.0 / 10000.0 ** (jnp.arange(quarter, dtype=jnp.float32) * 4.0 / HEAD_DIM)
    angles = jnp.concatenate([down[:, None] * frequency, side[:, None] * frequency], axis=-1)
    cosine, sine = jnp.cos(angles), jnp.sin(angles)
    gap = jnp.zeros((row_len, LANE // 2 - HALF), jnp.float32)
    return (
        picture,
        jnp.concatenate([cosine, gap, cosine, gap], axis=-1),
        jnp.concatenate([-sine, gap, sine, gap], axis=-1),
    )


def pack_heads(values):
    a = values.shape[0]
    values = values.reshape(a, 3, HEADS, HEAD_DIM).transpose(0, 2, 1, 3).reshape(a, HEADS, 3 * HEAD_DIM)
    return jnp.pad(values, ((0, 0), (0, 0), (0, 2 * LANE - 3 * HEAD_DIM))).reshape(a, HEADS * 2 * LANE)


def pick_lanes():
    spread = jnp.arange(3 * LANE)
    kind, lane = spread // LANE, spread % LANE
    turned = jnp.where(lane < LANE // 2, lane, lane - LANE // 2 + HALF)
    inside = jnp.where(kind < 2, lane % (LANE // 2) < HALF, lane < HEAD_DIM)
    target = jnp.where(inside, kind * HEAD_DIM + jnp.where(kind < 2, turned, lane), -1)
    return (target[:, None] == jnp.arange(2 * LANE)[None, :]).astype(jnp.bfloat16)


def natural(values):
    size, a, _ = values.shape
    values = values.reshape(size, a, HEADS // size, 3, LANE)
    turned = values[:, :, :, :2].reshape(size, a, HEADS // size, 2, 2, LANE // 2)[..., :HALF]
    turned = turned.reshape(size, a, HEADS // size, 2, HEAD_DIM)
    values = jnp.concatenate([turned, values[:, :, :, 2:, :HEAD_DIM]], axis=3)
    return values.transpose(1, 3, 0, 2, 4).reshape(a, 3 * HEADS * HEAD_DIM)


def add_blocks(outs, firsts, seconds, count, block, first_maps, second_maps):
    n = len(outs)

    def body(*refs):
        for a, b, o in zip(refs[:n], refs[n : 2 * n], refs[2 * n :]):
            o[...] = (a[...].astype(jnp.float32) + b[...].astype(jnp.float32)).astype(o.dtype)

    pltpu.emit_pipeline(
        body,
        grid=(count,),
        in_specs=[pl.BlockSpec(block, m, pipeline_mode=pl.Buffered(4)) for m in list(first_maps) + list(second_maps)],
        out_specs=[pl.BlockSpec(block, lambda i: (i, 0, 0))] * n,
    )(*firsts, *seconds, *outs)


class Reduce:
    def __init__(self, src, core, acc, come, done, row, seq, rows, size, sems, in_vmem):
        self.src, self.core, self.acc, self.come, self.done = src, core, acc, come, done
        self.row, self.seq, self.size, self.in_vmem = row, seq, size, in_vmem
        bits = [1 << i for i in range(1, rows.bit_length() - 1)]
        self.orders = (bits, bits[::-1])
        self.stages = len(bits)
        self.chips = rows // 2
        self.half = src.shape[2] // 2
        self.block = (size, src.shape[1], self.half)
        self.core_sems = [(sems.take(1)[0], sems.take(1)[0]) for _ in range(self.chips)]
        self.sems = [[(sems.take(1)[0], sems.take(1)[0]) for _ in bits] for _ in range(2)]

    def _core_copies(self):
        size = self.size
        other = flip(self.row, 1)
        for chip in range(self.chips):
            theirs = 2 * chip + other % 2
            yield remote(
                self.src.at[pl.ds(theirs * size, size)],
                self.core.at[pl.ds(chip * size, size)],
                *self.core_sems[chip],
                other,
                self.seq,
            )

    def core_send(self):
        for copy in self._core_copies():
            copy.start()

    def _chip(self, half, i):
        chip = self.row // 2
        for k in range(self.stages):
            bit = self.orders[half][self.stages - 1 - k] // 2
            chip = chip + ((i // (1 << k)) % 2) * (flip(chip, bit) - chip)
        return chip

    def core_add(self):
        size = self.size
        for copy in self._core_copies():
            copy.wait_recv()
        core = self.row % 2
        if not self.in_vmem:
            place = lambda half, i: (self._chip(half, i // size), i % size)
            mine = [lambda i, h=h: ((2 * place(h, i)[0] + core) * size + place(h, i)[1], 0, h) for h in range(2)]
            theirs = [lambda i, h=h: (place(h, i)[0] * size + place(h, i)[1], 0, h) for h in range(2)]
            block = (1,) + self.block[1:]
            count = self.chips * size
            add_blocks(self.acc, [self.src] * 2, [self.core] * 2, count, block, mine, theirs)
            return
        for half in range(2):
            cols = pl.ds(half * self.half, self.half)

            def body(i, carry, half=half, cols=cols):
                chip, z = self._chip(half, i // size), i % size
                mine = self.src[(2 * chip + core) * size + z, :, cols].astype(jnp.float32)
                total = mine + self.core[chip * size + z, :, cols].astype(jnp.float32)
                self.acc[half][i] = total.astype(self.acc[half].dtype)
                return carry

            lax.fori_loop(0, self.chips * size, body, 0)

    def _held(self, half, stage):
        return self.acc[half] if stage == 0 else self.done[half][stage - 1]

    def _stage_copy(self, half, stage):
        count = (self.chips >> (stage + 1)) * self.size
        return remote(
            self._held(half, stage).at[pl.ds(count, count)],
            self.come[half][stage],
            *self.sems[half][stage],
            flip(self.row, self.orders[half][stage]),
            self.seq,
        )

    def stage_send(self, stage):
        for half in range(2):
            self._stage_copy(half, stage).start()

    def stage_add(self, stage):
        count = (self.chips >> (stage + 1)) * self.size
        for half in range(2):
            self._stage_copy(half, stage).wait_recv()
        held = [self._held(half, stage) for half in range(2)]
        come, done = ([refs[half][stage] for half in range(2)] for refs in (self.come, self.done))
        if not self.in_vmem:
            plain = [lambda i: (i, 0, 0)] * 2
            add_blocks(done, held, come, count, (1,) + self.block[1:], plain, plain)
            return
        for half in range(2):

            def body(i, carry, half=half):
                total = held[half][i].astype(jnp.float32) + come[half][i].astype(jnp.float32)
                done[half][i] = total.astype(done[half].dtype)
                return carry

            lax.fori_loop(0, count, body, 0)

    @property
    def kept(self):
        return [self._held(half, self.stages) for half in range(2)]

    def finish(self):
        for copy in self._core_copies():
            copy.wait_send()
        for half in range(2):
            for stage in range(self.stages):
                self._stage_copy(half, stage).wait_send()


def reduce_shapes(src, rows, size):
    a, b = src[1], src[2] // 2
    chips = rows // 2
    stages = rows.bit_length() - 2
    shapes = [(chips * size, a, 2 * b)] + [(chips * size, a, b)] * 2
    for _ in range(2):
        for stage in range(stages):
            shapes += [((chips >> (stage + 1)) * size, a, b)] * 2
    return shapes + [(size, a, b)] * 2


def reduce_refs(refs, rows):
    stages = rows.bit_length() - 2
    core, acc, rest = refs[0], refs[1:3], refs[3:-2]
    come = [[rest[2 * (half * stages + j)] for j in range(stages)] for half in range(2)]
    done = [[rest[2 * (half * stages + j) + 1] for j in range(stages)] for half in range(2)]
    return (core, acc, come, done), refs[-2:]


FF_BLK = 1024
FF_CUT = 1280


def backward_kernel(rows, size, shard, group, counts, *refs):
    refs = list(refs)

    def take(count):
        out = refs[:count]
        del refs[:count]
        return out

    attd, x, cot, wp, w1, w2, b1, hat, qkv, k_t, o_t, wh, wq, cos, sin, pic_col, pic_row, lse, small, sel = take(20)
    dx_out, dq_out, layer_out, g_mid, g2_out, g1_out, gp_out, g2, g1, gp, go, b1_sum, wh_all, act, g_act = take(15)
    big = [take(counts) for _ in range(4)]
    vm = take(counts)
    do_in, packed_in, dq, rows_sum, sem_ref, load_sem = refs

    row, seq = lax.axis_index("row"), lax.axis_index("seq")
    length = qkv.shape[0]
    toks = length // size
    width = x.shape[1]
    wide = 3 * LANE
    packed = 2 * LANE
    sems = Sems(sem_ref)
    f32, bf = jnp.float32, jnp.bfloat16

    a_do = Scatter(go, lambda j: do_in.at[j], row, seq, size, sems)
    sources = []
    half_ff = w1.shape[1] // 2
    for i in range(2):
        cols = pl.ds(i * half_ff, half_ff)
        sources.append((g1.at[:, :, cols], g1_out.at[:, cols], big[i]))
    sources += [(g2, g2_out, big[2]), (gp, gp_out, big[3])]
    sources.append((dq, dq_out, vm))
    reducers, z_moves, z_bufs = [], [], []
    for src, out, bufs in sources:
        inner, z_refs = reduce_refs(bufs, rows)
        r = Reduce(src, *inner, row, seq, rows, size, sems, len(reducers) >= len(big))
        reducers.append(r)
        z_bufs.append(z_refs)
        z_moves.append(
            [Scatter(kept, lambda j, to=to: to.at[j], row, seq, size, sems) for kept, to in zip(r.kept, z_refs)]
        )
    rq = reducers[-1]
    rq_at = len(reducers) - 1
    stages = rq.stages

    def z_send(which):
        for move in z_moves[which]:
            move.send_all()

    def start(which):
        reducers[which].core_add()
        if stages:
            reducers[which].stage_send(0)
        else:
            z_send(which)

    def advance(which, stage):
        r = reducers[which]
        r.stage_add(stage)
        if stage + 1 < stages:
            r.stage_send(stage + 1)
        else:
            z_send(which)

    def z_sum(which):
        r, out = reducers[which], sources[which][1]
        cols = r.half // 2 if r.half % (4 * LANE) == 0 else r.half
        for half in range(2):
            z_moves[which][half].recv()
            buf = z_bufs[which][half]
            if which == rq_at:
                out[:, :, pl.ds(half * r.half, r.half)] = buf[...]
            else:

                def body(a, o):
                    total = a[0].astype(f32)
                    for z in range(1, size):
                        total += a[z].astype(f32)
                    o[...] = total

                pltpu.emit_pipeline(
                    body,
                    grid=(r.half // cols,),
                    in_specs=[pl.BlockSpec(r.block[:2] + (cols,), lambda i: (0, 0, i))],
                    out_specs=[pl.BlockSpec((r.block[1], cols), lambda i, half=half: (0, half * (r.half // cols) + i))],
                )(buf, out)

    ready = rq_at

    def load(src, dst, sem=0):
        return pltpu.make_async_copy(src, dst, load_sem.at[sem])

    ff = w1.shape[1]
    ff_blocks = ff // FF_BLK

    wh_chain = Chain(wh, wh_all, row * size, row, seq, size, sems)
    wh_spread = Spread(wh_all, row, seq, rows, size, sems)

    def chain_wh(step):
        wh_chain.recv(step)
        if step < size - 1:
            wh_chain.send(step + 1)
        else:
            wh_chain.keep().wait()

    def spread_wh(stage):
        if stage > wh_spread.stages:
            return
        if stage:
            wh_spread.recv(stage - 1)
        wh_spread.send(stage)

    def mlp(middle, n2, n2_turn, cot_v, out_sum, dn2, g_low, lines):
        loads = [load(cot, cot_v, 3)]
        loads[0].start()

        def head(attd_v, x_v, wp_v):
            copies = [load(attd, attd_v, 0), load(x, x_v, 1), load(wp, wp_v, 2)]
            for copy in copies:
                copy.start()
            for copy in copies:
                copy.wait()

            def one(i, carry):
                span = pl.ds(pl.multiple_of(i * QBLK, QBLK), QBLK)
                values = x_v[span, :].astype(f32) + small[2:3, :]
                values += jnp.dot(attd_v[span, :], wp_v[...], preferred_element_type=f32)
                middle[span, :] = values
                centered = values - jnp.mean(values, axis=-1, keepdims=True)
                variance = jnp.mean(centered * centered, axis=-1, keepdims=True)
                out = centered * lax.rsqrt(variance + NORM_EPS) * small[3:4, :] + small[4:5, :]
                n2[span, :] = out.astype(bf)
                n2_turn[:, span] = out.T.astype(bf)
                return carry

            lax.fori_loop(0, toks // QBLK, one, 0)

        pl.run_scoped(
            head, pltpu.VMEM((toks, width), bf), pltpu.VMEM((toks, width), bf), pltpu.VMEM((width, width), bf)
        )
        loads[0].wait()
        out_sum[...] = jnp.zeros_like(out_sum)
        dn2[...] = jnp.zeros_like(dn2)

        def body(w1_b, w2_b, b1_b, act_b, grad_b, sum_b):
            before = jnp.dot(n2[...], w1_b[...], preferred_element_type=f32) + b1_b[...]
            gate = jax.nn.sigmoid(1.702 * before)
            active = before * gate
            slope = gate + active * (1.702 * (1.0 - gate))
            low = active.astype(bf)
            act_b[...] = low
            out_sum[...] += jnp.dot(low, w2_b[...], preferred_element_type=f32)
            grad = lax.dot_general(cot_v[...], w2_b[...], (((1,), (1,)), ((), ())), preferred_element_type=f32)
            grad = (grad * slope).astype(bf)
            grad_b[...] = grad
            sum_b[...] = jnp.sum(grad.astype(f32), axis=0, keepdims=True)
            dn2[...] += lax.dot_general(grad, w1_b[...], (((1,), (1,)), ((), ())), preferred_element_type=f32)

        by_column = lambda i: (0, i)
        by_row = lambda i: (i, 0)
        chain_wh(1)
        pltpu.emit_pipeline(
            body,
            grid=(ff // FF_BLK,),
            in_specs=[
                pl.BlockSpec((width, FF_BLK), by_column),
                pl.BlockSpec((FF_BLK, width), by_row),
                pl.BlockSpec((1, FF_BLK), by_column),
            ],
            out_specs=[
                pl.BlockSpec((toks, FF_BLK), by_column),
                pl.BlockSpec((toks, FF_BLK), by_column),
                pl.BlockSpec((1, FF_BLK), by_column),
            ],
        )(w1, w2, b1, act, g_act, b1_sum)
        for step in range(2, size):
            chain_wh(step)
        spread_wh(0)

        def up_body(grad_b, g1_b):
            up = jnp.dot(n2_turn[...], grad_b[...], preferred_element_type=f32)
            for s in range(rows * size):
                g1_b[s] = up[s * shard : (s + 1) * shard].astype(bf)

        def up_range(first, count):
            pltpu.emit_pipeline(
                up_body,
                grid=(count,),
                in_specs=[pl.BlockSpec((toks, FF_CUT), lambda i: (0, i + first))],
                out_specs=[pl.BlockSpec((rows * size, shard, FF_CUT), lambda i: (0, 0, i + first))],
            )(g_act, g1)

        def down_body(act_b, g2_b):
            turned = act_b[...].astype(f32).T.astype(bf)
            down = jnp.dot(turned, cot_v[...], preferred_element_type=f32)
            rows_of = g2_b.shape[1]
            for s in range(g2_b.shape[0]):
                g2_b[s] = down[s * rows_of : (s + 1) * rows_of].astype(bf)

        def down_all():
            pltpu.emit_pipeline(
                down_body,
                grid=(ff // FF_CUT,),
                in_specs=[pl.BlockSpec((toks, FF_CUT), by_column)],
                out_specs=[pl.BlockSpec((FF_CUT // g2.shape[1], g2.shape[1], width), lambda i: (i, 0, 0))],
            )(act, g2)

        def tail(wp_v, go_v, out_v):
            copies = [load(wp, wp_v, 1)]
            for copy in copies:
                copy.start()
            lines[...] = jnp.zeros_like(lines)
            go_v[...] = jnp.zeros_like(go_v)

            def one(i, carry):
                span = pl.ds(pl.multiple_of(i * LANE, LANE), LANE)
                values = middle[span, :]
                out_v[span, :] = (values + out_sum[span, :] + small[5:6, :]).astype(bf)
                centered = values - jnp.mean(values, axis=-1, keepdims=True)
                variance = jnp.mean(centered * centered, axis=-1, keepdims=True)
                scale = lax.rsqrt(variance + NORM_EPS)
                hat = centered * scale
                grad = dn2[span, :]
                lines[1:2, :] += jnp.sum(grad * hat, axis=0, keepdims=True)
                lines[2:3, :] += jnp.sum(grad, axis=0, keepdims=True)
                grad = grad * small[3:4, :]
                grad -= jnp.mean(grad, axis=-1, keepdims=True) + hat * jnp.mean(grad * hat, axis=-1, keepdims=True)
                outer = cot_v[span, :].astype(f32)
                lines[3:4, :] += jnp.sum(outer, axis=0, keepdims=True)
                grad = grad * scale + outer
                dn2[span, :] = grad
                low = grad.astype(bf)
                lines[0:1, :] += jnp.sum(low.astype(f32), axis=0, keepdims=True)
                g_low[span, :] = low
                return carry

            lax.fori_loop(0, toks // LANE, one, 0)
            outs = [load(out_v, layer_out, 2), load(dn2, g_mid, 3)]
            for copy in outs:
                copy.start()
            for copy in copies:
                copy.wait()
            heads = group * HEAD_DIM
            for g in range(size):
                part = lax.dot_general(
                    g_low[...], wp_v[pl.ds(g * heads, heads), :], (((1,), (1,)), ((), ())), preferred_element_type=f32
                )
                go_v[g, :, pl.ds(0, heads)] = part.astype(bf)
            send = load(go_v, go, 0)
            send.start()
            send.wait()
            a_do.send_all()
            for copy in outs:
                copy.wait()

        def proj(attd_v, gp_v):
            get = load(attd, attd_v, 1)
            get.start()
            sums = load(b1_sum, rows_sum.at[0:1, pl.ds(0, ff)], 0)
            sums.start()
            sums.wait()
            for i in range(ff // width):
                lines[4 + i : 5 + i, :] = rows_sum[0:1, pl.ds(i * width, width)]
            low_lines = lines[0 : gp_v.shape[1] - shard, :].astype(bf)
            get.wait()
            tall = width // 2
            per = tall // shard
            for i in range(2):
                turned = attd_v[:, pl.ds(i * tall, tall)].astype(f32).T.astype(bf)
                grad = jnp.dot(turned, g_low[...], preferred_element_type=f32)
                for s in range(per):
                    gp_v[s, pl.ds(0, shard), :] = grad[s * shard : (s + 1) * shard].astype(bf)
                    gp_v[s, pl.ds(shard, low_lines.shape[0]), :] = low_lines
                put = load(gp_v, gp.at[pl.ds(i * per, per)], 0)
                put.start()
                put.wait()

        pl.run_scoped(
            tail,
            pltpu.VMEM((width, width), bf),
            pltpu.VMEM(go.shape, bf),
            pltpu.VMEM((toks, width), bf),
        )
        count = ff // FF_CUT
        up_range(0, count // 2)
        reducers[0].core_send()
        spread_wh(1)
        up_range(count // 2, count - count // 2)
        reducers[1].core_send()
        start(0)
        down_all()
        reducers[2].core_send()
        start(1)
        pl.run_scoped(
            proj, pltpu.VMEM((toks, width), bf), pltpu.VMEM((rows * size // 2,) + gp.shape[1:], bf)
        )
        reducers[3].core_send()
        for stage in range(2, wh_spread.stages + 1):
            spread_wh(stage)

    greet(row, seq, rows, size)
    wh_chain.send(1)
    pl.run_scoped(
        mlp,
        pltpu.VMEM((toks, width), f32),
        pltpu.VMEM((toks, width), bf),
        pltpu.VMEM((width, toks), bf),
        pltpu.VMEM((toks, width), bf),
        pltpu.VMEM((toks, width), f32),
        pltpu.VMEM((toks, width), f32),
        pltpu.VMEM((toks, width), bf),
        pltpu.VMEM((round_up(gp.shape[1] - shard, 8), width), f32),
    )
    start(2)
    if stages:
        advance(0, 0)
    start(3)
    wh_spread.finish()
    pl.run_scoped(
        functools.partial(
            attention_back, rows, size, shard, group, row, seq, sems, start, advance, z_sum, a_do, rq, rq_at,
            (hat, qkv, k_t, o_t, wh_all, wq, cos, sin, pic_col, pic_row, lse, small, sel, dx_out, do_in, packed_in, dq, rows_sum),
            load_sem,
        ),
        pltpu.VMEM((length, group * wide), bf),
        pltpu.VMEM((length, group * LANE), bf),
        pltpu.VMEM((group * LANE, length), bf),
        pltpu.VMEM((length, LANE), f32),
        pltpu.VMEM((length, LANE), f32),
        pltpu.VMEM((length, wide), bf),
        pltpu.VMEM((width, length), bf),
        pltpu.VMEM((width, LANE), f32),
        pltpu.VMEM((group, size, toks, packed), bf),
        pltpu.VMEM((2, rows * size, shard, packed), bf),
        pltpu.VMEM((width, packed), f32),
        pltpu.VMEM((width, wide), bf),
        pltpu.VMEM(o_t.shape, f32),
        pltpu.VMEM((group, 1, length), f32),
    )
    wh_chain.finish()
    for r in reducers:
        r.finish()
    for moves in z_moves:
        for move in moves:
            move.finish()
    a_do.finish()


EVENTS = (
    (0.15, ("advance", 1, 0)),
    (0.35, ("advance", 0, 1)),
    (0.45, ("advance", 1, 1)),
    (0.5, ("advance", 2, 0)),
    (0.55, ("advance", 3, 0)),
    (0.75, ("z_sum", 0)),
    (0.8, ("z_sum", 1)),
    (0.8, ("advance", 2, 1)),
    (0.85, ("advance", 3, 1)),
    (1, ("z_sum", 2)),
    (1, ("z_sum", 3)),
)


def attention_back(
    rows, size, shard, group, row, seq, sems, start, advance, z_sum, a_do, rq, rq_at, refs, load_sem,
    qkv_s, do_full, k_turn, gk_sum, gv_sum, gm, n_turn, columns, packs, w_cols, w_wide, wq_cols, o_turn, delta,
):
    hat, qkv, k_t, o_t, wh, wq, cos, sin, pic_col, pic_row, lse, small, sel, dx_out, do_in, packed_in, dq, rows_sum = refs
    length = qkv.shape[0]
    toks = length // size
    width = hat.shape[0]
    wide = 3 * LANE
    packed = 2 * LANE
    stages = rq.stages
    f32, bf = jnp.float32, jnp.bfloat16
    a_heads = [
        Scatter(packs.at[h], lambda j, h=h: packed_in.at[h, j], row, seq, size, sems) for h in range(group)
    ]
    loads = [
        pltpu.make_async_copy(a, b, load_sem.at[i])
        for i, (a, b) in enumerate(((qkv, qkv_s), (k_t, k_turn), (hat, n_turn), (o_t, o_turn)))
    ]
    for copy in loads:
        copy.start()
    columns[...] = jnp.zeros_like(columns)
    columns[:, pl.ds(8, 8)] = small[0:8, :].T
    for copy in loads:
        copy.wait()
    a_do.recv()

    def widen(i, carry):
        chunk, at = i // (toks // QBLK), (i % (toks // QBLK)) * QBLK
        values = do_in[chunk, pl.ds(pl.multiple_of(at, QBLK), QBLK), :].astype(f32)
        lanes = lax.broadcasted_iota(jnp.int32, (QBLK, LANE), 1)
        span = pl.ds(pl.multiple_of(i * QBLK, QBLK), QBLK)
        products = values.T * o_turn[:, span]
        for head in range(group):
            delta[head, :, span] = jnp.sum(
                products[head * HEAD_DIM : (head + 1) * HEAD_DIM], axis=0, keepdims=True
            )
        for head in range(group):
            first = head * HEAD_DIM
            begin = first // LANE * LANE
            window = values[:, begin : min(begin + 2 * LANE, values.shape[1])]
            shift = first - begin
            if shift:
                window = pltpu.roll(window, window.shape[1] - shift, 1)
            piece = jnp.where(lanes < HEAD_DIM, window[:, :LANE], 0.0)
            do_full[pl.ds(pl.multiple_of(i * QBLK, QBLK), QBLK), pl.ds(head * LANE, LANE)] = piece.astype(bf)
        return carry

    lax.fori_loop(0, length // QBLK, widen, 0)

    def unturn(grad, span):
        return grad * cos[span, :] + pltpu.roll(grad * sin[span, :], LANE // 2, 1)

    blocks = length // QBLK
    tile = min(length, 512)

    def query_block(head, i):
        at = pl.multiple_of(head * wide, LANE)
        q_lane, k_lane, v_lane = (pl.ds(pl.multiple_of(at + j * LANE, LANE), LANE) for j in range(3))
        lane = pl.ds(pl.multiple_of(head * LANE, LANE), LANE)
        span = pl.ds(pl.multiple_of(i * QBLK, QBLK), QBLK)
        q = qkv_s[span, q_lane]
        do = do_full[span, lane]
        shift = lse[head, :, span]
        less = delta[head, :, span]
        pic = pic_row[:, span]
        gq = jnp.zeros((LANE, QBLK), f32)
        for j in range(length // tile):
            part = pl.ds(j * tile, tile)
            scores = lax.dot_general(
                qkv_s[part, k_lane], q, (((1,), (1,)), ((), ())), preferred_element_type=f32
            )
            grad_probs = lax.dot_general(
                qkv_s[part, v_lane], do, (((1,), (1,)), ((), ())), preferred_element_type=f32
            )
            probs = jnp.exp2(scores * EXP_SCALE - shift)
            probs = jnp.where(pic_col[part, :] == pic, probs, 0.0)
            gv_sum[part, :] += jnp.dot(probs.astype(bf), do, preferred_element_type=f32)
            grad_scores = (probs * (grad_probs - less)).astype(bf)
            gk_sum[part, :] += jnp.dot(grad_scores, q, preferred_element_type=f32)
            gq += jnp.dot(k_turn[lane, part], grad_scores, preferred_element_type=f32)
        gm[span, pl.ds(0, LANE)] = unturn(gq.T * SCALE, span).astype(bf)

    def head_close(head):
        at = pl.multiple_of(head * wide, LANE)
        load_wq = pltpu.make_async_copy(wq.at[:, pl.ds(at, wide)], wq_cols, load_sem.at[0])
        load_wq.start()

        def close(i, line):
            span = pl.ds(pl.multiple_of(i * QBLK, QBLK), QBLK)
            gm[span, pl.ds(LANE, LANE)] = unturn(gk_sum[span, :] * SCALE, span).astype(bf)
            gm[span, pl.ds(2 * LANE, LANE)] = gv_sum[span, :].astype(bf)
            grads = gm[span, :]
            chunk, within = i // (toks // QBLK), (i % (toks // QBLK)) * QBLK
            packs[head, chunk, pl.ds(pl.multiple_of(within, QBLK), QBLK), :] = jnp.dot(
                grads, sel[...], preferred_element_type=f32
            ).astype(bf)
            return line + jnp.sum(grads.astype(f32), axis=0, keepdims=True)

        line = lax.fori_loop(0, blocks, close, jnp.zeros((1, wide), f32))
        rows_sum[0:1, pl.ds(at, wide)] = line

    def weight_back(head):
        at = pl.multiple_of(head * wide, LANE)
        line = rows_sum[0:1, pl.ds(at, wide)]
        pltpu.make_async_copy(wq.at[:, pl.ds(at, wide)], wq_cols, load_sem.at[0]).wait()
        tall = width // 2
        per = tall // shard
        for i in range(2):
            span = pl.ds(i * tall, tall)
            grad = jnp.dot(n_turn[span, :], gm[...], preferred_element_type=f32)
            weight = wq_cols[span, :].astype(f32)
            columns[span, 0:1] += jnp.sum(weight * grad, axis=1, keepdims=True)
            columns[span, 1:2] += jnp.sum(weight * line, axis=1, keepdims=True)
            grad = grad * columns[span, 8:9] + columns[span, 9:10] * line
            for s in range(per):
                dq[i * per + s, pl.ds(0, shard), pl.ds(at, wide)] = grad[s * shard : (s + 1) * shard].astype(bf)

    def load_cols(head, g):
        cols = pl.ds(pl.multiple_of((g * group + head) * packed, packed), packed)
        return pltpu.make_async_copy(wh.at[:, :, cols], w_cols.at[g % 2], load_sem.at[2 + g % 2])

    def input_back(head):
        for g in range(2):
            load_cols(head, g).start()
        for g in range(size):
            load_cols(head, g).wait()
            for s in range(rows * size):
                w_wide[pl.ds(s * shard, shard), :] = w_cols[g % 2, s].astype(f32)
            dx_out[...] += lax.dot_general(
                packed_in[head, g], w_wide[...].astype(bf), (((1,), (1,)), ((), ())), preferred_element_type=f32
            )
            if g + 2 < size:
                load_cols(head, g + 2).start()

    dx_out[...] = jnp.zeros_like(dx_out)
    rows_sum[...] = jnp.zeros_like(rows_sum)
    total = group * blocks
    events = []
    for where, event in EVENTS:
        if event[0] == "z_sum":
            events.append((where, functools.partial(z_sum, event[1])))
        else:
            _, which, stage = event
            for later in range(stage, min(stage + 1, stages) if stage == 0 else stages):
                events.append((where, functools.partial(advance, which, later)))

    def step(i, carry):
        head, block = i // blocks, i % blocks
        for where, event in events:
            if where < 1:
                pl.when(i == int(where * total))(event)

        @pl.when(block == 0)
        def _():
            gk_sum[...] = jnp.zeros_like(gk_sum)
            gv_sum[...] = jnp.zeros_like(gv_sum)

        query_block(head, block)

        @pl.when(block == blocks - 1)
        def _():
            head_close(head)
            for h in range(group):
                pl.when(head == h)(a_heads[h].send_all)
            weight_back(head)

        @pl.when((block == blocks - 1) & (head > 0))
        def _():
            for h in range(1, group):
                pl.when(head == h)(a_heads[h - 1].recv)
            input_back(head - 1)

        return carry

    lax.fori_loop(0, total, step, 0)

    lines = -(-width // (group * wide))
    turned = columns[:, pl.ds(0, 8)].T
    tail = [rows_sum[0:1, pl.ds(0, group * wide)]]
    for line in (0, 1):
        rows_sum[1 + line : 2 + line, pl.ds(0, width)] = turned[line : line + 1]
        tail += [rows_sum[1 + line : 2 + line, pl.ds(k * group * wide, group * wide)] for k in range(lines)]
    tail = jnp.concatenate(tail, axis=0).astype(bf)

    def put_tail(i, carry):
        dq[i, pl.ds(shard, tail.shape[0]), :] = tail
        return carry

    lax.fori_loop(0, rows * size, put_tail, 0)
    rq.core_send()
    start(rq_at)
    for where, event in events:
        if where >= 1:
            event()
    a_heads[group - 1].recv()
    input_back(group - 1)
    for stage in range(stages):
        advance(rq_at, stage)
    z_sum(rq_at)
    for move in a_heads:
        move.finish()


def backward_call(
    mesh, attd, x, cot, wp, w1, w2, b1, hat, qkv, k_t, o_t, wh, wq, cos, sin, pic_col, pic_row, lse, small, sel, tall
):
    rows, size = mesh.shape["row"], mesh.shape["seq"]
    toks, width = x.shape
    length = toks * size
    group = HEADS // size
    wide = group * 3 * LANE
    total = rows * size
    shard = width // total
    ff = w1.shape[1]
    bf, f32 = jnp.bfloat16, jnp.float32
    shape = jax.ShapeDtypeStruct
    dq_shape = (total, tall, wide)
    g1, g2 = shape((total, shard, ff), bf), shape((total, ff // total, width), bf)
    gp = shape((total, round_up(shard + 4 + ff // width, 16), width), bf)
    half = (total, shard, ff // 2)
    big = [[shape(s, bf) for s in reduce_shapes(g, rows, size)] for g in (half, half, g2.shape, gp.shape)]
    vm = [pltpu.VMEM(s, bf) for s in reduce_shapes(dq_shape, rows, size)]
    go_shape = (size, toks, round_up(group * HEAD_DIM, LANE))
    outs = (
        shape((toks, width), f32),
        shape((size, tall, wide), bf),
        shape((toks, width), bf),
        shape((toks, width), f32),
        shape(g2.shape[1:], f32),
        shape(g1.shape[1:], f32),
        shape(gp.shape[1:], f32),
        g2, g1, gp,
        shape(go_shape, bf),
        shape((1, ff), f32),
        shape((total,) + wh.shape, bf),
        shape((toks, ff), bf),
        shape((toks, ff), bf),
        *(s for group_of in big for s in group_of),
    )
    results = pl.pallas_call(
        functools.partial(backward_kernel, rows, size, shard, group, len(vm)),
        out_shape=outs,
        in_specs=[ANY] * 13 + [VMEM] * 7,
        out_specs=(VMEM,) * 2 + (ANY,) * (len(outs) - 2),
        scratch_shapes=[
            *vm,
            pltpu.VMEM(go_shape, bf),
            pltpu.VMEM((group, size, toks, 2 * LANE), bf),
            pltpu.VMEM(dq_shape, bf),
            pltpu.VMEM((8, max(ff, round_up(width, wide))), f32),
            pltpu.SemaphoreType.DMA((640,)),
            pltpu.SemaphoreType.DMA((4,)),
        ],
        compiler_params=pltpu.CompilerParams(
            collective_id=1, has_side_effects=True, vmem_limit_bytes=63 * 1024 * 1024
        ),
        name="backward",
    )(attd, x, cot, wp, w1, w2, b1, hat, qkv, k_t, o_t, wh, wq, cos, sin, pic_col, pic_row, lse, small, sel)
    return results[:7]


def layer_norm(values, norm_gain, norm_shift):
    centre = jnp.mean(values, axis=-1, keepdims=True)
    centered = values - centre
    variance = jnp.mean(centered * centered, axis=-1, keepdims=True)
    return centered * lax.rsqrt(variance + NORM_EPS) * norm_gain + norm_shift


def pack_small(vectors, more, width, index, total):
    lines = []
    for values in vectors:
        full = values.shape[0] * total
        line = lax.dynamic_update_slice(jnp.zeros((full,), values.dtype), values, (index * values.shape[0],))
        lines.append(line.reshape(-1, width))
    lines = jnp.concatenate(lines + [more], axis=0)
    return jnp.pad(lines, ((0, round_up(lines.shape[0], 16) - lines.shape[0]), (0, 0)))


def shards(
    mesh,
    activations,
    cotangent,
    pic_lengths,
    pic_widths,
    ln1_gain,
    ln1_bias,
    qkv_weight,
    qkv_bias,
    proj_weight,
    proj_bias,
    ln2_gain,
    ln2_bias,
    fc1_weight,
    fc1_bias,
    fc2_weight,
    fc2_bias,
):
    rows, size = mesh.shape["row"], mesh.shape["seq"]
    total = rows * size
    index = lax.axis_index("row") * size + lax.axis_index("seq")
    _, toks, width = activations.shape
    length = toks * size
    group = HEADS // size
    shard = proj_weight.shape[0]
    bf, f32 = jnp.bfloat16, jnp.float32

    picture, cos, sin = token_layout(pic_lengths[0], pic_widths[0], length)
    bias_line = lax.dynamic_update_slice(jnp.zeros((1, 3 * width), bf), qkv_bias[None], (0, index * qkv_bias.shape[0]))
    bias_lines = pack_heads(bias_line).reshape(size, -1)
    bias_lines = jnp.pad(bias_lines, ((0, 0), (0, width - bias_lines.shape[1])))
    small = pack_small(
        (ln1_gain, ln1_bias, proj_bias, ln2_gain, ln2_bias, fc2_bias, fc1_bias), bias_lines, width, index, total
    )
    sel = pick_lanes()
    x = activations[0]
    wh = pack_heads(qkv_weight)
    wq = wh.reshape(shard, size, -1).transpose(1, 0, 2)
    wp, w1, w2, att, hat, qkv, k_t, wq_full, o_t, lines, lse = forward_call(
        mesh, x, wq, proj_weight, fc1_weight, fc2_weight, small, sel.T, cos, sin,
        picture[:, None], picture[None, :],
    )
    wp, w1, w2 = (w.reshape(-1, w.shape[-1]) for w in (wp, w1, w2))
    attended = jnp.concatenate([att[g, :, : group * HEAD_DIM] for g in range(size)], axis=-1)
    b_up = lines[6 : 6 + w1.shape[1] // width].reshape(1, -1)
    grad_normed, grad_qkv, layer_out, grad_middle, grad_down, grad_up, grad_proj = backward_call(
        mesh, attended, x, cotangent[0], wp, w1, w2, b_up, hat, qkv, k_t, o_t, wh, wq_full, cos, sin,
        picture[:, None], picture[None, :], lse, lines, sel,
        round_up(shard + 1 + 2 * -(-width // (group * 3 * LANE)), 16),
    )
    own = [lax.dynamic_slice_in_dim(grad_proj[shard + i], index * shard, shard) for i in range(4)]
    grad_proj_bias, grad_gain_two, grad_shift_two, grad_down_bias = own
    up_lines = grad_proj[shard + 4 : shard + 4 + w1.shape[1] // width].reshape(-1)
    grad_up_bias = lax.dynamic_slice_in_dim(up_lines, index * fc1_bias.shape[0], fc1_bias.shape[0])
    grad_proj = grad_proj[:shard]

    grad_qkv = grad_qkv.astype(f32)
    grad_bias = natural(grad_qkv[:, shard : shard + 1])[0]
    lined = -(-width // (group * 3 * LANE))
    norm_lines = jnp.sum(grad_qkv[:, shard + 1 : shard + 1 + 2 * lined], axis=0).reshape(2, -1)[:, :width]
    grad_gain_one, grad_shift_one = (
        lax.dynamic_slice_in_dim(norm_lines[i], index * shard, shard) for i in range(2)
    )
    grad_qkv = natural(grad_qkv[:, :shard])
    grad_qk = lax.dynamic_slice_in_dim(grad_bias[: 2 * width], index * 2 * shard, 2 * shard)
    grad_value = lax.dynamic_slice_in_dim(grad_bias[2 * width :], index * shard, shard)
    _, norm_one_back = jax.vjp(layer_norm, x.astype(f32), lines[0], lines[1])
    grad_inputs, _, _ = norm_one_back(grad_normed)
    grad_acts = (grad_inputs + grad_middle).astype(bf)

    return (
        layer_out[None],
        grad_acts[None],
        grad_gain_one,
        grad_shift_one,
        grad_qkv,
        grad_qk,
        grad_value,
        grad_proj,
        grad_proj_bias,
        grad_gain_two,
        grad_shift_two,
        grad_up,
        grad_up_bias,
        grad_down,
        grad_down_bias,
    )


def solution(mesh):
    one, two = P(("row", "seq")), P(("row", "seq"), None)
    tokens = P("row", "seq", None)
    return jax.shard_map(
        functools.partial(shards, mesh),
        mesh=mesh,
        in_specs=(tokens, tokens, P("row", None), P("row", None), one, one, two, one, two, one, one, one, two, one, two, one),
        out_specs=(tokens, tokens, one, one, two, one, one, two, one, one, one, two, one, two, one),
        check_vma=False,
    )
```

```python
import functools
import math

import jax
import jax.numpy as jnp
from jax import lax
from jax.experimental import pallas as pl
from jax.experimental.pallas import tpu as pltpu
from jax.sharding import PartitionSpec as P
import ml_dtypes
import numpy as np

HEADS = 16
HEAD_DIM = 80
HALF = HEAD_DIM // 2
LANE = 128
NORM_EPS = 1e-06
SCALE = 1.0 / math.sqrt(HEAD_DIM)
LOG2E = 1.4426950408889634
EXP_SCALE = SCALE * LOG2E
QBLK = 256
MESH = pl.DeviceIdType.MESH
ANY = pl.BlockSpec(memory_space=pl.ANY)
VMEM = pl.BlockSpec(memory_space=pltpu.VMEM)


def round_up(value, unit):
    return -(-value // unit) * unit


def flip(index, bit):
    return index + bit - 2 * bit * ((index // bit) % 2)


def remote(src, dst, send_sem, recv_sem, row, seq):
    return pltpu.make_async_remote_copy(
        src_ref=src,
        dst_ref=dst,
        send_sem=send_sem,
        recv_sem=recv_sem,
        device_id=(row, seq),
        device_id_type=MESH,
    )


class Sems:
    def __init__(self, ref):
        self.ref = ref
        self.used = 0

    def take(self, count):
        first = self.used
        self.used += count
        assert self.used <= self.ref.shape[0]
        return [self.ref.at[first + i] for i in range(count)]


class Chain:
    def __init__(self, own, buf, base, row, seq, size, sems):
        self.own, self.buf, self.base = own, buf, base
        self.row, self.seq, self.size = row, seq, size
        self.sems = [[(sems.take(1)[0], sems.take(1)[0]) for _ in range(size - 1)] for _ in range(2)]
        (self.local,) = sems.take(1)

    def _copies(self, step):
        seq, size = self.seq, self.size
        out = []
        for way in range(2):
            sign = 1 - 2 * way
            block = seq - sign * (step - 1)
            peer = seq + sign
            going = (peer >= 0) & (peer < size) & (block >= 0) & (block < size)
            slot = self.buf.at[self.base + block]
            src = self.own if step == 1 else slot
            copy = functools.partial(remote, src, slot, *self.sems[way][step - 1], self.row, peer)
            come = seq - sign * step
            coming = (come >= 0) & (come < size)
            into = self.buf.at[self.base + come]
            arrive = functools.partial(remote, into, into, *self.sems[way][step - 1], self.row, peer)
            out.append((going, copy, coming, arrive))
        return out

    def keep(self):
        return pltpu.make_async_copy(self.own, self.buf.at[self.base + self.seq], self.local)

    def send(self, step):
        if step == 1:
            self.keep().start()
        for going, copy, _, _ in self._copies(step):
            pl.when(going)(lambda copy=copy: copy().start())

    def recv(self, step):
        for _, _, coming, arrive in self._copies(step):
            pl.when(coming)(lambda arrive=arrive: arrive().wait_recv())

    def finish(self):
        for step in range(1, self.size):
            for going, copy, _, _ in self._copies(step):
                pl.when(going)(lambda copy=copy: copy().wait_send())


class Scatter:
    def __init__(self, src, dst_of, row, seq, size, sems):
        self.src, self.dst_of = src, dst_of
        self.row, self.seq, self.size = row, seq, size
        self.sems = [(sems.take(1)[0], sems.take(1)[0]) for _ in range(size - 1)]
        (self.local,) = sems.take(1)

    def _to(self, step):
        peer = (self.seq + step) % self.size
        return remote(self.src.at[peer], self.dst_of(self.seq), *self.sems[step - 1], self.row, peer)

    def _from(self, step):
        peer = (self.seq + self.size - step) % self.size
        into = self.dst_of(peer)
        return remote(into, into, *self.sems[step - 1], self.row, peer)

    def keep(self):
        return pltpu.make_async_copy(self.src.at[self.seq], self.dst_of(self.seq), self.local)

    def send(self, step):
        self._to(step).start()

    def send_all(self):
        self.keep().start()
        for step in range(1, self.size):
            self.send(step)

    def recv(self):
        self.keep().wait()
        for step in range(1, self.size):
            self._from(step).wait_recv()

    def finish(self):
        for step in range(1, self.size):
            self._to(step).wait_send()


class Spread:
    def __init__(self, buf, row, seq, rows, size, sems):
        self.buf, self.row, self.seq, self.size = buf, row, seq, size
        bits = [1 << i for i in range(1, rows.bit_length() - 1)]
        self.stages = len(bits)
        self.orders = (bits, bits[::-1])
        self.half = buf.shape[2] // 2
        self.sems = [
            [[(sems.take(1)[0], sems.take(1)[0]) for _ in range(1 << j)] for j in range(self.stages)]
            for _ in range(2)
        ]
        self.core_sems = [(sems.take(1)[0], sems.take(1)[0])]
        self.core_sems += [
            (sems.take(1)[0], sems.take(1)[0]) for _ in range(2 * ((1 << self.stages) - 1))
        ]

    def _block(self, row, half):
        first = row * self.size
        if half is None:
            return self.buf.at[pl.ds(first, self.size)]
        return self.buf.at[pl.ds(first, self.size), :, pl.ds(half * self.half, self.half)]

    def _rows(self, start, half, stage):
        rows = [start]
        for bit in self.orders[half][:stage]:
            rows += [flip(row, bit) for row in rows]
        return rows

    def _pairs(self, stage):
        out = []
        for half in range(2):
            bit = self.orders[half][stage]
            peer = flip(self.row, bit)
            for i, row in enumerate(self._rows(self.row, half, stage)):
                here = self._block(row, half)
                there = self._block(flip(row, bit), half)
                pair = self.sems[half][stage][i]
                out.append((here, there, pair, peer))
        return out

    def _core(self, index, block):
        return remote(block, block, *self.core_sems[index], flip(self.row, 1), self.seq)

    def _core_blocks(self, row):
        out = [[self._block(row, None)]]
        for stage in range(self.stages):
            out.append([])
            for half in range(2):
                bit = self.orders[half][stage]
                for other in self._rows(row, half, stage):
                    out[-1].append(self._block(flip(other, bit), half))
        return out

    def _first(self, stage):
        return 0 if stage == 0 else 1 + 2 * ((1 << (stage - 1)) - 1)

    def send(self, stage):
        if stage < self.stages:
            for here, _, pair, peer in self._pairs(stage):
                remote(here, here, *pair, peer, self.seq).start()
        for i, block in enumerate(self._core_blocks(self.row)[stage]):
            self._core(self._first(stage) + i, block).start()

    def recv(self, stage):
        for _, there, pair, peer in self._pairs(stage):
            remote(there, there, *pair, peer, self.seq).wait_recv()

    def finish(self):
        for stage in range(self.stages):
            for here, _, pair, peer in self._pairs(stage):
                remote(here, here, *pair, peer, self.seq).wait_send()
        mine, theirs = self._core_blocks(self.row), self._core_blocks(flip(self.row, 1))
        for stage in range(self.stages + 1):
            for i, block in enumerate(theirs[stage]):
                self._core(self._first(stage) + i, block).wait_recv()
            for i, block in enumerate(mine[stage]):
                self._core(self._first(stage) + i, block).wait_send()


def greet(row, seq, rows, size):
    barrier = pltpu.get_barrier_semaphore()
    count = 0
    bit = 1
    while bit < rows:
        pl.semaphore_signal(barrier, inc=1, device_id=(flip(row, bit), seq), device_id_type=MESH)
        bit *= 2
        count += 1
    for step in range(1, size):
        pl.semaphore_signal(barrier, inc=1, device_id=(row, (seq + step) % size), device_id_type=MESH)
        count += 1
    pl.semaphore_wait(barrier, count)


def pieces(own, buf):
    a, b = own.shape
    if b % (8 * LANE) == 0:
        cut = [(slice(None), pl.ds(i * (b // 2), b // 2)) for i in range(2)]
    elif a % 32 == 0:
        cut = [(pl.ds(i * (a // 2), a // 2), slice(None)) for i in range(2)]
    else:
        cut = [(slice(None), slice(None))]
    return [(own.at[p], buf.at[(slice(None),) + p]) for p in cut]


def forward_kernel(
    rows, size, group,
    x, wq, wp, w1, w2, small, sel_t, cos, sin, pic_col, pic_row,
    wp_all, w1_all, w2_all, att, hat_out, qkv_out, k_out, wq_out, o_out, small_sum, lse,
    xg, normed, wq_buf, small_buf, wide, wq_full, bias, qkv, v_turn, k_turn, hat_turn, o_turn, o_part, o_send, sem_ref, out_sem,
):
    row, seq = lax.axis_index("row"), lax.axis_index("seq")
    toks, width = x.shape
    shard = wp.shape[0]
    packed = 2 * LANE
    sems = Sems(sem_ref)
    base = row * size

    def gather(own, buf):
        return Chain(own, buf, base, row, seq, size, sems), Spread(buf, row, seq, rows, size, sems)

    small_g, wp_g = gather(small, small_buf), gather(wp, wp_all)
    a_wq, s_wq = Scatter(wq, lambda j: wq_buf.at[base + j], row, seq, size, sems), Spread(wq_buf, row, seq, rows, size, sems)
    w1_g = [gather(*p) for p in pieces(w1, w1_all)]
    w2_g = [gather(*p) for p in pieces(w2, w2_all)]
    first, second, third = [small_g], w1_g, w2_g + [wp_g]
    g_x = Chain(x, xg, 0, row, seq, size, sems)
    a_o = Scatter(o_send, lambda j: att.at[j], row, seq, size, sems)
    last = small_g[1].stages

    def chain(group, step):
        for g, _ in group:
            if step > 0:
                g.recv(step)
            if step < size - 1:
                g.send(step + 1)
            else:
                g.keep().wait()

    def spread(group, stage):
        for _, s in group:
            if stage > 0:
                s.recv(stage - 1)
            s.send(stage)

    greet(row, seq, rows, size)
    chain(first, 0)
    a_wq.send_all()
    chain(second, 0)
    for step in range(1, size):
        chain(first, step)
        if step < size - 1:
            chain(second, step)
    a_wq.recv()
    early = first + [(a_wq, s_wq)]
    spread(early, 0)
    g_x.send(1)
    chain(second, size - 1)
    spread(second, 0)
    chain(third, 0)
    if last > 0:
        spread(early, 1)
    for step in range(1, size - 1):
        chain(third, step)
    for stage in range(2, last + 1):
        spread(early, stage)
    for _, s in early:
        s.finish()
    total = jnp.zeros(small_sum.shape, jnp.float32)
    for i in range(rows * size):
        total += small_buf[i].astype(jnp.float32)
    small_sum[...] = total
    for i in range(rows * size):
        wide[pl.ds(i * shard, shard), :] = wq_buf[i].astype(jnp.float32)
    own_bias = small_sum[pl.ds(10 + seq, 1), pl.ds(0, group * packed)]
    for head in range(group):
        cols = pl.ds(head * packed, packed)
        out = pl.ds(head * 3 * LANE, 3 * LANE)
        part = jnp.dot(wide[:, cols].astype(jnp.bfloat16), sel_t[...], preferred_element_type=jnp.float32)
        wq_full[:, out] = part.astype(jnp.bfloat16)
        line = jnp.broadcast_to(own_bias[:, head * packed : (head + 1) * packed], (16, packed))
        bias[:, out] = jnp.dot(line.astype(jnp.bfloat16), sel_t[...], preferred_element_type=jnp.float32)

    def project(chunk):
        start = pl.multiple_of(chunk * toks, toks)
        block = 128

        def norm(i, carry):
            at = pl.multiple_of(i * block, block)
            values = xg[chunk, pl.ds(at, block), :].astype(jnp.float32)
            centered = values - jnp.mean(values, axis=-1, keepdims=True)
            variance = jnp.mean(centered * centered, axis=-1, keepdims=True)
            hat = centered * lax.rsqrt(variance + NORM_EPS)
            hat_turn[:, pl.ds(pl.multiple_of(start + at, block), block)] = hat.T.astype(jnp.bfloat16)
            out = hat * small_sum[0:1, :] + small_sum[1:2, :]
            normed[pl.ds(at, block), :] = out.astype(jnp.bfloat16)
            return carry

        lax.fori_loop(0, toks // block, norm, 0)
        span = pl.ds(start, toks)

        def two_heads(i, carry):
            at = pl.multiple_of(i * 6 * LANE, 6 * LANE)
            mixed = jnp.dot(normed[...], wq_full[:, pl.ds(at, 6 * LANE)], preferred_element_type=jnp.float32)
            mixed += bias[0:1, pl.ds(at, 6 * LANE)]
            for j in range(6):
                u = mixed[:, j * LANE : (j + 1) * LANE]
                if j % 3 < 2:
                    u = u * cos[span, :] + pltpu.roll(u, LANE // 2, 1) * sin[span, :]
                if j % 3:
                    turned = pl.ds(pl.multiple_of((2 * i + j // 3) * LANE, LANE), LANE)
                    (k_turn, v_turn)[j % 3 - 1][turned, span] = u.T.astype(jnp.bfloat16)
                qkv[span, pl.ds(pl.multiple_of(at + j * LANE, LANE), LANE)] = u.astype(jnp.bfloat16)
            return carry

        lax.fori_loop(0, group // 2, two_heads, 0)

    g_x.keep().wait()
    project(seq)
    for step in range(1, size):
        g_x.recv(step)
        if step < size - 1:
            g_x.send(step + 1)
        def arrived(i, carry):
            chunk = seq + (2 * i - 1) * step
            pl.when((chunk >= 0) & (chunk < size))(lambda: project(chunk))
            return carry

        lax.fori_loop(0, 2, arrived, 0)
        if step == 1:
            chain(third, size - 1)
            spread(third, 0)
        if step == size - 2 and last > 0:
            spread(second, 1)
        if step == size - 1 and last > 0:
            spread(third, 1)
    outs = [
        pltpu.make_async_copy(a, b, out_sem.at[1 + i])
        for i, (a, b) in enumerate(((hat_turn, hat_out), (qkv, qkv_out), (k_turn, k_out), (wq_full, wq_out)))
    ]
    for copy in outs:
        copy.start()

    def attend(chunk):
        def one(i, carry):
            head = i % group
            block = chunk * (toks // QBLK) + i // group
            span = pl.ds(pl.multiple_of(block * QBLK, QBLK), QBLK)
            at = pl.multiple_of(head * 3 * LANE, LANE)
            q = qkv[span, pl.ds(at, LANE)]
            k = qkv[:, pl.ds(pl.multiple_of(at + LANE, LANE), LANE)]
            scores = lax.dot_general(k, q, (((1,), (1,)), ((), ())), preferred_element_type=jnp.float32)
            scores = jnp.where(pic_col[...] == pic_row[:, span], scores, -1e30)
            top = jnp.max(scores, axis=0, keepdims=True)
            weights = jnp.exp2((scores - top) * EXP_SCALE)
            sums = jnp.sum(weights, axis=0, keepdims=True)
            turned = pl.ds(pl.multiple_of(head * LANE, LANE), LANE)
            out = jnp.dot(v_turn[turned, :], weights.astype(jnp.bfloat16), preferred_element_type=jnp.float32)
            out = out / sums
            o_part[pl.ds(pl.multiple_of(head * HEAD_DIM, 8), HEAD_DIM), :] = out[:HEAD_DIM]
            lse[head, :, span] = top * EXP_SCALE + jnp.log2(sums)

            @pl.when(head == group - 1)
            def _():
                within = pl.multiple_of((i // group) * QBLK, QBLK)
                o_send[chunk, pl.ds(within, QBLK), :] = o_part[...].T.astype(jnp.bfloat16)
                o_turn[:, span] = o_part[...]

            return carry

        lax.fori_loop(0, group * (toks // QBLK), one, 0)

    o_part[...] = jnp.zeros_like(o_part)
    later = [(second, stage) for stage in range(2, last + 1)] + [(third, stage) for stage in range(2, last + 1)]
    for step in range(1, size + 1):
        attend((seq + step) % size)
        if step < size:
            a_o.send(step)
        else:
            a_o.keep().start()
        if step > 1 and later:
            spread(*later.pop(0))
    for group_of, stage in later:
        spread(group_of, stage)
    o_copy = pltpu.make_async_copy(o_turn, o_out, out_sem.at[0])
    o_copy.start()
    for _, s in second + third:
        s.finish()
    a_o.recv()
    for g, _ in early + second + third:
        g.finish()
    g_x.finish()
    a_o.finish()
    for copy in outs + [o_copy]:
        copy.wait()


def forward_call(mesh, x, wq, wp, w1, w2, small, sel_t, cos, sin, pic_col, pic_row):
    rows, size = mesh.shape["row"], mesh.shape["seq"]
    toks, width = x.shape
    length = toks * size
    group = HEADS // size
    shard = wp.shape[0]
    out_width = round_up(group * HEAD_DIM, LANE)
    total = rows * size
    wide = group * 3 * LANE
    bf, f32 = jnp.bfloat16, jnp.float32
    shape = jax.ShapeDtypeStruct
    return pl.pallas_call(
        functools.partial(forward_kernel, rows, size, group),
        out_shape=(
            shape((total,) + wp.shape, bf),
            shape((total,) + w1.shape, bf),
            shape((total,) + w2.shape, bf),
            shape((size, toks, out_width), bf),
            shape((width, length), bf),
            shape((length, wide), bf),
            shape((group * LANE, length), bf),
            shape((width, wide), bf),
            shape((out_width, length), f32),
            shape(small.shape, f32),
            shape((group, 1, length), f32),
        ),
        in_specs=[ANY] * 6 + [VMEM] * 5,
        out_specs=(ANY,) * 9 + (VMEM,) * 2,
        scratch_shapes=[
            pltpu.VMEM((size, toks, width), bf),
            pltpu.VMEM((toks, width), bf),
            pltpu.VMEM((total, shard, group * 2 * LANE), bf),
            pltpu.VMEM((total,) + small.shape, bf),
            pltpu.VMEM((width, group * 2 * LANE), f32),
            pltpu.VMEM((width, wide), bf),
            pltpu.VMEM((16, wide), f32),
            pltpu.VMEM((length, wide), bf),
            pltpu.VMEM((group * LANE, length), bf),
            pltpu.VMEM((group * LANE, length), bf),
            pltpu.VMEM((width, length), bf),
            pltpu.VMEM((out_width, length), f32),
            pltpu.VMEM((out_width, QBLK), f32),
            pltpu.VMEM((size, toks, out_width), bf),
            pltpu.SemaphoreType.DMA((640,)),
            pltpu.SemaphoreType.DMA((5,)),
        ],
        compiler_params=pltpu.CompilerParams(
            collective_id=0, has_side_effects=True, vmem_limit_bytes=62 * 1024 * 1024
        ),
        name="forward",
    )(x, wq, wp, w1, w2, small, sel_t, cos, sin, pic_col, pic_row)


def token_layout(lengths, widths, row_len):
    slots = jnp.arange(lengths.shape[0])
    pic_ends = jnp.sum(jnp.where(slots[:, None] >= slots[None, :], lengths[None, :], 0), axis=1)
    pic_starts = pic_ends - lengths
    positions = jnp.arange(row_len, dtype=jnp.int32)
    picture = jnp.sum((positions[:, None] >= pic_ends[None, :]).astype(jnp.int32), axis=1)
    matches = picture[:, None] == jnp.arange(lengths.shape[0], dtype=jnp.int32)[None, :]
    first = jnp.sum(jnp.where(matches, pic_starts[None, :], 0), axis=1)
    grid_width = jnp.maximum(jnp.sum(jnp.where(matches, widths[None, :], 0), axis=1), 1)
    within = positions - first
    down = (within // grid_width).astype(jnp.float32)
    side = (within % grid_width).astype(jnp.float32)
    quarter = HEAD_DIM // 4
    frequency = 1.0 / 10000.0 ** (jnp.arange(quarter, dtype=jnp.float32) * 4.0 / HEAD_DIM)
    angles = jnp.concatenate([down[:, None] * frequency, side[:, None] * frequency], axis=-1)
    cosine, sine = jnp.cos(angles), jnp.sin(angles)
    gap = jnp.zeros((row_len, LANE // 2 - HALF), jnp.float32)
    return (
        picture,
        jnp.concatenate([cosine, gap, cosine, gap], axis=-1),
        jnp.concatenate([-sine, gap, sine, gap], axis=-1),
    )


def pack_heads(values):
    a = values.shape[0]
    values = values.reshape(a, 3, HEADS, HEAD_DIM).transpose(0, 2, 1, 3).reshape(a, HEADS, 3 * HEAD_DIM)
    return jnp.pad(values, ((0, 0), (0, 0), (0, 2 * LANE - 3 * HEAD_DIM))).reshape(a, HEADS * 2 * LANE)


def pick_lanes():
    spread = np.arange(3 * LANE)
    kind, lane = spread // LANE, spread % LANE
    turned = np.where(lane < LANE // 2, lane, lane - LANE // 2 + HALF)
    inside = np.where(kind < 2, lane % (LANE // 2) < HALF, lane < HEAD_DIM)
    target = np.where(inside, kind * HEAD_DIM + np.where(kind < 2, turned, lane), -1)
    return (target[:, None] == np.arange(2 * LANE)[None, :]).astype(ml_dtypes.bfloat16)


def unpack_heads(values):
    size, a, _ = values.shape
    values = values.reshape(size, a, HEADS // size, 2 * LANE)[..., : 3 * HEAD_DIM]
    values = values.reshape(size, a, HEADS // size, 3, HEAD_DIM)
    return values.transpose(1, 3, 0, 2, 4).reshape(a, 3 * HEADS * HEAD_DIM)


def add_blocks(outs, firsts, seconds, count, block, first_maps, second_maps):
    n = len(outs)

    def body(*refs):
        for a, b, o in zip(refs[:n], refs[n : 2 * n], refs[2 * n :]):
            o[...] = (a[...].astype(jnp.float32) + b[...].astype(jnp.float32)).astype(o.dtype)

    pltpu.emit_pipeline(
        body,
        grid=(count,),
        in_specs=[pl.BlockSpec(block, m, pipeline_mode=pl.Buffered(4)) for m in list(first_maps) + list(second_maps)],
        out_specs=[pl.BlockSpec(block, lambda i: (i, 0, 0))] * n,
    )(*firsts, *seconds, *outs)


class Reduce:
    def __init__(self, src, core, acc, come, done, row, seq, rows, size, sems, in_vmem):
        self.src, self.core, self.acc, self.come, self.done = src, core, acc, come, done
        self.row, self.seq, self.size, self.in_vmem = row, seq, size, in_vmem
        bits = [1 << i for i in range(1, rows.bit_length() - 1)]
        self.orders = (bits, bits[::-1])
        self.stages = len(bits)
        self.chips = rows // 2
        self.half = src.shape[2] // 2
        self.block = (size, src.shape[1], self.half)
        self.core_sems = [(sems.take(1)[0], sems.take(1)[0]) for _ in range(self.chips)]
        self.sems = [[(sems.take(1)[0], sems.take(1)[0]) for _ in bits] for _ in range(2)]

    def _core_copies(self):
        size = self.size
        other = flip(self.row, 1)
        for chip in range(self.chips):
            theirs = 2 * chip + other % 2
            yield remote(
                self.src.at[pl.ds(theirs * size, size)],
                self.core.at[pl.ds(chip * size, size)],
                *self.core_sems[chip],
                other,
                self.seq,
            )

    def core_send(self):
        for copy in self._core_copies():
            copy.start()

    def _chip(self, half, i):
        chip = self.row // 2
        for k in range(self.stages):
            bit = self.orders[half][self.stages - 1 - k] // 2
            chip = chip + ((i // (1 << k)) % 2) * (flip(chip, bit) - chip)
        return chip

    def core_add(self):
        size = self.size
        for copy in self._core_copies():
            copy.wait_recv()
        core = self.row % 2
        if not self.in_vmem:
            place = lambda half, i: (self._chip(half, i // size), i % size)
            mine = [lambda i, h=h: ((2 * place(h, i)[0] + core) * size + place(h, i)[1], 0, h) for h in range(2)]
            theirs = [lambda i, h=h: (place(h, i)[0] * size + place(h, i)[1], 0, h) for h in range(2)]
            block = (1,) + self.block[1:]
            count = self.chips * size
            add_blocks(self.acc, [self.src] * 2, [self.core] * 2, count, block, mine, theirs)
            return
        for half in range(2):
            cols = pl.ds(half * self.half, self.half)

            def body(i, carry, half=half, cols=cols):
                chip, z = self._chip(half, i // size), i % size
                mine = self.src[(2 * chip + core) * size + z, :, cols].astype(jnp.float32)
                total = mine + self.core[chip * size + z, :, cols].astype(jnp.float32)
                self.acc[half][i] = total.astype(self.acc[half].dtype)
                return carry

            lax.fori_loop(0, self.chips * size, body, 0)

    def _held(self, half, stage):
        return self.acc[half] if stage == 0 else self.done[half][stage - 1]

    def _stage_copy(self, half, stage):
        count = (self.chips >> (stage + 1)) * self.size
        return remote(
            self._held(half, stage).at[pl.ds(count, count)],
            self.come[half][stage],
            *self.sems[half][stage],
            flip(self.row, self.orders[half][stage]),
            self.seq,
        )

    def stage_send(self, stage):
        for half in range(2):
            self._stage_copy(half, stage).start()

    def stage_add(self, stage):
        count = (self.chips >> (stage + 1)) * self.size
        for half in range(2):
            self._stage_copy(half, stage).wait_recv()
        held = [self._held(half, stage) for half in range(2)]
        come, done = ([refs[half][stage] for half in range(2)] for refs in (self.come, self.done))
        if not self.in_vmem:
            plain = [lambda i: (i, 0, 0)] * 2
            add_blocks(done, held, come, count, (1,) + self.block[1:], plain, plain)
            return
        for half in range(2):

            def body(i, carry, half=half):
                total = held[half][i].astype(jnp.float32) + come[half][i].astype(jnp.float32)
                done[half][i] = total.astype(done[half].dtype)
                return carry

            lax.fori_loop(0, count, body, 0)

    @property
    def kept(self):
        return [self._held(half, self.stages) for half in range(2)]

    def finish(self):
        for copy in self._core_copies():
            copy.wait_send()
        for half in range(2):
            for stage in range(self.stages):
                self._stage_copy(half, stage).wait_send()


def reduce_shapes(src, rows, size):
    a, b = src[1], src[2] // 2
    chips = rows // 2
    stages = rows.bit_length() - 2
    shapes = [(chips * size, a, 2 * b)] + [(chips * size, a, b)] * 2
    for _ in range(2):
        for stage in range(stages):
            shapes += [((chips >> (stage + 1)) * size, a, b)] * 2
    return shapes + [(size, a, b)] * 2


def reduce_refs(refs, rows):
    stages = rows.bit_length() - 2
    core, acc, rest = refs[0], refs[1:3], refs[3:-2]
    come = [[rest[2 * (half * stages + j)] for j in range(stages)] for half in range(2)]
    done = [[rest[2 * (half * stages + j) + 1] for j in range(stages)] for half in range(2)]
    return (core, acc, come, done), refs[-2:]


FF_BLK = 1024
FF_CUT = 1280


def backward_kernel(rows, size, shard, group, counts, *refs):
    refs = list(refs)

    def take(count):
        out = refs[:count]
        del refs[:count]
        return out

    attd, x, cot, wp, w1, w2, b1, hat, qkv, k_t, o_t, wh, wq, cos, sin, pic_col, pic_row, lse, small, sel = take(20)
    dx_out, dq_out, dq_pack, layer_out, g_mid, g2, g1, gp, go, b1_sum, wh_all, act, g_act = take(13)
    big = [take(counts) for _ in range(4)]
    vm = take(counts)
    do_in, packed_in, dq, rows_sum, sem_ref, load_sem = refs

    row, seq = lax.axis_index("row"), lax.axis_index("seq")
    length = qkv.shape[0]
    toks = length // size
    width = x.shape[1]
    wide = 3 * LANE
    packed = 2 * LANE
    sems = Sems(sem_ref)
    f32, bf = jnp.float32, jnp.bfloat16

    a_do = Scatter(go, lambda j: do_in.at[j], row, seq, size, sems)
    sources = []
    half_ff = w1.shape[1] // 2
    for i in range(2):
        cols = pl.ds(i * half_ff, half_ff)
        sources.append((g1.at[:, :, cols], big[i]))
    sources += [(g2, big[2]), (gp, big[3])]
    sources.append((dq, vm))
    reducers, z_moves, z_bufs = [], [], []
    for src, bufs in sources:
        inner, z_refs = reduce_refs(bufs, rows)
        r = Reduce(src, *inner, row, seq, rows, size, sems, len(reducers) >= len(big))
        reducers.append(r)
        z_bufs.append(z_refs)
        z_moves.append(
            [Scatter(kept, lambda j, to=to: to.at[j], row, seq, size, sems) for kept, to in zip(r.kept, z_refs)]
        )
    rq = reducers[-1]
    rq_at = len(reducers) - 1
    stages = rq.stages

    def z_send(which):
        for move in z_moves[which]:
            move.send_all()

    def start(which):
        reducers[which].core_add()
        if stages:
            reducers[which].stage_send(0)
        else:
            z_send(which)

    def advance(which, stage):
        r = reducers[which]
        r.stage_add(stage)
        if stage + 1 < stages:
            r.stage_send(stage + 1)
        else:
            z_send(which)

    def z_wait(which):
        for half in range(2):
            z_moves[which][half].recv()
            if which == rq_at:
                dq_out[:, :, pl.ds(half * rq.half, rq.half)] = z_bufs[which][half][...]

    ready = rq_at

    def load(src, dst, sem=0):
        return pltpu.make_async_copy(src, dst, load_sem.at[sem])

    ff = w1.shape[1]
    ff_blocks = ff // FF_BLK

    wh_chain = Chain(wh, wh_all, row * size, row, seq, size, sems)
    wh_spread = Spread(wh_all, row, seq, rows, size, sems)

    def chain_wh(step):
        wh_chain.recv(step)
        if step < size - 1:
            wh_chain.send(step + 1)
        else:
            wh_chain.keep().wait()

    def spread_wh(stage):
        if stage > wh_spread.stages:
            return
        if stage:
            wh_spread.recv(stage - 1)
        wh_spread.send(stage)

    def mlp(middle, n2, n2_turn, cot_v, out_sum, dn2, g_low, lines):
        loads = [load(cot, cot_v, 3)]
        loads[0].start()

        def head(attd_v, x_v, wp_v):
            copies = [load(attd, attd_v, 0), load(x, x_v, 1), load(wp, wp_v, 2)]
            for copy in copies:
                copy.start()
            for copy in copies:
                copy.wait()

            def one(i, carry):
                span = pl.ds(pl.multiple_of(i * QBLK, QBLK), QBLK)
                values = x_v[span, :].astype(f32) + small[2:3, :]
                values += jnp.dot(attd_v[span, :], wp_v[...], preferred_element_type=f32)
                middle[span, :] = values
                centered = values - jnp.mean(values, axis=-1, keepdims=True)
                variance = jnp.mean(centered * centered, axis=-1, keepdims=True)
                out = centered * lax.rsqrt(variance + NORM_EPS) * small[3:4, :] + small[4:5, :]
                n2[span, :] = out.astype(bf)
                n2_turn[:, span] = out.T.astype(bf)
                return carry

            lax.fori_loop(0, toks // QBLK, one, 0)

        pl.run_scoped(
            head, pltpu.VMEM((toks, width), bf), pltpu.VMEM((toks, width), bf), pltpu.VMEM((width, width), bf)
        )
        loads[0].wait()
        out_sum[...] = jnp.zeros_like(out_sum)
        dn2[...] = jnp.zeros_like(dn2)

        def body(w1_b, w2_b, b1_b, act_b, grad_b, sum_b):
            before = jnp.dot(n2[...], w1_b[...], preferred_element_type=f32) + b1_b[...]
            gate = jax.nn.sigmoid(1.702 * before)
            active = before * gate
            slope = gate + active * (1.702 * (1.0 - gate))
            low = active.astype(bf)
            act_b[...] = low
            out_sum[...] += jnp.dot(low, w2_b[...], preferred_element_type=f32)
            grad = lax.dot_general(cot_v[...], w2_b[...], (((1,), (1,)), ((), ())), preferred_element_type=f32)
            grad = (grad * slope).astype(bf)
            grad_b[...] = grad
            sum_b[...] = jnp.sum(grad.astype(f32), axis=0, keepdims=True)
            dn2[...] += lax.dot_general(grad, w1_b[...], (((1,), (1,)), ((), ())), preferred_element_type=f32)

        by_column = lambda i: (0, i)
        by_row = lambda i: (i, 0)
        chain_wh(1)
        pltpu.emit_pipeline(
            body,
            grid=(ff // FF_BLK,),
            in_specs=[
                pl.BlockSpec((width, FF_BLK), by_column),
                pl.BlockSpec((FF_BLK, width), by_row),
                pl.BlockSpec((1, FF_BLK), by_column),
            ],
            out_specs=[
                pl.BlockSpec((toks, FF_BLK), by_column),
                pl.BlockSpec((toks, FF_BLK), by_column),
                pl.BlockSpec((1, FF_BLK), by_column),
            ],
        )(w1, w2, b1, act, g_act, b1_sum)
        for step in range(2, size):
            chain_wh(step)
        spread_wh(0)

        def up_body(grad_b, g1_b):
            up = jnp.dot(n2_turn[...], grad_b[...], preferred_element_type=f32)
            for s in range(rows * size):
                g1_b[s] = up[s * shard : (s + 1) * shard].astype(bf)

        def up_range(first, count):
            pltpu.emit_pipeline(
                up_body,
                grid=(count,),
                in_specs=[pl.BlockSpec((toks, FF_CUT), lambda i: (0, i + first))],
                out_specs=[pl.BlockSpec((rows * size, shard, FF_CUT), lambda i: (0, 0, i + first))],
            )(g_act, g1)

        def down_body(act_b, g2_b):
            turned = act_b[...].astype(f32).T.astype(bf)
            down = jnp.dot(turned, cot_v[...], preferred_element_type=f32)
            rows_of = g2_b.shape[1]
            for s in range(g2_b.shape[0]):
                g2_b[s] = down[s * rows_of : (s + 1) * rows_of].astype(bf)

        def down_all():
            pltpu.emit_pipeline(
                down_body,
                grid=(ff // FF_CUT,),
                in_specs=[pl.BlockSpec((toks, FF_CUT), by_column)],
                out_specs=[pl.BlockSpec((FF_CUT // g2.shape[1], g2.shape[1], width), lambda i: (i, 0, 0))],
            )(act, g2)

        def tail(wp_v, go_v, out_v):
            copies = [load(wp, wp_v, 1)]
            for copy in copies:
                copy.start()
            lines[...] = jnp.zeros_like(lines)
            go_v[...] = jnp.zeros_like(go_v)

            def one(i, carry):
                span = pl.ds(pl.multiple_of(i * LANE, LANE), LANE)
                values = middle[span, :]
                out_v[span, :] = (values + out_sum[span, :] + small[5:6, :]).astype(bf)
                centered = values - jnp.mean(values, axis=-1, keepdims=True)
                variance = jnp.mean(centered * centered, axis=-1, keepdims=True)
                scale = lax.rsqrt(variance + NORM_EPS)
                hat = centered * scale
                grad = dn2[span, :]
                lines[1:2, :] += jnp.sum(grad * hat, axis=0, keepdims=True)
                lines[2:3, :] += jnp.sum(grad, axis=0, keepdims=True)
                grad = grad * small[3:4, :]
                grad -= jnp.mean(grad, axis=-1, keepdims=True) + hat * jnp.mean(grad * hat, axis=-1, keepdims=True)
                outer = cot_v[span, :].astype(f32)
                lines[3:4, :] += jnp.sum(outer, axis=0, keepdims=True)
                grad = grad * scale + outer
                dn2[span, :] = grad
                low = grad.astype(bf)
                lines[0:1, :] += jnp.sum(low.astype(f32), axis=0, keepdims=True)
                g_low[span, :] = low
                return carry

            lax.fori_loop(0, toks // LANE, one, 0)
            outs = [load(out_v, layer_out, 2), load(dn2, g_mid, 3)]
            for copy in outs:
                copy.start()
            for copy in copies:
                copy.wait()
            heads = group * HEAD_DIM
            for g in range(size):
                part = lax.dot_general(
                    g_low[...], wp_v[pl.ds(g * heads, heads), :], (((1,), (1,)), ((), ())), preferred_element_type=f32
                )
                go_v[g, :, pl.ds(0, heads)] = part.astype(bf)
            send = load(go_v, go, 0)
            send.start()
            send.wait()
            a_do.send_all()
            for copy in outs:
                copy.wait()

        def proj(attd_v, gp_v):
            get = load(attd, attd_v, 1)
            get.start()
            sums = load(b1_sum, rows_sum.at[0:1, pl.ds(0, ff)], 0)
            sums.start()
            sums.wait()
            for i in range(ff // width):
                lines[4 + i : 5 + i, :] = rows_sum[0:1, pl.ds(i * width, width)]
            low_lines = lines[0 : gp_v.shape[1] - shard, :].astype(bf)
            get.wait()
            tall = width // 2
            per = tall // shard
            for i in range(2):
                turned = attd_v[:, pl.ds(i * tall, tall)].astype(f32).T.astype(bf)
                grad = jnp.dot(turned, g_low[...], preferred_element_type=f32)
                for s in range(per):
                    gp_v[s, pl.ds(0, shard), :] = grad[s * shard : (s + 1) * shard].astype(bf)
                    gp_v[s, pl.ds(shard, low_lines.shape[0]), :] = low_lines
                put = load(gp_v, gp.at[pl.ds(i * per, per)], 0)
                put.start()
                put.wait()

        pl.run_scoped(
            tail,
            pltpu.VMEM((width, width), bf),
            pltpu.VMEM(go.shape, bf),
            pltpu.VMEM((toks, width), bf),
        )
        count = ff // FF_CUT
        up_range(0, count // 2)
        reducers[0].core_send()
        spread_wh(1)
        up_range(count // 2, count - count // 2)
        reducers[1].core_send()
        start(0)
        down_all()
        reducers[2].core_send()
        start(1)
        pl.run_scoped(
            proj, pltpu.VMEM((toks, width), bf), pltpu.VMEM((rows * size // 2,) + gp.shape[1:], bf)
        )
        reducers[3].core_send()
        for stage in range(2, wh_spread.stages + 1):
            spread_wh(stage)

    greet(row, seq, rows, size)
    wh_chain.send(1)
    pl.run_scoped(
        mlp,
        pltpu.VMEM((toks, width), f32),
        pltpu.VMEM((toks, width), bf),
        pltpu.VMEM((width, toks), bf),
        pltpu.VMEM((toks, width), bf),
        pltpu.VMEM((toks, width), f32),
        pltpu.VMEM((toks, width), f32),
        pltpu.VMEM((toks, width), bf),
        pltpu.VMEM((round_up(gp.shape[1] - shard, 8), width), f32),
    )
    if stages:
        advance(0, 0)
    start(2)
    if stages:
        advance(1, 0)
    wh_spread.finish()
    pl.run_scoped(
        functools.partial(
            attention_back, rows, size, shard, group, row, seq, sems, start, advance, z_wait, a_do, rq, rq_at,
            (hat, qkv, k_t, o_t, wh_all, wq, cos, sin, pic_col, pic_row, lse, small, sel, dx_out, do_in, packed_in, dq, rows_sum, dq_out, dq_pack),
            load_sem,
        ),
        pltpu.VMEM((length, group * wide), bf),
        pltpu.VMEM((length, group * LANE), bf),
        pltpu.VMEM((group * LANE, length), bf),
        pltpu.VMEM((length, LANE), f32),
        pltpu.VMEM((length, LANE), f32),
        pltpu.VMEM((length, wide), bf),
        pltpu.VMEM((width, length), bf),
        pltpu.VMEM((width, LANE), f32),
        pltpu.VMEM((group, size, toks, packed), bf),
        pltpu.VMEM((2, rows * size, shard, packed), bf),
        pltpu.VMEM((width, packed), f32),
        pltpu.VMEM((width, wide), bf),
        pltpu.VMEM(o_t.shape, f32),
        pltpu.VMEM((group, 1, length), f32),
    )
    wh_chain.finish()
    for r in reducers:
        r.finish()
    for moves in z_moves:
        for move in moves:
            move.finish()
    a_do.finish()


EVENTS = (
    (0.15, ("advance", 0, 1)),
    (0.2, ("start", 3)),
    (0.3, ("advance", 1, 1)),
    (0.55, ("advance", 2, 0)),
    (0.6, ("advance", 3, 0)),
    (0.8, ("advance", 2, 1)),
    (0.85, ("advance", 3, 1)),
    (1, ("wait", 0)),
    (1, ("wait", 1)),
    (1, ("wait", 2)),
    (1, ("wait", 3)),
)


def attention_back(
    rows, size, shard, group, row, seq, sems, start, advance, z_wait, a_do, rq, rq_at, refs, load_sem,
    qkv_s, do_full, k_turn, gk_sum, gv_sum, gm, n_turn, columns, packs, w_cols, w_wide, wq_cols, o_turn, delta,
):
    hat, qkv, k_t, o_t, wh, wq, cos, sin, pic_col, pic_row, lse, small, sel, dx_out, do_in, packed_in, dq, rows_sum, dq_out, dq_pack = refs
    length = qkv.shape[0]
    toks = length // size
    width = hat.shape[0]
    wide = 3 * LANE
    packed = 2 * LANE
    stages = rq.stages
    f32, bf = jnp.float32, jnp.bfloat16
    a_heads = [
        Scatter(packs.at[h], lambda j, h=h: packed_in.at[h, j], row, seq, size, sems) for h in range(group)
    ]
    loads = [
        pltpu.make_async_copy(a, b, load_sem.at[i])
        for i, (a, b) in enumerate(((qkv, qkv_s), (k_t, k_turn), (hat, n_turn), (o_t, o_turn)))
    ]
    for copy in loads:
        copy.start()
    columns[...] = jnp.zeros_like(columns)
    columns[:, pl.ds(8, 8)] = small[0:8, :].T
    for copy in loads[:2] + loads[3:]:
        copy.wait()
    a_do.recv()

    def widen(i, carry):
        chunk, at = i // (toks // QBLK), (i % (toks // QBLK)) * QBLK
        values = do_in[chunk, pl.ds(pl.multiple_of(at, QBLK), QBLK), :].astype(f32)
        lanes = lax.broadcasted_iota(jnp.int32, (QBLK, LANE), 1)
        span = pl.ds(pl.multiple_of(i * QBLK, QBLK), QBLK)
        products = values.T * o_turn[:, span]
        for head in range(group):
            delta[head, :, span] = jnp.sum(
                products[head * HEAD_DIM : (head + 1) * HEAD_DIM], axis=0, keepdims=True
            )
        for head in range(group):
            first = head * HEAD_DIM
            begin = first // LANE * LANE
            window = values[:, begin : min(begin + 2 * LANE, values.shape[1])]
            shift = first - begin
            if shift:
                window = pltpu.roll(window, window.shape[1] - shift, 1)
            piece = jnp.where(lanes < HEAD_DIM, window[:, :LANE], 0.0)
            do_full[pl.ds(pl.multiple_of(i * QBLK, QBLK), QBLK), pl.ds(head * LANE, LANE)] = piece.astype(bf)
        return carry

    lax.fori_loop(0, length // QBLK, widen, 0)
    loads[2].wait()

    def unturn(grad, span):
        return grad * cos[span, :] + pltpu.roll(grad * sin[span, :], LANE // 2, 1)

    blocks = length // QBLK
    tile = min(length, 512)

    def query_block(head, i):
        at = pl.multiple_of(head * wide, LANE)
        q_lane, k_lane, v_lane = (pl.ds(pl.multiple_of(at + j * LANE, LANE), LANE) for j in range(3))
        lane = pl.ds(pl.multiple_of(head * LANE, LANE), LANE)
        span = pl.ds(pl.multiple_of(i * QBLK, QBLK), QBLK)
        q = qkv_s[span, q_lane]
        do = do_full[span, lane]
        shift = lse[head, :, span]
        less = delta[head, :, span]
        pic = pic_row[:, span]
        gq = jnp.zeros((LANE, QBLK), f32)
        for j in range(length // tile):
            part = pl.ds(j * tile, tile)
            scores = lax.dot_general(
                qkv_s[part, k_lane], q, (((1,), (1,)), ((), ())), preferred_element_type=f32
            )
            grad_probs = lax.dot_general(
                qkv_s[part, v_lane], do, (((1,), (1,)), ((), ())), preferred_element_type=f32
            )
            probs = jnp.exp2(scores * EXP_SCALE - shift)
            probs = jnp.where(pic_col[part, :] == pic, probs, 0.0)
            gv_sum[part, :] += jnp.dot(probs.astype(bf), do, preferred_element_type=f32)
            grad_scores = (probs * (grad_probs - less)).astype(bf)
            gk_sum[part, :] += jnp.dot(grad_scores, q, preferred_element_type=f32)
            gq += jnp.dot(k_turn[lane, part], grad_scores, preferred_element_type=f32)
        gm[span, pl.ds(0, LANE)] = unturn(gq.T * SCALE, span).astype(bf)

    def head_close(head):
        at = pl.multiple_of(head * wide, LANE)
        load_wq = pltpu.make_async_copy(wq.at[:, pl.ds(at, wide)], wq_cols, load_sem.at[0])
        load_wq.start()

        def close(i, line):
            span = pl.ds(pl.multiple_of(i * QBLK, QBLK), QBLK)
            gm[span, pl.ds(LANE, LANE)] = unturn(gk_sum[span, :] * SCALE, span).astype(bf)
            gm[span, pl.ds(2 * LANE, LANE)] = gv_sum[span, :].astype(bf)
            grads = gm[span, :]
            chunk, within = i // (toks // QBLK), (i % (toks // QBLK)) * QBLK
            packs[head, chunk, pl.ds(pl.multiple_of(within, QBLK), QBLK), :] = jnp.dot(
                grads, sel[...], preferred_element_type=f32
            ).astype(bf)
            return line + jnp.sum(grads.astype(f32), axis=0, keepdims=True)

        line = lax.fori_loop(0, blocks, close, jnp.zeros((1, wide), f32))
        rows_sum[0:1, pl.ds(at, wide)] = line

    def weight_back(head):
        at = pl.multiple_of(head * wide, LANE)
        line = rows_sum[0:1, pl.ds(at, wide)]
        pltpu.make_async_copy(wq.at[:, pl.ds(at, wide)], wq_cols, load_sem.at[0]).wait()
        tall = width // 2
        per = tall // shard
        for i in range(2):
            span = pl.ds(i * tall, tall)
            grad = jnp.dot(n_turn[span, :], gm[...], preferred_element_type=f32)
            weight = wq_cols[span, :].astype(f32)
            columns[span, 0:1] += jnp.sum(weight * grad, axis=1, keepdims=True)
            columns[span, 1:2] += jnp.sum(weight * line, axis=1, keepdims=True)
            grad = grad * columns[span, 8:9] + columns[span, 9:10] * line
            for s in range(per):
                dq[i * per + s, pl.ds(0, shard), pl.ds(at, wide)] = grad[s * shard : (s + 1) * shard].astype(bf)

    def load_cols(head, g):
        cols = pl.ds(pl.multiple_of((g * group + head) * packed, packed), packed)
        return pltpu.make_async_copy(wh.at[:, :, cols], w_cols.at[g % 2], load_sem.at[2 + g % 2])

    def input_back(head):
        for g in range(2):
            load_cols(head, g).start()
        for g in range(size):
            load_cols(head, g).wait()
            for s in range(rows * size):
                w_wide[pl.ds(s * shard, shard), :] = w_cols[g % 2, s].astype(f32)
            dx_out[...] += lax.dot_general(
                packed_in[head, g], w_wide[...].astype(bf), (((1,), (1,)), ((), ())), preferred_element_type=f32
            )
            if g + 2 < size:
                load_cols(head, g + 2).start()

    dx_out[...] = jnp.zeros_like(dx_out)
    rows_sum[...] = jnp.zeros_like(rows_sum)
    total = group * blocks
    events = []
    for where, event in EVENTS:
        if event[0] == "wait":
            events.append((where, functools.partial(z_wait, event[1])))
        elif event[0] == "start":
            events.append((where, functools.partial(start, event[1])))
        else:
            _, which, stage = event
            for later in range(stage, min(stage + 1, stages) if stage == 0 else stages):
                events.append((where, functools.partial(advance, which, later)))

    def step(i, carry):
        head, block = i // blocks, i % blocks
        for where, event in events:
            if where < 1:
                pl.when(i == int(where * total))(event)

        @pl.when(block == 0)
        def _():
            gk_sum[...] = jnp.zeros_like(gk_sum)
            gv_sum[...] = jnp.zeros_like(gv_sum)

        query_block(head, block)

        @pl.when(block == blocks - 1)
        def _():
            head_close(head)
            for h in range(group):
                pl.when(head == h)(a_heads[h].send_all)
            weight_back(head)

        @pl.when((block == blocks - 1) & (head > 0) & (head < group - 1))
        def _():
            for h in range(1, group - 1):
                pl.when(head == h)(a_heads[h - 1].recv)
            input_back(head - 1)

        return carry

    lax.fori_loop(0, total, step, 0)

    lines = -(-width // (group * wide))
    turned = columns[:, pl.ds(0, 8)].T
    tail = [rows_sum[0:1, pl.ds(0, group * wide)]]
    for line in (0, 1):
        rows_sum[1 + line : 2 + line, pl.ds(0, width)] = turned[line : line + 1]
        tail += [rows_sum[1 + line : 2 + line, pl.ds(k * group * wide, group * wide)] for k in range(lines)]
    tail = jnp.concatenate(tail, axis=0).astype(bf)

    def put_tail(i, carry):
        dq[i, pl.ds(shard, tail.shape[0]), :] = tail
        return carry

    lax.fori_loop(0, rows * size, put_tail, 0)
    rq.core_send()
    start(rq_at)
    for head in range(max(0, group - 2), group):
        a_heads[head].recv()
        input_back(head)
        if head == group - 2 and stages:
            advance(rq_at, 0)
    for stage in range(0 if group < 2 else 1, stages):
        advance(rq_at, stage)
    for where, event in events:
        if where >= 1:
            event()
    z_wait(rq_at)

    def pack(i, carry):
        g, head = i // group, i % group
        raw = dq_out[g, :, pl.ds(pl.multiple_of(head * wide, LANE), wide)]
        dq_pack[g, :, pl.ds(pl.multiple_of(head * packed, LANE), packed)] = jnp.dot(
            raw, sel[...], preferred_element_type=f32
        ).astype(bf)
        return carry

    lax.fori_loop(0, size * group, pack, 0)
    for move in a_heads:
        move.finish()


def backward_call(
    mesh, attd, x, cot, wp, w1, w2, b1, hat, qkv, k_t, o_t, wh, wq, cos, sin, pic_col, pic_row, lse, small, sel, tall
):
    rows, size = mesh.shape["row"], mesh.shape["seq"]
    toks, width = x.shape
    length = toks * size
    group = HEADS // size
    wide = group * 3 * LANE
    total = rows * size
    shard = width // total
    ff = w1.shape[1]
    bf, f32 = jnp.bfloat16, jnp.float32
    shape = jax.ShapeDtypeStruct
    dq_shape = (total, tall, wide)
    g1, g2 = shape((total, shard, ff), bf), shape((total, ff // total, width), bf)
    gp = shape((total, round_up(shard + 4 + ff // width, 16), width), bf)
    half = (total, shard, ff // 2)
    big = [[shape(s, bf) for s in reduce_shapes(g, rows, size)] for g in (half, half, g2.shape, gp.shape)]
    vm = [pltpu.VMEM(s, bf) for s in reduce_shapes(dq_shape, rows, size)]
    go_shape = (size, toks, round_up(group * HEAD_DIM, LANE))
    outs = (
        shape((toks, width), f32),
        shape((size, tall, wide), bf),
        shape((size, tall, group * 2 * LANE), bf),
        shape((toks, width), bf),
        shape((toks, width), f32),
        g2, g1, gp,
        shape(go_shape, bf),
        shape((1, ff), f32),
        shape((total,) + wh.shape, bf),
        shape((toks, ff), bf),
        shape((toks, ff), bf),
        *(s for group_of in big for s in group_of),
    )
    results = pl.pallas_call(
        functools.partial(backward_kernel, rows, size, shard, group, len(vm)),
        out_shape=outs,
        in_specs=[ANY] * 13 + [VMEM] * 7,
        out_specs=(VMEM,) * 3 + (ANY,) * (len(outs) - 3),
        scratch_shapes=[
            *vm,
            pltpu.VMEM(go_shape, bf),
            pltpu.VMEM((group, size, toks, 2 * LANE), bf),
            pltpu.VMEM(dq_shape, bf),
            pltpu.VMEM((8, max(ff, round_up(width, wide))), f32),
            pltpu.SemaphoreType.DMA((640,)),
            pltpu.SemaphoreType.DMA((4,)),
        ],
        compiler_params=pltpu.CompilerParams(
            collective_id=1, has_side_effects=True, vmem_limit_bytes=63 * 1024 * 1024
        ),
        name="backward",
    )(attd, x, cot, wp, w1, w2, b1, hat, qkv, k_t, o_t, wh, wq, cos, sin, pic_col, pic_row, lse, small, sel)
    sums = [
        jnp.concatenate([jnp.sum(r.astype(f32), axis=0) for r in results[i - 2 : i]], axis=-1)
        for i in range(len(results) - 3 * len(vm), len(results) + 1, len(vm))
    ]
    return (*results[:5], sums[2], jnp.concatenate(sums[:2], axis=-1), sums[3])


def layer_norm(values, norm_gain, norm_shift):
    centre = jnp.mean(values, axis=-1, keepdims=True)
    centered = values - centre
    variance = jnp.mean(centered * centered, axis=-1, keepdims=True)
    return centered * lax.rsqrt(variance + NORM_EPS) * norm_gain + norm_shift


def at_own_place(values, index, total):
    mine = jnp.arange(total, dtype=jnp.int32)[:, None] == index
    return jnp.where(mine, values[None, :], jnp.zeros((), values.dtype)).reshape(-1)


def pack_small(vectors, more, width, index, total):
    lines = [at_own_place(values, index, total).reshape(-1, width) for values in vectors]
    lines = jnp.concatenate(lines + [more], axis=0)
    return jnp.pad(lines, ((0, round_up(lines.shape[0], 16) - lines.shape[0]), (0, 0)))


def shards(
    mesh,
    activations,
    cotangent,
    pic_lengths,
    pic_widths,
    ln1_gain,
    ln1_bias,
    qkv_weight,
    qkv_bias,
    proj_weight,
    proj_bias,
    ln2_gain,
    ln2_bias,
    fc1_weight,
    fc1_bias,
    fc2_weight,
    fc2_bias,
):
    rows, size = mesh.shape["row"], mesh.shape["seq"]
    total = rows * size
    index = lax.axis_index("row") * size + lax.axis_index("seq")
    _, toks, width = activations.shape
    length = toks * size
    group = HEADS // size
    shard = proj_weight.shape[0]
    bf, f32 = jnp.bfloat16, jnp.float32

    picture, cos, sin = token_layout(pic_lengths[0], pic_widths[0], length)
    bias_line = at_own_place(qkv_bias, index, total)[None]
    bias_lines = pack_heads(bias_line).reshape(size, -1)
    bias_lines = jnp.pad(bias_lines, ((0, 0), (0, width - bias_lines.shape[1])))
    small = pack_small(
        (ln1_gain, ln1_bias, proj_bias, ln2_gain, ln2_bias, fc2_bias, fc1_bias), bias_lines, width, index, total
    )
    sel = pick_lanes()
    x = activations[0]
    wh = pack_heads(qkv_weight)
    wq = wh.reshape(shard, size, -1).transpose(1, 0, 2)
    wp, w1, w2, att, hat, qkv, k_t, wq_full, o_t, lines, lse = forward_call(
        mesh, x, wq, proj_weight, fc1_weight, fc2_weight, small, sel.T, cos, sin,
        picture[:, None], picture[None, :],
    )
    wp, w1, w2 = (w.reshape(-1, w.shape[-1]) for w in (wp, w1, w2))
    attended = jnp.concatenate([att[g, :, : group * HEAD_DIM] for g in range(size)], axis=-1)
    b_up = lines[6 : 6 + w1.shape[1] // width].reshape(1, -1)
    grad_normed, grad_qkv, packed, layer_out, grad_middle, grad_down, grad_up, grad_proj = backward_call(
        mesh, attended, x, cotangent[0], wp, w1, w2, b_up, hat, qkv, k_t, o_t, wh, wq_full, cos, sin,
        picture[:, None], picture[None, :], lse, lines, sel,
        round_up(shard + 1 + 2 * -(-width // (group * 3 * LANE)), 16),
    )
    lined = -(-width // (group * 3 * LANE))
    norm_lines = jnp.sum(grad_qkv[:, shard + 1 : shard + 1 + 2 * lined].astype(f32), axis=0).reshape(2, -1)[:, :width]
    sums = jnp.concatenate([grad_proj[shard : shard + 4], norm_lines], axis=0).reshape(6, total, shard)
    sums = lax.dynamic_index_in_dim(sums, index, 1, keepdims=False)
    up_lines = grad_proj[shard + 4 : shard + 4 + w1.shape[1] // width].reshape(total, -1)
    grad_up_bias = lax.dynamic_index_in_dim(up_lines, index, 0, keepdims=False)
    grad_proj = grad_proj[:shard]
    grad_qkv = unpack_heads(packed[:, :shard].astype(f32))
    grad_bias = unpack_heads(packed[:, shard : shard + 1].astype(f32))[0]
    grad_qk = lax.dynamic_slice_in_dim(grad_bias[: 2 * width], index * 2 * shard, 2 * shard)
    grad_value = lax.dynamic_slice_in_dim(grad_bias[2 * width :], index * shard, shard)
    _, norm_one_back = jax.vjp(layer_norm, x.astype(f32), lines[0], lines[1])
    grad_inputs, _, _ = norm_one_back(grad_normed)
    grad_acts = (grad_inputs + grad_middle).astype(bf)

    return (
        layer_out[None],
        grad_acts[None],
        sums[4],
        sums[5],
        grad_qkv,
        grad_qk,
        grad_value,
        grad_proj,
        sums[0],
        sums[1],
        sums[2],
        grad_up,
        grad_up_bias,
        grad_down,
        sums[3],
    )


def solution(mesh):
    one, two = P(("row", "seq")), P(("row", "seq"), None)
    tokens = P("row", "seq", None)
    return jax.shard_map(
        functools.partial(shards, mesh),
        mesh=mesh,
        in_specs=(tokens, tokens, P("row", None), P("row", None), one, one, two, one, two, one, one, one, two, one, two, one),
        out_specs=(tokens, tokens, one, one, two, one, one, two, one, one, one, two, one, two, one),
        check_vma=False,
    )
```

```python
import functools
import math

import jax
import jax.numpy as jnp
from jax import lax
from jax.experimental import pallas as pl
from jax.experimental.pallas import tpu as pltpu
from jax.sharding import PartitionSpec as P
import ml_dtypes
import numpy as np

HEADS = 16
HEAD_DIM = 80
HALF = HEAD_DIM // 2
LANE = 128
NORM_EPS = 1e-06
SCALE = 1.0 / math.sqrt(HEAD_DIM)
LOG2E = 1.4426950408889634
EXP_SCALE = SCALE * LOG2E
QBLK = 256
MESH = pl.DeviceIdType.MESH
ANY = pl.BlockSpec(memory_space=pl.ANY)
VMEM = pl.BlockSpec(memory_space=pltpu.VMEM)


def round_up(value, unit):
    return -(-value // unit) * unit


def flip(index, bit):
    return index + bit - 2 * bit * ((index // bit) % 2)


def remote(src, dst, send_sem, recv_sem, row, seq):
    return pltpu.make_async_remote_copy(
        src_ref=src,
        dst_ref=dst,
        send_sem=send_sem,
        recv_sem=recv_sem,
        device_id=(row, seq),
        device_id_type=MESH,
    )


class Sems:
    def __init__(self, ref):
        self.ref = ref
        self.used = 0

    def take(self, count):
        first = self.used
        self.used += count
        assert self.used <= self.ref.shape[0]
        return [self.ref.at[first + i] for i in range(count)]


class Chain:
    def __init__(self, own, buf, base, row, seq, size, sems):
        self.own, self.buf, self.base = own, buf, base
        self.row, self.seq, self.size = row, seq, size
        self.sems = [[(sems.take(1)[0], sems.take(1)[0]) for _ in range(size - 1)] for _ in range(2)]
        (self.local,) = sems.take(1)

    def _copies(self, step):
        seq, size = self.seq, self.size
        out = []
        for way in range(2):
            sign = 1 - 2 * way
            block = seq - sign * (step - 1)
            peer = seq + sign
            going = (peer >= 0) & (peer < size) & (block >= 0) & (block < size)
            slot = self.buf.at[self.base + block]
            src = self.own if step == 1 else slot
            copy = functools.partial(remote, src, slot, *self.sems[way][step - 1], self.row, peer)
            come = seq - sign * step
            coming = (come >= 0) & (come < size)
            into = self.buf.at[self.base + come]
            arrive = functools.partial(remote, into, into, *self.sems[way][step - 1], self.row, peer)
            out.append((going, copy, coming, arrive))
        return out

    def keep(self):
        return pltpu.make_async_copy(self.own, self.buf.at[self.base + self.seq], self.local)

    def send(self, step):
        if step == 1:
            self.keep().start()
        for going, copy, _, _ in self._copies(step):
            pl.when(going)(lambda copy=copy: copy().start())

    def recv(self, step):
        for _, _, coming, arrive in self._copies(step):
            pl.when(coming)(lambda arrive=arrive: arrive().wait_recv())

    def finish(self):
        for step in range(1, self.size):
            for going, copy, _, _ in self._copies(step):
                pl.when(going)(lambda copy=copy: copy().wait_send())


class Scatter:
    def __init__(self, src, dst_of, row, seq, size, sems):
        self.src, self.dst_of = src, dst_of
        self.row, self.seq, self.size = row, seq, size
        self.sems = [(sems.take(1)[0], sems.take(1)[0]) for _ in range(size - 1)]
        (self.local,) = sems.take(1)

    def _to(self, step):
        peer = (self.seq + step) % self.size
        return remote(self.src.at[peer], self.dst_of(self.seq), *self.sems[step - 1], self.row, peer)

    def _from(self, step):
        peer = (self.seq + self.size - step) % self.size
        into = self.dst_of(peer)
        return remote(into, into, *self.sems[step - 1], self.row, peer)

    def keep(self):
        return pltpu.make_async_copy(self.src.at[self.seq], self.dst_of(self.seq), self.local)

    def send(self, step):
        self._to(step).start()

    def send_all(self):
        self.keep().start()
        for step in range(1, self.size):
            self.send(step)

    def recv(self):
        self.keep().wait()
        for step in range(1, self.size):
            self._from(step).wait_recv()

    def finish(self):
        for step in range(1, self.size):
            self._to(step).wait_send()


class Spread:
    def __init__(self, buf, row, seq, rows, size, sems):
        self.buf, self.row, self.seq, self.size = buf, row, seq, size
        bits = [1 << i for i in range(1, rows.bit_length() - 1)]
        self.stages = len(bits)
        self.orders = (bits, bits[::-1])
        self.half = buf.shape[2] // 2
        self.sems = [
            [[(sems.take(1)[0], sems.take(1)[0]) for _ in range(1 << j)] for j in range(self.stages)]
            for _ in range(2)
        ]
        self.core_sems = [(sems.take(1)[0], sems.take(1)[0])]
        self.core_sems += [
            (sems.take(1)[0], sems.take(1)[0]) for _ in range(2 * ((1 << self.stages) - 1))
        ]

    def _block(self, row, half):
        first = row * self.size
        if half is None:
            return self.buf.at[pl.ds(first, self.size)]
        return self.buf.at[pl.ds(first, self.size), :, pl.ds(half * self.half, self.half)]

    def _rows(self, start, half, stage):
        rows = [start]
        for bit in self.orders[half][:stage]:
            rows += [flip(row, bit) for row in rows]
        return rows

    def _pairs(self, stage):
        out = []
        for half in range(2):
            bit = self.orders[half][stage]
            peer = flip(self.row, bit)
            for i, row in enumerate(self._rows(self.row, half, stage)):
                here = self._block(row, half)
                there = self._block(flip(row, bit), half)
                pair = self.sems[half][stage][i]
                out.append((here, there, pair, peer))
        return out

    def _core(self, index, block):
        return remote(block, block, *self.core_sems[index], flip(self.row, 1), self.seq)

    def _core_blocks(self, row):
        out = [[self._block(row, None)]]
        for stage in range(self.stages):
            out.append([])
            for half in range(2):
                bit = self.orders[half][stage]
                for other in self._rows(row, half, stage):
                    out[-1].append(self._block(flip(other, bit), half))
        return out

    def _first(self, stage):
        return 0 if stage == 0 else 1 + 2 * ((1 << (stage - 1)) - 1)

    def send(self, stage):
        if stage < self.stages:
            for here, _, pair, peer in self._pairs(stage):
                remote(here, here, *pair, peer, self.seq).start()
        for i, block in enumerate(self._core_blocks(self.row)[stage]):
            self._core(self._first(stage) + i, block).start()

    def recv(self, stage):
        for _, there, pair, peer in self._pairs(stage):
            remote(there, there, *pair, peer, self.seq).wait_recv()

    def finish(self):
        for stage in range(self.stages):
            for here, _, pair, peer in self._pairs(stage):
                remote(here, here, *pair, peer, self.seq).wait_send()
        mine, theirs = self._core_blocks(self.row), self._core_blocks(flip(self.row, 1))
        for stage in range(self.stages + 1):
            for i, block in enumerate(theirs[stage]):
                self._core(self._first(stage) + i, block).wait_recv()
            for i, block in enumerate(mine[stage]):
                self._core(self._first(stage) + i, block).wait_send()


def greet(row, seq, rows, size):
    barrier = pltpu.get_barrier_semaphore()
    count = 0
    bit = 1
    while bit < rows:
        pl.semaphore_signal(barrier, inc=1, device_id=(flip(row, bit), seq), device_id_type=MESH)
        bit *= 2
        count += 1
    for step in range(1, size):
        pl.semaphore_signal(barrier, inc=1, device_id=(row, (seq + step) % size), device_id_type=MESH)
        count += 1
    pl.semaphore_wait(barrier, count)


def pieces(own, buf):
    a, b = own.shape
    if b % (8 * LANE) == 0:
        cut = [(slice(None), pl.ds(i * (b // 2), b // 2)) for i in range(2)]
    elif a % 32 == 0:
        cut = [(pl.ds(i * (a // 2), a // 2), slice(None)) for i in range(2)]
    else:
        cut = [(slice(None), slice(None))]
    return [(own.at[p], buf.at[(slice(None),) + p]) for p in cut]


def forward_kernel(
    rows, size, group,
    x, wq, wp, w1, w2, small, sel_t, cos, sin, pic_col, pic_row,
    wp_all, w1_all, w2_all, att, hat_out, qkv_out, k_out, wq_out, o_out, small_sum, lse,
    xg, normed, wq_buf, small_buf, wide, wq_full, bias, qkv, v_turn, k_turn, hat_turn, o_turn, o_part, o_send, sem_ref, out_sem,
):
    row, seq = lax.axis_index("row"), lax.axis_index("seq")
    toks, width = x.shape
    shard = wp.shape[0]
    packed = 2 * LANE
    sems = Sems(sem_ref)
    base = row * size

    def gather(own, buf):
        return Chain(own, buf, base, row, seq, size, sems), Spread(buf, row, seq, rows, size, sems)

    small_g, wp_g = gather(small, small_buf), gather(wp, wp_all)
    a_wq, s_wq = Scatter(wq, lambda j: wq_buf.at[base + j], row, seq, size, sems), Spread(wq_buf, row, seq, rows, size, sems)
    w1_g = [gather(*p) for p in pieces(w1, w1_all)]
    w2_g = [gather(*p) for p in pieces(w2, w2_all)]
    first, second, third = [small_g], w1_g, w2_g + [wp_g]
    g_x = Chain(x, xg, 0, row, seq, size, sems)
    a_o = Scatter(o_send, lambda j: att.at[j], row, seq, size, sems)
    last = small_g[1].stages

    def chain(group, step):
        for g, _ in group:
            if step > 0:
                g.recv(step)
            if step < size - 1:
                g.send(step + 1)
            else:
                g.keep().wait()

    def spread(group, stage):
        for _, s in group:
            if stage > 0:
                s.recv(stage - 1)
            s.send(stage)

    greet(row, seq, rows, size)
    chain(first, 0)
    a_wq.send_all()
    chain(second, 0)
    for step in range(1, size):
        chain(first, step)
        if step < size - 1:
            chain(second, step)
    a_wq.recv()
    early = first + [(a_wq, s_wq)]
    spread(early, 0)
    g_x.send(1)
    chain(second, size - 1)
    spread(second, 0)
    chain(third, 0)
    if last > 0:
        spread(early, 1)
    for step in range(1, size - 1):
        chain(third, step)
    for stage in range(2, last + 1):
        spread(early, stage)
    for _, s in early:
        s.finish()
    total = jnp.zeros(small_sum.shape, jnp.float32)
    for i in range(rows * size):
        total += small_buf[i].astype(jnp.float32)
    small_sum[...] = total
    for i in range(rows * size):
        wide[pl.ds(i * shard, shard), :] = wq_buf[i].astype(jnp.float32)
    own_bias = small_sum[pl.ds(10 + seq, 1), pl.ds(0, group * packed)]
    for head in range(group):
        cols = pl.ds(head * packed, packed)
        out = pl.ds(head * 3 * LANE, 3 * LANE)
        part = jnp.dot(wide[:, cols].astype(jnp.bfloat16), sel_t[...], preferred_element_type=jnp.float32)
        wq_full[:, out] = part.astype(jnp.bfloat16)
        line = jnp.broadcast_to(own_bias[:, head * packed : (head + 1) * packed], (16, packed))
        bias[:, out] = jnp.dot(line.astype(jnp.bfloat16), sel_t[...], preferred_element_type=jnp.float32)

    def project(chunk):
        start = pl.multiple_of(chunk * toks, toks)
        block = 128

        def norm(i, carry):
            at = pl.multiple_of(i * block, block)
            values = xg[chunk, pl.ds(at, block), :].astype(jnp.float32)
            centered = values - jnp.mean(values, axis=-1, keepdims=True)
            variance = jnp.mean(centered * centered, axis=-1, keepdims=True)
            hat = centered * lax.rsqrt(variance + NORM_EPS)
            hat_turn[:, pl.ds(pl.multiple_of(start + at, block), block)] = hat.T.astype(jnp.bfloat16)
            out = hat * small_sum[0:1, :] + small_sum[1:2, :]
            normed[pl.ds(at, block), :] = out.astype(jnp.bfloat16)
            return carry

        lax.fori_loop(0, toks // block, norm, 0)
        span = pl.ds(start, toks)

        def two_heads(i, carry):
            at = pl.multiple_of(i * 6 * LANE, 6 * LANE)
            mixed = jnp.dot(normed[...], wq_full[:, pl.ds(at, 6 * LANE)], preferred_element_type=jnp.float32)
            mixed += bias[0:1, pl.ds(at, 6 * LANE)]
            for j in range(6):
                u = mixed[:, j * LANE : (j + 1) * LANE]
                if j % 3 < 2:
                    u = u * cos[span, :] + pltpu.roll(u, LANE // 2, 1) * sin[span, :]
                if j % 3:
                    turned = pl.ds(pl.multiple_of((2 * i + j // 3) * LANE, LANE), LANE)
                    (k_turn, v_turn)[j % 3 - 1][turned, span] = u.T.astype(jnp.bfloat16)
                qkv[span, pl.ds(pl.multiple_of(at + j * LANE, LANE), LANE)] = u.astype(jnp.bfloat16)
            return carry

        lax.fori_loop(0, group // 2, two_heads, 0)

    g_x.keep().wait()
    project(seq)
    for step in range(1, size):
        g_x.recv(step)
        if step < size - 1:
            g_x.send(step + 1)
        def arrived(i, carry):
            chunk = seq + (2 * i - 1) * step
            pl.when((chunk >= 0) & (chunk < size))(lambda: project(chunk))
            return carry

        lax.fori_loop(0, 2, arrived, 0)
        if step == 1:
            chain(third, size - 1)
            spread(third, 0)
        if step == size - 2 and last > 0:
            spread(second, 1)
        if step == size - 1 and last > 0:
            spread(third, 1)
    outs = [
        pltpu.make_async_copy(a, b, out_sem.at[1 + i])
        for i, (a, b) in enumerate(((hat_turn, hat_out), (qkv, qkv_out), (k_turn, k_out), (wq_full, wq_out)))
    ]
    for copy in outs:
        copy.start()

    def attend(chunk):
        def one(i, carry):
            head = i % group
            block = chunk * (toks // QBLK) + i // group
            span = pl.ds(pl.multiple_of(block * QBLK, QBLK), QBLK)
            at = pl.multiple_of(head * 3 * LANE, LANE)
            q = qkv[span, pl.ds(at, LANE)]
            k = qkv[:, pl.ds(pl.multiple_of(at + LANE, LANE), LANE)]
            scores = lax.dot_general(k, q, (((1,), (1,)), ((), ())), preferred_element_type=jnp.float32)
            scores = jnp.where(pic_col[...] == pic_row[:, span], scores, -1e30)
            top = jnp.max(scores, axis=0, keepdims=True)
            weights = jnp.exp2((scores - top) * EXP_SCALE)
            sums = jnp.sum(weights, axis=0, keepdims=True)
            turned = pl.ds(pl.multiple_of(head * LANE, LANE), LANE)
            out = jnp.dot(v_turn[turned, :], weights.astype(jnp.bfloat16), preferred_element_type=jnp.float32)
            out = out / sums
            o_part[pl.ds(pl.multiple_of(head * HEAD_DIM, 8), HEAD_DIM), :] = out[:HEAD_DIM]
            lse[head, :, span] = top * EXP_SCALE + jnp.log2(sums)

            @pl.when(head == group - 1)
            def _():
                within = pl.multiple_of((i // group) * QBLK, QBLK)
                o_send[chunk, pl.ds(within, QBLK), :] = o_part[...].T.astype(jnp.bfloat16)
                o_turn[:, span] = o_part[...]

            return carry

        lax.fori_loop(0, group * (toks // QBLK), one, 0)

    o_part[...] = jnp.zeros_like(o_part)
    later = [(second, stage) for stage in range(2, last + 1)] + [(third, stage) for stage in range(2, last + 1)]
    for step in range(1, size + 1):
        attend((seq + step) % size)
        if step < size:
            a_o.send(step)
        else:
            a_o.keep().start()
        if step > 1 and later:
            spread(*later.pop(0))
    for group_of, stage in later:
        spread(group_of, stage)
    o_copy = pltpu.make_async_copy(o_turn, o_out, out_sem.at[0])
    o_copy.start()
    for _, s in second + third:
        s.finish()
    a_o.recv()
    for g, _ in early + second + third:
        g.finish()
    g_x.finish()
    a_o.finish()
    for copy in outs + [o_copy]:
        copy.wait()


def forward_call(mesh, x, wq, wp, w1, w2, small, sel_t, cos, sin, pic_col, pic_row):
    rows, size = mesh.shape["row"], mesh.shape["seq"]
    toks, width = x.shape
    length = toks * size
    group = HEADS // size
    shard = wp.shape[0]
    out_width = round_up(group * HEAD_DIM, LANE)
    total = rows * size
    wide = group * 3 * LANE
    bf, f32 = jnp.bfloat16, jnp.float32
    shape = jax.ShapeDtypeStruct
    return pl.pallas_call(
        functools.partial(forward_kernel, rows, size, group),
        out_shape=(
            shape((total,) + wp.shape, bf),
            shape((total,) + w1.shape, bf),
            shape((total,) + w2.shape, bf),
            shape((size, toks, out_width), bf),
            shape((width, length), bf),
            shape((length, wide), bf),
            shape((group * LANE, length), bf),
            shape((width, wide), bf),
            shape((out_width, length), f32),
            shape(small.shape, f32),
            shape((group, 1, length), f32),
        ),
        in_specs=[ANY] * 6 + [VMEM] * 5,
        out_specs=(ANY,) * 9 + (VMEM,) * 2,
        scratch_shapes=[
            pltpu.VMEM((size, toks, width), bf),
            pltpu.VMEM((toks, width), bf),
            pltpu.VMEM((total, shard, group * 2 * LANE), bf),
            pltpu.VMEM((total,) + small.shape, bf),
            pltpu.VMEM((width, group * 2 * LANE), f32),
            pltpu.VMEM((width, wide), bf),
            pltpu.VMEM((16, wide), f32),
            pltpu.VMEM((length, wide), bf),
            pltpu.VMEM((group * LANE, length), bf),
            pltpu.VMEM((group * LANE, length), bf),
            pltpu.VMEM((width, length), bf),
            pltpu.VMEM((out_width, length), f32),
            pltpu.VMEM((out_width, QBLK), f32),
            pltpu.VMEM((size, toks, out_width), bf),
            pltpu.SemaphoreType.DMA((640,)),
            pltpu.SemaphoreType.DMA((5,)),
        ],
        compiler_params=pltpu.CompilerParams(
            collective_id=0, has_side_effects=True, vmem_limit_bytes=62 * 1024 * 1024
        ),
        name="forward",
    )(x, wq, wp, w1, w2, small, sel_t, cos, sin, pic_col, pic_row)


def token_layout(lengths, widths, row_len):
    slots = jnp.arange(lengths.shape[0])
    pic_ends = jnp.sum(jnp.where(slots[:, None] >= slots[None, :], lengths[None, :], 0), axis=1)
    pic_starts = pic_ends - lengths
    positions = jnp.arange(row_len, dtype=jnp.int32)
    picture = jnp.sum((positions[:, None] >= pic_ends[None, :]).astype(jnp.int32), axis=1)
    matches = picture[:, None] == jnp.arange(lengths.shape[0], dtype=jnp.int32)[None, :]
    first = jnp.sum(jnp.where(matches, pic_starts[None, :], 0), axis=1)
    grid_width = jnp.maximum(jnp.sum(jnp.where(matches, widths[None, :], 0), axis=1), 1)
    within = positions - first
    down = (within // grid_width).astype(jnp.float32)
    side = (within % grid_width).astype(jnp.float32)
    quarter = HEAD_DIM // 4
    frequency = 1.0 / 10000.0 ** (jnp.arange(quarter, dtype=jnp.float32) * 4.0 / HEAD_DIM)
    angles = jnp.concatenate([down[:, None] * frequency, side[:, None] * frequency], axis=-1)
    cosine, sine = jnp.cos(angles), jnp.sin(angles)
    gap = jnp.zeros((row_len, LANE // 2 - HALF), jnp.float32)
    return (
        picture,
        jnp.concatenate([cosine, gap, cosine, gap], axis=-1),
        jnp.concatenate([-sine, gap, sine, gap], axis=-1),
    )


def pack_heads(values):
    a = values.shape[0]
    values = values.reshape(a, 3, HEADS, HEAD_DIM).transpose(0, 2, 1, 3).reshape(a, HEADS, 3 * HEAD_DIM)
    return jnp.pad(values, ((0, 0), (0, 0), (0, 2 * LANE - 3 * HEAD_DIM))).reshape(a, HEADS * 2 * LANE)


def pick_lanes():
    spread = np.arange(3 * LANE)
    kind, lane = spread // LANE, spread % LANE
    turned = np.where(lane < LANE // 2, lane, lane - LANE // 2 + HALF)
    inside = np.where(kind < 2, lane % (LANE // 2) < HALF, lane < HEAD_DIM)
    target = np.where(inside, kind * HEAD_DIM + np.where(kind < 2, turned, lane), -1)
    return (target[:, None] == np.arange(2 * LANE)[None, :]).astype(ml_dtypes.bfloat16)


def unpack_heads(values):
    size, a, _ = values.shape
    values = values.reshape(size, a, HEADS // size, 2 * LANE)[..., : 3 * HEAD_DIM]
    values = values.reshape(size, a, HEADS // size, 3, HEAD_DIM)
    return values.transpose(1, 3, 0, 2, 4).reshape(a, 3 * HEADS * HEAD_DIM)


def add_blocks(outs, firsts, seconds, count, block, first_maps, second_maps):
    n = len(outs)

    def body(*refs):
        for a, b, o in zip(refs[:n], refs[n : 2 * n], refs[2 * n :]):
            o[...] = (a[...].astype(jnp.float32) + b[...].astype(jnp.float32)).astype(o.dtype)

    pltpu.emit_pipeline(
        body,
        grid=(count,),
        in_specs=[pl.BlockSpec(block, m, pipeline_mode=pl.Buffered(4)) for m in list(first_maps) + list(second_maps)],
        out_specs=[pl.BlockSpec(block, lambda i: (i, 0, 0))] * n,
    )(*firsts, *seconds, *outs)


class Reduce:
    def __init__(self, src, core, acc, come, done, row, seq, rows, size, sems, in_vmem):
        self.src, self.core, self.acc, self.come, self.done = src, core, acc, come, done
        self.row, self.seq, self.size, self.in_vmem = row, seq, size, in_vmem
        bits = [1 << i for i in range(1, rows.bit_length() - 1)]
        self.orders = (bits, bits[::-1])
        self.stages = len(bits)
        self.chips = rows // 2
        self.half = src.shape[2] // 2
        self.block = (size, src.shape[1], self.half)
        self.core_sems = [(sems.take(1)[0], sems.take(1)[0]) for _ in range(self.chips)]
        self.sems = [[(sems.take(1)[0], sems.take(1)[0]) for _ in bits] for _ in range(2)]

    def _core_copies(self):
        size = self.size
        other = flip(self.row, 1)
        for chip in range(self.chips):
            theirs = 2 * chip + other % 2
            yield remote(
                self.src.at[pl.ds(theirs * size, size)],
                self.core.at[pl.ds(chip * size, size)],
                *self.core_sems[chip],
                other,
                self.seq,
            )

    def core_send(self):
        for copy in self._core_copies():
            copy.start()

    def _chip(self, half, i):
        chip = self.row // 2
        for k in range(self.stages):
            bit = self.orders[half][self.stages - 1 - k] // 2
            chip = chip + ((i // (1 << k)) % 2) * (flip(chip, bit) - chip)
        return chip

    def core_add(self):
        size = self.size
        for copy in self._core_copies():
            copy.wait_recv()
        core = self.row % 2
        if not self.in_vmem:
            place = lambda half, i: (self._chip(half, i // size), i % size)
            mine = [lambda i, h=h: ((2 * place(h, i)[0] + core) * size + place(h, i)[1], 0, h) for h in range(2)]
            theirs = [lambda i, h=h: (place(h, i)[0] * size + place(h, i)[1], 0, h) for h in range(2)]
            block = (1,) + self.block[1:]
            count = self.chips * size
            add_blocks(self.acc, [self.src] * 2, [self.core] * 2, count, block, mine, theirs)
            return
        for half in range(2):
            cols = pl.ds(half * self.half, self.half)

            def body(i, carry, half=half, cols=cols):
                chip, z = self._chip(half, i // size), i % size
                mine = self.src[(2 * chip + core) * size + z, :, cols].astype(jnp.float32)
                total = mine + self.core[chip * size + z, :, cols].astype(jnp.float32)
                self.acc[half][i] = total.astype(self.acc[half].dtype)
                return carry

            lax.fori_loop(0, self.chips * size, body, 0)

    def _held(self, half, stage):
        return self.acc[half] if stage == 0 else self.done[half][stage - 1]

    def _stage_copy(self, half, stage):
        count = (self.chips >> (stage + 1)) * self.size
        return remote(
            self._held(half, stage).at[pl.ds(count, count)],
            self.come[half][stage],
            *self.sems[half][stage],
            flip(self.row, self.orders[half][stage]),
            self.seq,
        )

    def stage_send(self, stage):
        for half in range(2):
            self._stage_copy(half, stage).start()

    def stage_add(self, stage):
        count = (self.chips >> (stage + 1)) * self.size
        for half in range(2):
            self._stage_copy(half, stage).wait_recv()
        held = [self._held(half, stage) for half in range(2)]
        come, done = ([refs[half][stage] for half in range(2)] for refs in (self.come, self.done))
        if not self.in_vmem:
            plain = [lambda i: (i, 0, 0)] * 2
            add_blocks(done, held, come, count, (1,) + self.block[1:], plain, plain)
            return
        for half in range(2):

            def body(i, carry, half=half):
                total = held[half][i].astype(jnp.float32) + come[half][i].astype(jnp.float32)
                done[half][i] = total.astype(done[half].dtype)
                return carry

            lax.fori_loop(0, count, body, 0)

    @property
    def kept(self):
        return [self._held(half, self.stages) for half in range(2)]

    def finish(self):
        for copy in self._core_copies():
            copy.wait_send()
        for half in range(2):
            for stage in range(self.stages):
                self._stage_copy(half, stage).wait_send()


def reduce_shapes(src, rows, size):
    a, b = src[1], src[2] // 2
    chips = rows // 2
    stages = rows.bit_length() - 2
    shapes = [(chips * size, a, 2 * b)] + [(chips * size, a, b)] * 2
    for _ in range(2):
        for stage in range(stages):
            shapes += [((chips >> (stage + 1)) * size, a, b)] * 2
    return shapes + [(size, a, b)] * 2


def reduce_refs(refs, rows):
    stages = rows.bit_length() - 2
    core, acc, rest = refs[0], refs[1:3], refs[3:-2]
    come = [[rest[2 * (half * stages + j)] for j in range(stages)] for half in range(2)]
    done = [[rest[2 * (half * stages + j) + 1] for j in range(stages)] for half in range(2)]
    return (core, acc, come, done), refs[-2:]


FF_BLK = 1024
FF_CUT = 1280


def backward_kernel(rows, size, shard, group, counts, *refs):
    refs = list(refs)

    def take(count):
        out = refs[:count]
        del refs[:count]
        return out

    attd, x, cot, wp, w1, w2, b1, hat, qkv, k_t, o_t, wh, wq, cos, sin, pic_col, pic_row, lse, small, sel = take(20)
    dx_out, dq_out, dq_pack, layer_out, g_mid, g2, g1, gp, go, b1_sum, wh_all, act, g_act = take(13)
    big = [take(counts) for _ in range(4)]
    vm = take(counts)
    do_in, packed_in, dq, rows_sum, sem_ref, load_sem = refs

    row, seq = lax.axis_index("row"), lax.axis_index("seq")
    length = qkv.shape[0]
    toks = length // size
    width = x.shape[1]
    wide = 3 * LANE
    packed = 2 * LANE
    sems = Sems(sem_ref)
    f32, bf = jnp.float32, jnp.bfloat16

    a_do = Scatter(go, lambda j: do_in.at[j], row, seq, size, sems)
    sources = []
    half_ff = w1.shape[1] // 2
    for i in range(2):
        cols = pl.ds(i * half_ff, half_ff)
        sources.append((g1.at[:, :, cols], big[i]))
    sources += [(g2, big[2]), (gp, big[3])]
    sources.append((dq, vm))
    reducers, z_moves, z_bufs = [], [], []
    for src, bufs in sources:
        inner, z_refs = reduce_refs(bufs, rows)
        r = Reduce(src, *inner, row, seq, rows, size, sems, len(reducers) >= len(big))
        reducers.append(r)
        z_bufs.append(z_refs)
        z_moves.append(
            [Scatter(kept, lambda j, to=to: to.at[j], row, seq, size, sems) for kept, to in zip(r.kept, z_refs)]
        )
    rq = reducers[-1]
    rq_at = len(reducers) - 1
    stages = rq.stages

    def z_send(which):
        for move in z_moves[which]:
            move.send_all()

    def start(which):
        reducers[which].core_add()
        if stages:
            reducers[which].stage_send(0)
        else:
            z_send(which)

    def advance(which, stage):
        r = reducers[which]
        r.stage_add(stage)
        if stage + 1 < stages:
            r.stage_send(stage + 1)
        else:
            z_send(which)

    def z_wait(which):
        for half in range(2):
            z_moves[which][half].recv()
            if which == rq_at:
                dq_out[:, :, pl.ds(half * rq.half, rq.half)] = z_bufs[which][half][...]

    ready = rq_at

    def load(src, dst, sem=0):
        return pltpu.make_async_copy(src, dst, load_sem.at[sem])

    ff = w1.shape[1]
    heads = group * HEAD_DIM

    wh_chain = Chain(wh, wh_all, row * size, row, seq, size, sems)
    wh_spread = Spread(wh_all, row, seq, rows, size, sems)

    def chain_wh(step):
        wh_chain.recv(step)
        if step < size - 1:
            wh_chain.send(step + 1)
        else:
            wh_chain.keep().wait()

    def spread_wh(stage):
        if stage > wh_spread.stages:
            return
        if stage:
            wh_spread.recv(stage - 1)
        wh_spread.send(stage)

    def mlp(middle, n2, n2_turn, cot_v, out_sum, dn2, g_low, lines):
        loads = [load(cot, cot_v, 3)]
        loads[0].start()

        def head(attd_v, x_v, wp_v):
            copies = [load(attd, attd_v, 0), load(x, x_v, 1), load(wp, wp_v, 2)]
            for copy in copies:
                copy.start()
            for copy in copies:
                copy.wait()

            def one(i, carry):
                span = pl.ds(pl.multiple_of(i * QBLK, QBLK), QBLK)
                values = x_v[span, :].astype(f32) + small[2:3, :]
                for g in range(size):
                    values += jnp.dot(
                        attd_v[g, span, pl.ds(0, heads)], wp_v[pl.ds(g * heads, heads), :], preferred_element_type=f32
                    )
                middle[span, :] = values
                centered = values - jnp.mean(values, axis=-1, keepdims=True)
                variance = jnp.mean(centered * centered, axis=-1, keepdims=True)
                out = centered * lax.rsqrt(variance + NORM_EPS) * small[3:4, :] + small[4:5, :]
                n2[span, :] = out.astype(bf)
                n2_turn[:, span] = out.T.astype(bf)
                return carry

            lax.fori_loop(0, toks // QBLK, one, 0)

        pl.run_scoped(
            head, pltpu.VMEM(attd.shape, bf), pltpu.VMEM((toks, width), bf), pltpu.VMEM((width, width), bf)
        )
        loads[0].wait()
        out_sum[...] = jnp.zeros_like(out_sum)
        dn2[...] = jnp.zeros_like(dn2)

        def body(w1_b, w2_b, b1_b, act_b, grad_b, sum_b):
            before = jnp.dot(n2[...], w1_b[...], preferred_element_type=f32) + b1_b[...]
            gate = jax.nn.sigmoid(1.702 * before)
            active = before * gate
            slope = gate + active * (1.702 * (1.0 - gate))
            low = active.astype(bf)
            act_b[...] = low
            out_sum[...] += jnp.dot(low, w2_b[...], preferred_element_type=f32)
            grad = lax.dot_general(cot_v[...], w2_b[...], (((1,), (1,)), ((), ())), preferred_element_type=f32)
            grad = (grad * slope).astype(bf)
            grad_b[...] = grad
            sum_b[...] = jnp.sum(grad.astype(f32), axis=0, keepdims=True)
            dn2[...] += lax.dot_general(grad, w1_b[...], (((1,), (1,)), ((), ())), preferred_element_type=f32)

        by_column = lambda i: (0, i)
        by_row = lambda i: (i, 0)
        chain_wh(1)
        pltpu.emit_pipeline(
            body,
            grid=(ff // FF_BLK,),
            in_specs=[
                pl.BlockSpec((width, FF_BLK), by_column),
                pl.BlockSpec((FF_BLK, width), by_row),
                pl.BlockSpec((1, FF_BLK), by_column),
            ],
            out_specs=[
                pl.BlockSpec((toks, FF_BLK), by_column),
                pl.BlockSpec((toks, FF_BLK), by_column),
                pl.BlockSpec((1, FF_BLK), by_column),
            ],
        )(w1, w2, b1, act, g_act, b1_sum)
        for step in range(2, size):
            chain_wh(step)
        spread_wh(0)

        def up_body(grad_b, g1_b):
            up = jnp.dot(n2_turn[...], grad_b[...], preferred_element_type=f32)
            for s in range(rows * size):
                g1_b[s] = up[s * shard : (s + 1) * shard].astype(bf)

        def up_range(first, count):
            pltpu.emit_pipeline(
                up_body,
                grid=(count,),
                in_specs=[pl.BlockSpec((toks, FF_CUT), lambda i: (0, i + first))],
                out_specs=[pl.BlockSpec((rows * size, shard, FF_CUT), lambda i: (0, 0, i + first))],
            )(g_act, g1)

        def down_body(act_b, g2_b):
            turned = act_b[...].astype(f32).T.astype(bf)
            down = jnp.dot(turned, cot_v[...], preferred_element_type=f32)
            rows_of = g2_b.shape[1]
            for s in range(g2_b.shape[0]):
                g2_b[s] = down[s * rows_of : (s + 1) * rows_of].astype(bf)

        def down_all():
            pltpu.emit_pipeline(
                down_body,
                grid=(ff // FF_CUT,),
                in_specs=[pl.BlockSpec((toks, FF_CUT), by_column)],
                out_specs=[pl.BlockSpec((FF_CUT // g2.shape[1], g2.shape[1], width), lambda i: (i, 0, 0))],
            )(act, g2)

        def tail(wp_v, go_v, out_v):
            copies = [load(wp, wp_v, 1)]
            for copy in copies:
                copy.start()
            lines[...] = jnp.zeros_like(lines)
            go_v[...] = jnp.zeros_like(go_v)

            def one(i, carry):
                span = pl.ds(pl.multiple_of(i * LANE, LANE), LANE)
                values = middle[span, :]
                out_v[span, :] = (values + out_sum[span, :] + small[5:6, :]).astype(bf)
                centered = values - jnp.mean(values, axis=-1, keepdims=True)
                variance = jnp.mean(centered * centered, axis=-1, keepdims=True)
                scale = lax.rsqrt(variance + NORM_EPS)
                hat = centered * scale
                grad = dn2[span, :]
                lines[1:2, :] += jnp.sum(grad * hat, axis=0, keepdims=True)
                lines[2:3, :] += jnp.sum(grad, axis=0, keepdims=True)
                grad = grad * small[3:4, :]
                grad -= jnp.mean(grad, axis=-1, keepdims=True) + hat * jnp.mean(grad * hat, axis=-1, keepdims=True)
                outer = cot_v[span, :].astype(f32)
                lines[3:4, :] += jnp.sum(outer, axis=0, keepdims=True)
                grad = grad * scale + outer
                dn2[span, :] = grad
                low = grad.astype(bf)
                lines[0:1, :] += jnp.sum(low.astype(f32), axis=0, keepdims=True)
                g_low[span, :] = low
                return carry

            lax.fori_loop(0, toks // LANE, one, 0)
            outs = [load(out_v, layer_out, 2), load(dn2, g_mid, 3)]
            for copy in outs:
                copy.start()
            for copy in copies:
                copy.wait()
            for g in range(size):
                part = lax.dot_general(
                    g_low[...], wp_v[pl.ds(g * heads, heads), :], (((1,), (1,)), ((), ())), preferred_element_type=f32
                )
                go_v[g, :, pl.ds(0, heads)] = part.astype(bf)
            send = load(go_v, go, 0)
            send.start()
            send.wait()
            a_do.send_all()
            for copy in outs:
                copy.wait()

        def proj(attd_v, gp_v):
            get = load(attd, attd_v, 1)
            get.start()
            sums = load(b1_sum, rows_sum.at[0:1, pl.ds(0, ff)], 0)
            sums.start()
            sums.wait()
            for i in range(ff // width):
                lines[4 + i : 5 + i, :] = rows_sum[0:1, pl.ds(i * width, width)]
            low_lines = lines[0 : gp_v.shape[1] - shard, :].astype(bf)
            get.wait()
            per = heads // shard
            for i in range(size):
                turned = attd_v[i].astype(f32).T[:heads].astype(bf)
                grad = jnp.dot(turned, g_low[...], preferred_element_type=f32)
                for s in range(per):
                    gp_v[s, pl.ds(0, shard), :] = grad[s * shard : (s + 1) * shard].astype(bf)
                    gp_v[s, pl.ds(shard, low_lines.shape[0]), :] = low_lines
                put = load(gp_v, gp.at[pl.ds(i * per, per)], 0)
                put.start()
                put.wait()

        pl.run_scoped(
            tail,
            pltpu.VMEM((width, width), bf),
            pltpu.VMEM(go.shape, bf),
            pltpu.VMEM((toks, width), bf),
        )
        count = ff // FF_CUT
        up_range(0, count // 2)
        reducers[0].core_send()
        spread_wh(1)
        up_range(count // 2, count - count // 2)
        reducers[1].core_send()
        start(0)
        down_all()
        reducers[2].core_send()
        start(1)
        pl.run_scoped(
            proj, pltpu.VMEM(attd.shape, bf), pltpu.VMEM((rows,) + gp.shape[1:], bf)
        )
        reducers[3].core_send()
        for stage in range(2, wh_spread.stages + 1):
            spread_wh(stage)

    greet(row, seq, rows, size)
    wh_chain.send(1)
    pl.run_scoped(
        mlp,
        pltpu.VMEM((toks, width), f32),
        pltpu.VMEM((toks, width), bf),
        pltpu.VMEM((width, toks), bf),
        pltpu.VMEM((toks, width), bf),
        pltpu.VMEM((toks, width), f32),
        pltpu.VMEM((toks, width), f32),
        pltpu.VMEM((toks, width), bf),
        pltpu.VMEM((round_up(gp.shape[1] - shard, 8), width), f32),
    )
    if stages:
        advance(0, 0)
    start(2)
    if stages:
        advance(1, 0)
    wh_spread.finish()
    pl.run_scoped(
        functools.partial(
            attention_back, rows, size, shard, group, row, seq, sems, start, advance, z_wait, a_do, rq, rq_at,
            (hat, qkv, k_t, o_t, wh_all, wq, cos, sin, pic_col, pic_row, lse, small, sel, dx_out, do_in, packed_in, dq, rows_sum, dq_out, dq_pack),
            load_sem,
        ),
        pltpu.VMEM((length, group * wide), bf),
        pltpu.VMEM((length, group * LANE), bf),
        pltpu.VMEM((group * LANE, length), bf),
        pltpu.VMEM((length, LANE), f32),
        pltpu.VMEM((length, LANE), f32),
        pltpu.VMEM((length, wide), bf),
        pltpu.VMEM((width, length), bf),
        pltpu.VMEM((width, LANE), f32),
        pltpu.VMEM((group, size, toks, packed), bf),
        pltpu.VMEM((2, rows * size, shard, packed), bf),
        pltpu.VMEM((width, packed), f32),
        pltpu.VMEM((width, wide), bf),
        pltpu.VMEM(o_t.shape, f32),
        pltpu.VMEM((group, 1, length), f32),
    )
    wh_chain.finish()
    for r in reducers:
        r.finish()
    for moves in z_moves:
        for move in moves:
            move.finish()
    a_do.finish()


EVENTS = (
    (0.15, ("advance", 0, 1)),
    (0.2, ("start", 3)),
    (0.3, ("advance", 1, 1)),
    (0.55, ("advance", 2, 0)),
    (0.6, ("advance", 3, 0)),
    (0.8, ("advance", 2, 1)),
    (0.85, ("advance", 3, 1)),
    (1, ("wait", 0)),
    (1, ("wait", 1)),
    (1, ("wait", 2)),
    (1, ("wait", 3)),
)


def attention_back(
    rows, size, shard, group, row, seq, sems, start, advance, z_wait, a_do, rq, rq_at, refs, load_sem,
    qkv_s, do_full, k_turn, gk_sum, gv_sum, gm, n_turn, columns, packs, w_cols, w_wide, wq_cols, o_turn, delta,
):
    hat, qkv, k_t, o_t, wh, wq, cos, sin, pic_col, pic_row, lse, small, sel, dx_out, do_in, packed_in, dq, rows_sum, dq_out, dq_pack = refs
    length = qkv.shape[0]
    toks = length // size
    width = hat.shape[0]
    wide = 3 * LANE
    packed = 2 * LANE
    stages = rq.stages
    f32, bf = jnp.float32, jnp.bfloat16
    a_heads = [
        Scatter(packs.at[h], lambda j, h=h: packed_in.at[h, j], row, seq, size, sems) for h in range(group)
    ]
    loads = [
        pltpu.make_async_copy(a, b, load_sem.at[i])
        for i, (a, b) in enumerate(((qkv, qkv_s), (k_t, k_turn), (hat, n_turn), (o_t, o_turn)))
    ]
    for copy in loads:
        copy.start()
    columns[...] = jnp.zeros_like(columns)
    columns[:, pl.ds(8, 8)] = small[0:8, :].T
    for copy in loads[:2] + loads[3:]:
        copy.wait()
    a_do.recv()

    def widen(i, carry):
        chunk, at = i // (toks // QBLK), (i % (toks // QBLK)) * QBLK
        values = do_in[chunk, pl.ds(pl.multiple_of(at, QBLK), QBLK), :].astype(f32)
        lanes = lax.broadcasted_iota(jnp.int32, (QBLK, LANE), 1)
        span = pl.ds(pl.multiple_of(i * QBLK, QBLK), QBLK)
        products = values.T * o_turn[:, span]
        for head in range(group):
            delta[head, :, span] = jnp.sum(
                products[head * HEAD_DIM : (head + 1) * HEAD_DIM], axis=0, keepdims=True
            )
        for head in range(group):
            first = head * HEAD_DIM
            begin = first // LANE * LANE
            window = values[:, begin : min(begin + 2 * LANE, values.shape[1])]
            shift = first - begin
            if shift:
                window = pltpu.roll(window, window.shape[1] - shift, 1)
            piece = jnp.where(lanes < HEAD_DIM, window[:, :LANE], 0.0)
            do_full[pl.ds(pl.multiple_of(i * QBLK, QBLK), QBLK), pl.ds(head * LANE, LANE)] = piece.astype(bf)
        return carry

    lax.fori_loop(0, length // QBLK, widen, 0)
    loads[2].wait()

    def unturn(grad, span):
        return grad * cos[span, :] + pltpu.roll(grad * sin[span, :], LANE // 2, 1)

    blocks = length // QBLK
    tile = min(length, 512)

    def query_block(head, i):
        at = pl.multiple_of(head * wide, LANE)
        q_lane, k_lane, v_lane = (pl.ds(pl.multiple_of(at + j * LANE, LANE), LANE) for j in range(3))
        lane = pl.ds(pl.multiple_of(head * LANE, LANE), LANE)
        span = pl.ds(pl.multiple_of(i * QBLK, QBLK), QBLK)
        q = qkv_s[span, q_lane]
        do = do_full[span, lane]
        shift = lse[head, :, span]
        less = delta[head, :, span]
        pic = pic_row[:, span]
        gq = jnp.zeros((LANE, QBLK), f32)
        for j in range(length // tile):
            part = pl.ds(j * tile, tile)
            scores = lax.dot_general(
                qkv_s[part, k_lane], q, (((1,), (1,)), ((), ())), preferred_element_type=f32
            )
            grad_probs = lax.dot_general(
                qkv_s[part, v_lane], do, (((1,), (1,)), ((), ())), preferred_element_type=f32
            )
            probs = jnp.exp2(scores * EXP_SCALE - shift)
            probs = jnp.where(pic_col[part, :] == pic, probs, 0.0)
            gv_sum[part, :] += jnp.dot(probs.astype(bf), do, preferred_element_type=f32)
            grad_scores = (probs * (grad_probs - less)).astype(bf)
            gk_sum[part, :] += jnp.dot(grad_scores, q, preferred_element_type=f32)
            gq += jnp.dot(k_turn[lane, part], grad_scores, preferred_element_type=f32)
        gm[span, pl.ds(0, LANE)] = unturn(gq.T * SCALE, span).astype(bf)

    def head_close(head):
        at = pl.multiple_of(head * wide, LANE)
        load_wq = pltpu.make_async_copy(wq.at[:, pl.ds(at, wide)], wq_cols, load_sem.at[0])
        load_wq.start()

        def close(i, line):
            span = pl.ds(pl.multiple_of(i * QBLK, QBLK), QBLK)
            gm[span, pl.ds(LANE, LANE)] = unturn(gk_sum[span, :] * SCALE, span).astype(bf)
            gm[span, pl.ds(2 * LANE, LANE)] = gv_sum[span, :].astype(bf)
            grads = gm[span, :]
            chunk, within = i // (toks // QBLK), (i % (toks // QBLK)) * QBLK
            packs[head, chunk, pl.ds(pl.multiple_of(within, QBLK), QBLK), :] = jnp.dot(
                grads, sel[...], preferred_element_type=f32
            ).astype(bf)
            return line + jnp.sum(grads.astype(f32), axis=0, keepdims=True)

        line = lax.fori_loop(0, blocks, close, jnp.zeros((1, wide), f32))
        rows_sum[0:1, pl.ds(at, wide)] = line

    def weight_back(head):
        at = pl.multiple_of(head * wide, LANE)
        line = rows_sum[0:1, pl.ds(at, wide)]
        pltpu.make_async_copy(wq.at[:, pl.ds(at, wide)], wq_cols, load_sem.at[0]).wait()
        tall = width // 2
        per = tall // shard
        for i in range(2):
            span = pl.ds(i * tall, tall)
            grad = jnp.dot(n_turn[span, :], gm[...], preferred_element_type=f32)
            weight = wq_cols[span, :].astype(f32)
            columns[span, 0:1] += jnp.sum(weight * grad, axis=1, keepdims=True)
            columns[span, 1:2] += jnp.sum(weight * line, axis=1, keepdims=True)
            grad = grad * columns[span, 8:9] + columns[span, 9:10] * line
            for s in range(per):
                dq[i * per + s, pl.ds(0, shard), pl.ds(at, wide)] = grad[s * shard : (s + 1) * shard].astype(bf)

    def load_cols(head, g):
        cols = pl.ds(pl.multiple_of((g * group + head) * packed, packed), packed)
        return pltpu.make_async_copy(wh.at[:, :, cols], w_cols.at[g % 2], load_sem.at[2 + g % 2])

    def input_back(head):
        for g in range(2):
            load_cols(head, g).start()
        for g in range(size):
            load_cols(head, g).wait()
            for s in range(rows * size):
                w_wide[pl.ds(s * shard, shard), :] = w_cols[g % 2, s].astype(f32)
            dx_out[...] += lax.dot_general(
                packed_in[head, g], w_wide[...].astype(bf), (((1,), (1,)), ((), ())), preferred_element_type=f32
            )
            if g + 2 < size:
                load_cols(head, g + 2).start()

    dx_out[...] = jnp.zeros_like(dx_out)
    rows_sum[...] = jnp.zeros_like(rows_sum)
    total = group * blocks
    events = []
    for where, event in EVENTS:
        if event[0] == "wait":
            events.append((where, functools.partial(z_wait, event[1])))
        elif event[0] == "start":
            events.append((where, functools.partial(start, event[1])))
        else:
            _, which, stage = event
            for later in range(stage, min(stage + 1, stages) if stage == 0 else stages):
                events.append((where, functools.partial(advance, which, later)))

    def step(i, carry):
        head, block = i // blocks, i % blocks
        for where, event in events:
            if where < 1:
                pl.when(i == int(where * total))(event)

        @pl.when(block == 0)
        def _():
            gk_sum[...] = jnp.zeros_like(gk_sum)
            gv_sum[...] = jnp.zeros_like(gv_sum)

        query_block(head, block)

        @pl.when(block == blocks - 1)
        def _():
            head_close(head)
            for h in range(group):
                pl.when(head == h)(a_heads[h].send_all)
            weight_back(head)

        @pl.when((block == blocks - 1) & (head > 0) & (head < group - 1))
        def _():
            for h in range(1, group - 1):
                pl.when(head == h)(a_heads[h - 1].recv)
            input_back(head - 1)

        return carry

    lax.fori_loop(0, total, step, 0)

    lines = -(-width // (group * wide))
    turned = columns[:, pl.ds(0, 8)].T
    tail = [rows_sum[0:1, pl.ds(0, group * wide)]]
    for line in (0, 1):
        rows_sum[1 + line : 2 + line, pl.ds(0, width)] = turned[line : line + 1]
        tail += [rows_sum[1 + line : 2 + line, pl.ds(k * group * wide, group * wide)] for k in range(lines)]
    tail = jnp.concatenate(tail, axis=0).astype(bf)

    def put_tail(i, carry):
        dq[i, pl.ds(shard, tail.shape[0]), :] = tail
        return carry

    lax.fori_loop(0, rows * size, put_tail, 0)
    rq.core_send()
    start(rq_at)
    for head in range(max(0, group - 2), group):
        a_heads[head].recv()
        input_back(head)
        if head == group - 2 and stages:
            advance(rq_at, 0)
    for stage in range(0 if group < 2 else 1, stages):
        advance(rq_at, stage)
    for where, event in events:
        if where >= 1:
            event()
    z_wait(rq_at)

    def pack(i, carry):
        g, head = i // group, i % group
        raw = dq_out[g, :, pl.ds(pl.multiple_of(head * wide, LANE), wide)]
        dq_pack[g, :, pl.ds(pl.multiple_of(head * packed, LANE), packed)] = jnp.dot(
            raw, sel[...], preferred_element_type=f32
        ).astype(bf)
        return carry

    lax.fori_loop(0, size * group, pack, 0)
    for move in a_heads:
        move.finish()


def backward_call(
    mesh, attd, x, cot, wp, w1, w2, b1, hat, qkv, k_t, o_t, wh, wq, cos, sin, pic_col, pic_row, lse, small, sel, tall
):
    rows, size = mesh.shape["row"], mesh.shape["seq"]
    toks, width = x.shape
    length = toks * size
    group = HEADS // size
    wide = group * 3 * LANE
    total = rows * size
    shard = width // total
    ff = w1.shape[1]
    bf, f32 = jnp.bfloat16, jnp.float32
    shape = jax.ShapeDtypeStruct
    dq_shape = (total, tall, wide)
    g1, g2 = shape((total, shard, ff), bf), shape((total, ff // total, width), bf)
    gp = shape((total, round_up(shard + 4 + ff // width, 16), width), bf)
    half = (total, shard, ff // 2)
    big = [[shape(s, bf) for s in reduce_shapes(g, rows, size)] for g in (half, half, g2.shape, gp.shape)]
    vm = [pltpu.VMEM(s, bf) for s in reduce_shapes(dq_shape, rows, size)]
    go_shape = (size, toks, round_up(group * HEAD_DIM, LANE))
    outs = (
        shape((toks, width), f32),
        shape((size, tall, wide), bf),
        shape((size, tall, group * 2 * LANE), bf),
        shape((toks, width), bf),
        shape((toks, width), f32),
        g2, g1, gp,
        shape(go_shape, bf),
        shape((1, ff), f32),
        shape((total,) + wh.shape, bf),
        shape((toks, ff), bf),
        shape((toks, ff), bf),
        *(s for group_of in big for s in group_of),
    )
    results = pl.pallas_call(
        functools.partial(backward_kernel, rows, size, shard, group, len(vm)),
        out_shape=outs,
        in_specs=[ANY] * 13 + [VMEM] * 7,
        out_specs=(VMEM,) * 3 + (ANY,) * (len(outs) - 3),
        scratch_shapes=[
            *vm,
            pltpu.VMEM(go_shape, bf),
            pltpu.VMEM((group, size, toks, 2 * LANE), bf),
            pltpu.VMEM(dq_shape, bf),
            pltpu.VMEM((8, max(ff, round_up(width, wide))), f32),
            pltpu.SemaphoreType.DMA((640,)),
            pltpu.SemaphoreType.DMA((4,)),
        ],
        compiler_params=pltpu.CompilerParams(
            collective_id=1, has_side_effects=True, vmem_limit_bytes=63 * 1024 * 1024
        ),
        name="backward",
    )(attd, x, cot, wp, w1, w2, b1, hat, qkv, k_t, o_t, wh, wq, cos, sin, pic_col, pic_row, lse, small, sel)
    sums = [
        jnp.concatenate([jnp.sum(r.astype(f32), axis=0) for r in results[i - 2 : i]], axis=-1)
        for i in range(len(results) - 3 * len(vm), len(results) + 1, len(vm))
    ]
    return (*results[:5], sums[2], jnp.concatenate(sums[:2], axis=-1), sums[3])


def layer_norm(values, norm_gain, norm_shift):
    centre = jnp.mean(values, axis=-1, keepdims=True)
    centered = values - centre
    variance = jnp.mean(centered * centered, axis=-1, keepdims=True)
    return centered * lax.rsqrt(variance + NORM_EPS) * norm_gain + norm_shift


def at_own_place(values, index, total):
    mine = jnp.arange(total, dtype=jnp.int32)[:, None] == index
    return jnp.where(mine, values[None, :], jnp.zeros((), values.dtype)).reshape(-1)


def pack_small(vectors, more, width, index, total):
    lines = [at_own_place(values, index, total).reshape(-1, width) for values in vectors]
    lines = jnp.concatenate(lines + [more], axis=0)
    return jnp.pad(lines, ((0, round_up(lines.shape[0], 16) - lines.shape[0]), (0, 0)))


def shards(
    mesh,
    activations,
    cotangent,
    pic_lengths,
    pic_widths,
    ln1_gain,
    ln1_bias,
    qkv_weight,
    qkv_bias,
    proj_weight,
    proj_bias,
    ln2_gain,
    ln2_bias,
    fc1_weight,
    fc1_bias,
    fc2_weight,
    fc2_bias,
):
    rows, size = mesh.shape["row"], mesh.shape["seq"]
    total = rows * size
    index = lax.axis_index("row") * size + lax.axis_index("seq")
    _, toks, width = activations.shape
    length = toks * size
    group = HEADS // size
    shard = proj_weight.shape[0]
    bf, f32 = jnp.bfloat16, jnp.float32

    picture, cos, sin = token_layout(pic_lengths[0], pic_widths[0], length)
    bias_line = at_own_place(qkv_bias, index, total)[None]
    bias_lines = pack_heads(bias_line).reshape(size, -1)
    bias_lines = jnp.pad(bias_lines, ((0, 0), (0, width - bias_lines.shape[1])))
    small = pack_small(
        (ln1_gain, ln1_bias, proj_bias, ln2_gain, ln2_bias, fc2_bias, fc1_bias), bias_lines, width, index, total
    )
    sel = pick_lanes()
    x = activations[0]
    wh = pack_heads(qkv_weight)
    wq = wh.reshape(shard, size, -1).transpose(1, 0, 2)
    wp, w1, w2, att, hat, qkv, k_t, wq_full, o_t, lines, lse = forward_call(
        mesh, x, wq, proj_weight, fc1_weight, fc2_weight, small, sel.T, cos, sin,
        picture[:, None], picture[None, :],
    )
    wp, w1, w2 = (w.reshape(-1, w.shape[-1]) for w in (wp, w1, w2))
    b_up = lines[6 : 6 + w1.shape[1] // width].reshape(1, -1)
    grad_normed, grad_qkv, packed, layer_out, grad_middle, grad_down, grad_up, grad_proj = backward_call(
        mesh, att, x, cotangent[0], wp, w1, w2, b_up, hat, qkv, k_t, o_t, wh, wq_full, cos, sin,
        picture[:, None], picture[None, :], lse, lines, sel,
        round_up(shard + 1 + 2 * -(-width // (group * 3 * LANE)), 16),
    )
    lined = -(-width // (group * 3 * LANE))
    norm_lines = jnp.sum(grad_qkv[:, shard + 1 : shard + 1 + 2 * lined].astype(f32), axis=0).reshape(2, -1)[:, :width]
    sums = jnp.concatenate([grad_proj[shard : shard + 4], norm_lines], axis=0).reshape(6, total, shard)
    sums = lax.dynamic_index_in_dim(sums, index, 1, keepdims=False)
    up_lines = grad_proj[shard + 4 : shard + 4 + w1.shape[1] // width].reshape(total, -1)
    grad_up_bias = lax.dynamic_index_in_dim(up_lines, index, 0, keepdims=False)
    grad_proj = grad_proj[:shard]
    grad_qkv = unpack_heads(packed[:, :shard].astype(f32))
    grad_bias = unpack_heads(packed[:, shard : shard + 1].astype(f32))[0]
    grad_qk = lax.dynamic_slice_in_dim(grad_bias[: 2 * width], index * 2 * shard, 2 * shard)
    grad_value = lax.dynamic_slice_in_dim(grad_bias[2 * width :], index * shard, shard)
    _, norm_one_back = jax.vjp(layer_norm, x.astype(f32), lines[0], lines[1])
    grad_inputs, _, _ = norm_one_back(grad_normed)
    grad_acts = (grad_inputs + grad_middle).astype(bf)

    return (
        layer_out[None],
        grad_acts[None],
        sums[4],
        sums[5],
        grad_qkv,
        grad_qk,
        grad_value,
        grad_proj,
        sums[0],
        sums[1],
        sums[2],
        grad_up,
        grad_up_bias,
        grad_down,
        sums[3],
    )


def solution(mesh):
    one, two = P(("row", "seq")), P(("row", "seq"), None)
    tokens = P("row", "seq", None)
    return jax.shard_map(
        functools.partial(shards, mesh),
        mesh=mesh,
        in_specs=(tokens, tokens, P("row", None), P("row", None), one, one, two, one, two, one, one, one, two, one, two, one),
        out_specs=(tokens, tokens, one, one, two, one, one, two, one, one, one, two, one, two, one),
        check_vma=False,
    )
```
